32 devices in a mesh: dp: 8 (over y, x, core), tensor: 4 (over z).
Axes of the slice: x: 2, y: 2, z: 4, core: 2. Of those that a mesh axis runs over, the one named last changes fastest.
Arguments:
- tokens: bfloat16 [16384, 1280], P(('dp', 'tensor')), may hold values from -6 to 6
- cotangent: bfloat16 [16384, 1280], P(('dp', 'tensor')), may hold values from -6 to 6
- prefix_len: int32 [16], P('dp'), may hold values from 102 to 512, as said below
- w_query: float32 [1280, 1280], P('dp', 'tensor'), may hold values from -0.15625 to 0.15625
- w_kv: float32 [2, 1280, 320], P(None, ('dp', 'tensor')), may hold values from -0.15625 to 0.15625
- w_out: float32 [1280, 1280], P('tensor', 'dp'), may hold values from -2.5 to 2.5
- w_gate_up: float32 [2, 1280, 3584], P(None, 'dp', 'tensor'), may hold values from -0.15625 to 0.15625
- w_down: float32 [3584, 1280], P('tensor', 'dp'), may hold values from -0.09375 to 0.09375
- norm_gains: float32 [2, 1280], P(None, ('dp', 'tensor')), may hold values from 0.5 to 1.5
- m_query: float32 [1280, 1280], P('dp', 'tensor'), may hold values from -80 to 80
- v_query: float32 [1280, 1280], P('dp', 'tensor'), may hold values from 983.04 to 3932.16
- m_kv: float32 [2, 1280, 320], P(None, ('dp', 'tensor')), may hold values from -160 to 160
- v_kv: float32 [2, 1280, 320], P(None, ('dp', 'tensor')), may hold values from 3932.16 to 15728.64
- m_out: float32 [1280, 1280], P('tensor', 'dp'), may hold values from -6 to 6
- v_out: float32 [1280, 1280], P('tensor', 'dp'), may hold values from 4.8 to 19.2
- m_gate_up: float32 [2, 1280, 3584], P(None, 'dp', 'tensor'), may hold values from -32 to 32
- v_gate_up: float32 [2, 1280, 3584], P(None, 'dp', 'tensor'), may hold values from 157.2864 to 622.592
- m_down: float32 [3584, 1280], P('tensor', 'dp'), may hold values from -48 to 48
- v_down: float32 [3584, 1280], P('tensor', 'dp'), may hold values from 360.448 to 1409.024
- m_gains: float32 [2, 1280], P(None, ('dp', 'tensor')), may hold values from -128 to 128
- v_gains: float32 [2, 1280], P(None, ('dp', 'tensor')), may hold values from 2211.84 to 8847.36
Outputs:
- layer_out: bfloat16 [16384, 1280], P(('dp', 'tensor'))
- input_grad: float32 [16384, 1280], P(('dp', 'tensor'))
- first_query: float32 [1280, 1280], P('dp', 'tensor')
- second_query: float32 [1280, 1280], P('dp', 'tensor')
- new_query: float32 [1280, 1280], P('dp', 'tensor')
- first_kv: float32 [2, 1280, 320], P(None, ('dp', 'tensor'))
- second_kv: float32 [2, 1280, 320], P(None, ('dp', 'tensor'))
- new_kv: float32 [2, 1280, 320], P(None, ('dp', 'tensor'))
- first_out: float32 [1280, 1280], P('tensor', 'dp')
- second_out: float32 [1280, 1280], P('tensor', 'dp')
- new_out: float32 [1280, 1280], P('tensor', 'dp')
- first_gate_up: float32 [2, 1280, 3584], P(None, 'dp', 'tensor')
- second_gate_up: float32 [2, 1280, 3584], P(None, 'dp', 'tensor')
- new_gate_up: float32 [2, 1280, 3584], P(None, 'dp', 'tensor')
- first_down: float32 [3584, 1280], P('tensor', 'dp')
- second_down: float32 [3584, 1280], P('tensor', 'dp')
- new_down: float32 [3584, 1280], P('tensor', 'dp')
- first_gains: float32 [2, 1280], P(None, ('dp', 'tensor'))
- second_gains: float32 [2, 1280], P(None, ('dp', 'tensor'))
- new_gains: float32 [2, 1280], P(None, ('dp', 'tensor'))
The draws below stay inside these ranges and needn't reach their ends.
Inputs may be any that keep to these rules, and one draw needn't show every extreme that they name: `prefix_len`: the prefix length of each sequence; some sequence has exactly 512 and some exactly 102.
All inputs are finite; a program needn't handle non-finite values.
Results may differ from the reference program's by a relative error of at most 0.022.
Values may be sent and summed in bfloat16 or wider, within the bound.
No kernel may reach another device: no remote copies, remote signals or barrier semaphores. Data moves between devices by JAX's collectives and lax.ppermute only.
A program may use at most 192 MiB of HBM per device.

```python
import math
import jax
import jax.numpy as jnp
from jax import lax

D = 1280
H = 20
KV = 5
HD = 64
FF = 3584
LEN = 1024
SEQ_DP = 2
STEP = 10
SEQS = 16
TOKENS = 16384
N_DP = 8
N_TENSOR = 4


def draw_prefix_len(key, part):
    key = jax.random.fold_in(key, 7)
    lengths = jax.random.randint(key, (SEQS,), LEN // 10, LEN // 2 + 1)
    positions = jax.random.permutation(jax.random.fold_in(key, 1), SEQS)
    lengths = lengths.at[positions[0]].set(LEN // 2)
    lengths = lengths.at[positions[1]].set(LEN // 10)
    return lengths.astype(jnp.int32)


def with_spikes(values, stream_key, source, target, blocks, factor):
    owner, partner = [(jnp.arange(values.shape[position]) // (values.shape[position] // blocks)).reshape([-1 if axis == position else 1 for axis in range(values.ndim)]) for position in (source, target)]
    chosen = jax.random.permutation(stream_key, blocks)[partner]
    strong = (owner == chosen) | (owner == (partner + blocks // 2) % blocks)
    return jnp.where(strong, factor * values, values)


def level_of(stream_key, extent, shards, least, high):
    def one(axis_at, shards_of):
        draws = jax.random.uniform(jax.random.fold_in(jax.random.fold_in(stream_key, 6), axis_at), (shards_of,), jnp.float32, least / len(shards), high / len(shards))
        return jnp.repeat(jnp.exp(draws), extent[axis_at] // shards_of).reshape((-1,) + (1,) * (len(extent) - axis_at - 1))

    gain = one(*shards[0])
    for cut in shards[1:]:
        gain = gain * one(*cut)
    return gain


def noise(rng, extent, deviation, most, pieces=(), kind=jnp.bfloat16):
    result = jax.random.normal(rng, extent, jnp.float32) * deviation
    if len(pieces) > 0:
        result = level_of(rng, extent, pieces, -0.22, 0.18) * result
    return jnp.clip(result, min=-most, max=most).astype(kind)


def heavy_noise(stream_key, shape, scale, most, shards, heavy, kind=jnp.bfloat16):
    drawn = scale * jax.random.normal(stream_key, shape, jnp.float32)
    if shards:
        drawn = drawn * level_of(stream_key, shape, shards, -0.22, 0.18)
    return jnp.clip(with_spikes(drawn, jax.random.fold_in(stream_key, 3), *heavy), -most, most).astype(kind)


def setup_inputs(seed: int = 0) -> dict:
    key_of = jax.random.split(jax.random.key(seed), 22)
    return {
        "tokens": heavy_noise(key_of[0], (TOKENS, D), 1.0, 6.0, ((0, 32),), (0, 1, 32, 2.75)),
        "cotangent": heavy_noise(key_of[1], (TOKENS, D), 1.0, 6.0, ((0, 32),), (0, 1, 32, 2.75)),
        "prefix_len": draw_prefix_len(jax.random.fold_in(key_of[21], 71), 0),
        "w_query": noise(key_of[3], (D, H * HD), D ** -0.5, 0.15625, ((0, 8), (1, 4)), jnp.float32),
        "w_kv": noise(key_of[4], (2, D, KV * HD), D ** -0.5, 0.15625, ((1, 32),), jnp.float32),
        "w_out": noise(key_of[5], (H * HD, D), (H * HD * 5 // LEN) ** -0.5, 2.5, ((0, 4), (1, 8)), jnp.float32),
        "w_gate_up": noise(key_of[6], (2, D, FF), D ** -0.5, 0.15625, ((1, 8), (2, 4)), jnp.float32),
        "w_down": noise(key_of[7], (FF, D), FF ** -0.5, 0.09375, ((0, 4), (1, 8)), jnp.float32),
        "norm_gains": jnp.clip(1.0 + 0.1 * jax.random.normal(key_of[8], (2, D), jnp.float32), 0.5, 1.5),
        "m_query": noise(key_of[9], (D, H * HD), (0.11 * TOKENS ** 0.5), 80.0, ((0, 8), (1, 4)), jnp.float32),
        "v_query": jnp.clip(jnp.exp(math.log(3932.16) - 1.3862944 * jax.random.uniform(key_of[10], (D, H * HD), jnp.float32) ** level_of(key_of[10], (D, H * HD), ((0, 8), (1, 4)), -0.2, 0.2)), 983.04, 3932.16),
        "m_kv": noise(key_of[11], (2, D, KV * HD), (0.22 * TOKENS ** 0.5), 160.0, ((1, 32),), jnp.float32),
        "v_kv": jnp.clip(jnp.exp(math.log(15728.64) - 1.3862944 * jax.random.uniform(key_of[12], (2, D, KV * HD), jnp.float32) ** level_of(key_of[12], (2, D, KV * HD), ((1, 32),), -0.2, 0.2)), 3932.16, 15728.64),
        "m_out": noise(key_of[13], (H * HD, D), (0.25 * (TOKENS // LEN) ** 0.5), 6.0, ((0, 4), (1, 8)), jnp.float32),
        "v_out": jnp.clip(jnp.exp(math.log(19.2) - 1.3862944 * jax.random.uniform(key_of[14], (H * HD, D), jnp.float32) ** level_of(key_of[14], (H * HD, D), ((0, 4), (1, 8)), -0.2, 0.2)), 4.8, 19.2),
        "m_gate_up": noise(key_of[15], (2, D, FF), (0.045 * TOKENS ** 0.5), 32.0, ((1, 8), (2, 4)), jnp.float32),
        "v_gate_up": jnp.clip(jnp.exp(math.log(622.592) - 1.375823 * jax.random.uniform(key_of[16], (2, D, FF), jnp.float32) ** level_of(key_of[16], (2, D, FF), ((1, 8), (2, 4)), -0.2, 0.2)), 157.2864, 622.592),
        "m_down": noise(key_of[17], (FF, D), (0.066 * TOKENS ** 0.5), 48.0, ((0, 4), (1, 8)), jnp.float32),
        "v_down": jnp.clip(jnp.exp(math.log(1409.024) - 1.3633049 * jax.random.uniform(key_of[18], (FF, D), jnp.float32) ** level_of(key_of[18], (FF, D), ((0, 4), (1, 8)), -0.2, 0.2)), 360.448, 1409.024),
        "m_gains": noise(key_of[19], (2, D), (0.16 * TOKENS ** 0.5), 128.0, ((1, 32),), jnp.float32),
        "v_gains": jnp.clip(jnp.exp(math.log(8847.36) - 1.3862944 * jax.random.uniform(key_of[20], (2, D), jnp.float32) ** level_of(key_of[20], (2, D), ((1, 32),), -0.2, 0.2)), 2211.84, 8847.36),
    }


@jax.custom_vjp
def low(v):
    return lax.optimization_barrier(v.astype(jnp.bfloat16)).astype(jnp.float32)

@jax.custom_vjp
def low_back(v):
    return v

def low_keep(v):
    return (low(v), None)

def low_pass(kept, grad):
    return (grad,)

def back_keep(v):
    return (v, None)

def back_low(kept, grad):
    return (low(grad),)
low.defvjp(low_keep, low_pass)
low_back.defvjp(back_keep, back_low)
beta_one = 0.9
beta_two = 0.95
adam_eps = 1e-08
decay_rate = 0.1
rate_query = 0.06
rate_shared = 0.06
rate_output = 0.8
rate_gate_up = 0.06
rate_down = 0.05
rate_gains = 0.6
norm_eps = 1e-05
neg_fill = -1e+30

def matmul(left_side, right_side):
    return jnp.dot(left_side, right_side, precision=lax.Precision.HIGHEST, preferred_element_type=jnp.float32)

def normalize(matrix, gain_row):
    scaling = lax.rsqrt(lax.optimization_barrier(jnp.mean(matrix * matrix, axis=-1, keepdims=True)) + norm_eps)
    return low(matrix * scaling * gain_row)

def adamw_step(weight, gradient, moment_one, moment_two, step_rate, decay_coef):
    moment_one = beta_one * moment_one + (1.0 - beta_one) * gradient
    moment_two = beta_two * moment_two + (1.0 - beta_two) * gradient * gradient
    unbiased_one = moment_one / (1.0 - beta_one ** STEP)
    unbiased_two = moment_two / (1.0 - beta_two ** STEP)
    updated = weight - step_rate * (unbiased_one / (jnp.sqrt(unbiased_two) + adam_eps) + decay_coef * weight)
    return (moment_one, moment_two, updated)

def attend(bundle):
    queries_seq, keys_seq, values_seq, prefix_one = bundle
    seq_len = queries_seq.shape[0]
    query_heads = queries_seq.reshape(seq_len, N_TENSOR, KV, HD)
    key_heads = keys_seq.reshape(N_TENSOR, seq_len, KV, HD)
    value_heads = values_seq.reshape(N_TENSOR, seq_len, KV, HD)
    scores = jnp.einsum('qrhd,rkhd->rhqk', query_heads, key_heads, precision=lax.Precision.HIGHEST) * HD ** (-0.5)
    scores = low_back(scores)
    row_ids = jnp.arange(seq_len)
    allowed = (row_ids[None, :] <= row_ids[:, None]) | (row_ids[None, :] < prefix_one)
    probs = low(jax.nn.softmax(jnp.where(allowed, scores, neg_fill), axis=-1))
    mixed_heads = jnp.einsum('rhqk,rkhd->qrhd', probs, value_heads, precision=lax.Precision.HIGHEST)
    return mixed_heads.reshape(seq_len, H * HD)

def forward(inputs, prefix_group, w_query, w_kv, w_out, w_gate_up, w_down, norm_gains):
    gains_low = low(norm_gains)
    normed_one = normalize(inputs, gains_low[0])
    queries = low(low_back(matmul(normed_one, low(w_query))))
    kv_low = low(w_kv)
    key_pre = matmul(normed_one, kv_low[0])
    value_pre = matmul(normed_one, kv_low[1])
    key_copies = jnp.stack([low(low_back(key_pre)) for replica in range(N_TENSOR)])
    value_copies = jnp.stack([low(low_back(value_pre)) for replica in range(N_TENSOR)])
    key_seqs = jnp.transpose(key_copies.reshape(N_TENSOR, SEQ_DP, LEN, KV * HD), (1, 0, 2, 3))
    value_seqs = jnp.transpose(value_copies.reshape(N_TENSOR, SEQ_DP, LEN, KV * HD), (1, 0, 2, 3))
    mixed_all = lax.map(jax.checkpoint(attend), (queries.reshape(SEQ_DP, LEN, H * HD), key_seqs, value_seqs, prefix_group))
    attended = low(low_back(mixed_all.reshape(SEQ_DP * LEN, H * HD)))
    middle = inputs + low_back(matmul(attended, low(w_out)))
    normed_two = normalize(middle, gains_low[1])
    gate_up_low = low(w_gate_up)
    gate_pre = low_back(matmul(normed_two, gate_up_low[0]))
    up_pre = low_back(matmul(normed_two, gate_up_low[1]))
    hidden = low(jax.nn.silu(gate_pre) * up_pre)
    return middle + low_back(matmul(hidden, low(w_down)))

def reference(tokens, cotangent, prefix_len, w_query, w_kv, w_out, w_gate_up, w_down, norm_gains, m_query, v_query, m_kv, v_kv, m_out, v_out, m_gate_up, v_gate_up, m_down, v_down, m_gains, v_gains):
    params = (w_query, w_kv, w_out, w_gate_up, w_down, norm_gains)
    group_rows = SEQ_DP * LEN
    input_groups = tokens.astype(jnp.float32).reshape(N_DP, group_rows, D)
    cot_groups = cotangent.astype(jnp.float32).reshape(N_DP, group_rows, D)
    prefix_groups = prefix_len.reshape(N_DP, SEQ_DP).astype(jnp.int32)

    def one_group(running, bundle):
        inputs, cots, prefix_group = bundle

        def run_group(inputs, *weights):
            return forward(inputs, prefix_group, *weights)
        outputs, pullback = jax.vjp(run_group, inputs, *params)
        grads = pullback(cots)
        running = tuple((running_sum + fresh_grad for running_sum, fresh_grad in zip(running, grads[1:])))
        return (running, (outputs.astype(jnp.bfloat16), grads[0]))
    start_sums = tuple((jnp.zeros(weight.shape, jnp.float32) for weight in params))
    totals, (out_groups, grad_groups) = lax.scan(one_group, start_sums, (input_groups, cot_groups, prefix_groups))
    layer_out = out_groups.reshape(TOKENS, D)
    input_grad = grad_groups.reshape(TOKENS, D)
    first_query, second_query, new_query = adamw_step(w_query, totals[0], m_query, v_query, rate_query, decay_rate)
    first_kv, second_kv, new_kv = adamw_step(w_kv, totals[1], m_kv, v_kv, rate_shared, decay_rate)
    first_out, second_out, new_out = adamw_step(w_out, totals[2], m_out, v_out, rate_output, decay_rate)
    first_gate_up, second_gate_up, new_gate_up = adamw_step(w_gate_up, totals[3], m_gate_up, v_gate_up, rate_gate_up, decay_rate)
    first_down, second_down, new_down = adamw_step(w_down, totals[4], m_down, v_down, rate_down, decay_rate)
    first_gains, second_gains, new_gains = adamw_step(norm_gains, totals[5], m_gains, v_gains, rate_gains, 0.0)
    return (layer_out, input_grad, first_query, second_query, new_query, first_kv, second_kv, new_kv, first_out, second_out, new_out, first_gate_up, second_gate_up, new_gate_up, first_down, second_down, new_down, first_gains, second_gains, new_gains)
```

```python
import functools

import jax
import jax.numpy as jnp
from jax import lax
from jax.experimental import pallas as pl
from jax.experimental.pallas import tpu as pltpu
from jax.sharding import Mesh, PartitionSpec as P

KV = 5
HD = 64
LEN = 1024
STEP = 10
RB = 256

beta_one = 0.9
beta_two = 0.95
adam_eps = 1e-08
decay_rate = 0.1
rate_query = 0.06
rate_shared = 0.06
rate_output = 0.8
rate_gate_up = 0.06
rate_down = 0.05
rate_gains = 0.6
norm_eps = 1e-05
neg_fill = -1e30

bf16 = jnp.bfloat16
f32 = jnp.float32
NN = (((1,), (0,)), ((), ()))
NT = (((1,), (1,)), ((), ()))
TN = (((0,), (0,)), ((), ()))
VMEM_LIMIT = 52 * 2**20


def dot(a, b, dims=NN):
    return lax.dot_general(a, b, dims, preferred_element_type=f32)


def rms_scale(matrix):
    return lax.rsqrt(jnp.mean(matrix * matrix, axis=-1, keepdims=True) + norm_eps)


def norm_back(matrix, gain_row, upstream):
    scaling = rms_scale(matrix)
    unit_rows = matrix * scaling
    weighted = upstream * gain_row
    inner_mean = jnp.mean(weighted * unit_rows, axis=-1, keepdims=True)
    return (scaling * (weighted - unit_rows * inner_mean), jnp.sum(upstream * unit_rows, axis=0))


def adamw_step(weight, gradient, moment_one, moment_two, step_rate, decay_coef):
    moment_one = beta_one * moment_one + (1.0 - beta_one) * gradient
    moment_two = beta_two * moment_two + (1.0 - beta_two) * gradient * gradient
    unbiased_one = moment_one / (1.0 - beta_one**STEP)
    unbiased_two = moment_two / (1.0 - beta_two**STEP)
    updated = weight - step_rate * (
        unbiased_one / (jnp.sqrt(unbiased_two) + adam_eps) + decay_coef * weight
    )
    return (moment_one, moment_two, updated)


def attend_forward_kernel(info, q_ref, k_ref, v_ref, o_ref, lse_ref, *, rows):
    second, prefix = info[0], info[1]

    def run(is_second):
        for block in range(rows // RB):
            base = (rows if is_second else 0) + block * RB
            keys = base + RB if is_second else rows
            masked = base if is_second else 0
            row_slice = slice(block * RB, (block + 1) * RB)
            col = lax.broadcasted_iota(jnp.int32, (RB, keys - masked), 1) + masked
            row = lax.broadcasted_iota(jnp.int32, (RB, keys - masked), 0) + base
            allowed = (col <= row) | (col < prefix)
            outs, logs = [], []
            for c in range(KV):
                cols = slice(c * HD, (c + 1) * HD)
                scores = dot(q_ref[0, row_slice, cols], k_ref[:keys, cols], NT)
                tail = jnp.where(allowed, scores[:, masked:], neg_fill)
                scores = jnp.concatenate([scores[:, :masked], tail], 1) if masked else tail
                highest = jnp.max(scores, axis=1, keepdims=True)
                expo = jnp.exp(scores - highest)
                total = jnp.sum(expo, axis=1, keepdims=True)
                outs.append((dot(expo.astype(bf16), v_ref[:keys, cols]) / total).astype(bf16))
                logs.append(highest + jnp.log(total))
            o_ref[0, row_slice, :] = jnp.concatenate(outs, 1)
            lse_ref[0, row_slice, :] = jnp.concatenate(logs + [jnp.zeros((RB, 3), f32)], 1)

    pl.when(second == 0)(lambda: run(False))
    pl.when(second == 1)(lambda: run(True))


def attend_forward(info, queries, keys, values):
    groups, rows, width = queries.shape
    block = pl.BlockSpec((1, rows, width), lambda r, _: (r, 0, 0))
    whole = pl.BlockSpec(keys.shape, lambda r, _: (0, 0))
    elements = groups * rows * KV * keys.shape[0]
    return pl.pallas_call(
        functools.partial(attend_forward_kernel, rows=rows),
        grid_spec=pltpu.PrefetchScalarGridSpec(
            num_scalar_prefetch=1,
            grid=(groups,),
            in_specs=[block, whole, whole],
            out_specs=[block, pl.BlockSpec((1, rows, 8), lambda r, _: (r, 0, 0))],
        ),
        out_shape=[
            jax.ShapeDtypeStruct(queries.shape, bf16),
            jax.ShapeDtypeStruct((groups, rows, 8), f32),
        ],
        compiler_params=pltpu.CompilerParams(vmem_limit_bytes=VMEM_LIMIT),
        cost_estimate=pl.CostEstimate(
            flops=elements * HD * 4, bytes_accessed=4 * 2**20, transcendentals=elements
        ),
        name="attend_forward",
    )(info, queries, keys, values)


def attend_backward_kernel(
    info, q_ref, k_ref, v_ref, do_ref, lse_ref, delta_ref, dq_ref, dk_ref, dv_ref, dk_acc, dv_acc, *, rows
):
    second, prefix = info[0], info[1]
    group = pl.program_id(0)

    @pl.when(group == 0)
    def _():
        dk_acc[...] = jnp.zeros_like(dk_acc)
        dv_acc[...] = jnp.zeros_like(dv_acc)

    def run(is_second):
        for block in range(rows // RB):
            base = (rows if is_second else 0) + block * RB
            keys = base + RB if is_second else rows
            masked = base if is_second else 0
            row_slice = slice(block * RB, (block + 1) * RB)
            query_grads = []
            for c in range(KV):
                cols = slice(c * HD, (c + 1) * HD)
                query, out_grad = q_ref[0, row_slice, cols], do_ref[0, row_slice, cols]
                log_sum = lse_ref[0, c : c + 1, row_slice]
                delta = delta_ref[0, c : c + 1, row_slice]
                query_grad = jnp.zeros((RB, HD), f32)
                for start in range(0, keys, RB):
                    key_slice = slice(start, start + RB)
                    key, value = k_ref[key_slice, cols], v_ref[key_slice, cols]
                    scores = dot(key, query, NT) - log_sum
                    if start >= masked:
                        at = lax.broadcasted_iota(jnp.int32, (RB, RB), 0) + start
                        row = lax.broadcasted_iota(jnp.int32, (RB, RB), 1) + base
                        scores = jnp.where((at <= row) | (at < prefix), scores, neg_fill)
                    probs = jnp.exp(scores)
                    probs_grad = dot(value, out_grad, NT)
                    score_grad = (probs * (probs_grad - delta)).astype(bf16)
                    dv_acc[c, key_slice, :] += dot(probs.astype(bf16), out_grad)
                    dk_acc[c, key_slice, :] += dot(score_grad, query)
                    query_grad = query_grad + dot(score_grad, key, TN)
                query_grads.append((query_grad * HD**-0.5).astype(bf16))
            dq_ref[0, row_slice, :] = jnp.concatenate(query_grads, 1)

    pl.when(second == 0)(lambda: run(False))
    pl.when(second == 1)(lambda: run(True))

    @pl.when(group == pl.num_programs(0) - 1)
    def _():
        dk_ref[...] = jnp.concatenate([dk_acc[c] for c in range(KV)], 1)
        dv_ref[...] = jnp.concatenate([dv_acc[c] for c in range(KV)], 1)


def attend_backward(info, queries, keys, values, out_grad, log_sums, delta):
    groups, rows, width = queries.shape
    block = pl.BlockSpec((1, rows, width), lambda r, _: (r, 0, 0))
    whole = pl.BlockSpec(keys.shape, lambda r, _: (0, 0))
    stats = pl.BlockSpec((1, 8, rows), lambda r, _: (r, 0, 0))
    elements = groups * rows * KV * keys.shape[0]
    return pl.pallas_call(
        functools.partial(attend_backward_kernel, rows=rows),
        grid_spec=pltpu.PrefetchScalarGridSpec(
            num_scalar_prefetch=1,
            grid=(groups,),
            in_specs=[block, whole, whole, block, stats, stats],
            out_specs=[block, whole, whole],
            scratch_shapes=[pltpu.VMEM((KV, keys.shape[0], HD), f32)] * 2,
        ),
        out_shape=[jax.ShapeDtypeStruct(queries.shape, bf16)]
        + [jax.ShapeDtypeStruct(keys.shape, f32)] * 2,
        compiler_params=pltpu.CompilerParams(vmem_limit_bytes=VMEM_LIMIT),
        cost_estimate=pl.CostEstimate(
            flops=elements * HD * 10, bytes_accessed=8 * 2**20, transcendentals=elements
        ),
        name="attend_backward",
    )(info, queries, keys, values, out_grad, log_sums, delta)


def query_kernel(x_ref, w_ref, q_ref):
    q_ref[0] = (dot(x_ref[...], w_ref[0]).astype(bf16) * HD**-0.5).astype(bf16)


def project_queries(normed, w_groups):
    groups, depth, width = w_groups.shape
    rows = normed.shape[0]
    return pl.pallas_call(
        query_kernel,
        grid=(groups,),
        in_specs=[
            pl.BlockSpec((rows, depth), lambda r: (0, 0)),
            pl.BlockSpec((1, depth, width), lambda r: (r, 0, 0)),
        ],
        out_specs=pl.BlockSpec((1, rows, width), lambda r: (r, 0, 0)),
        out_shape=jax.ShapeDtypeStruct((groups, rows, width), bf16),
        compiler_params=pltpu.CompilerParams(vmem_limit_bytes=VMEM_LIMIT),
        cost_estimate=pl.CostEstimate(
            flops=2 * groups * rows * depth * width, bytes_accessed=6 * 2**20, transcendentals=0
        ),
        name="project_queries",
    )(normed, w_groups)


def attended_grad_kernel(m_ref, w_ref, o_ref, do_ref, delta_ref):
    grad = dot(m_ref[...], w_ref[0]).astype(bf16)
    do_ref[0] = grad
    product = grad.astype(f32) * o_ref[0].astype(f32)
    sums = [
        jnp.sum(product[:, c * HD : (c + 1) * HD], axis=1, keepdims=True) for c in range(KV)
    ]
    delta_ref[0] = jnp.concatenate(sums + [jnp.zeros((product.shape[0], 3), f32)], 1)


def project_attended_grad(middle_low, w_groups, attended):
    groups, depth, width = w_groups.shape
    rows = middle_low.shape[0]
    block = pl.BlockSpec((1, rows, width), lambda r: (r, 0, 0))
    return pl.pallas_call(
        attended_grad_kernel,
        grid=(groups,),
        in_specs=[
            pl.BlockSpec((rows, depth), lambda r: (0, 0)),
            pl.BlockSpec((1, depth, width), lambda r: (r, 0, 0)),
            block,
        ],
        out_specs=[block, pl.BlockSpec((1, rows, 8), lambda r: (r, 0, 0))],
        out_shape=[
            jax.ShapeDtypeStruct((groups, rows, width), bf16),
            jax.ShapeDtypeStruct((groups, rows, 8), f32),
        ],
        compiler_params=pltpu.CompilerParams(vmem_limit_bytes=VMEM_LIMIT),
        cost_estimate=pl.CostEstimate(
            flops=2 * groups * rows * depth * width, bytes_accessed=8 * 2**20, transcendentals=0
        ),
        name="project_attended_grad",
    )(middle_low, w_groups, attended)


def accumulate_kernel(a_ref, w_ref, init_ref, out_ref, acc):
    group = pl.program_id(0)

    @pl.when(group == 0)
    def _():
        acc[...] = init_ref[...].astype(f32)

    acc[...] += dot(a_ref[0], w_ref[0], NT)

    @pl.when(group == pl.num_programs(0) - 1)
    def _():
        out_ref[...] = acc[...]


def project_back(groups_in, w_groups, init):
    groups, rows, width = groups_in.shape
    depth = w_groups.shape[1]
    return pl.pallas_call(
        accumulate_kernel,
        grid=(groups,),
        in_specs=[
            pl.BlockSpec((1, rows, width), lambda r: (r, 0, 0)),
            pl.BlockSpec((1, depth, width), lambda r: (r, 0, 0)),
            pl.BlockSpec((rows, depth), lambda r: (0, 0)),
        ],
        out_specs=pl.BlockSpec((rows, depth), lambda r: (0, 0)),
        out_shape=jax.ShapeDtypeStruct((rows, depth), f32),
        scratch_shapes=[pltpu.VMEM((rows, depth), f32)],
        compiler_params=pltpu.CompilerParams(vmem_limit_bytes=VMEM_LIMIT),
        cost_estimate=pl.CostEstimate(
            flops=2 * groups * rows * depth * width, bytes_accessed=8 * 2**20, transcendentals=0
        ),
        name="project_back",
    )(groups_in, w_groups, init)


def core_swap(value):
    return lax.ppermute(value, "c", [(0, 1), (1, 0)])


def pair_swap(value):
    size = lax.axis_size("z")
    return lax.ppermute(value, "z", [(i, i ^ 1) for i in range(size)])


def far_swap(value):
    size = lax.axis_size("z")
    return lax.ppermute(value, "z", [(i, i ^ 2) for i in range(size)])


def spread_tokens(own):
    near = core_swap(own)
    far = pair_swap(own)
    return jnp.concatenate([own, near], 0), jnp.concatenate([far, core_swap(far)], 0)


def collect_tokens(near_part, far_part, rows):
    far_sum = far_part[:rows] + core_swap(far_part[rows:])
    near_sum = near_part[:rows].astype(f32) + core_swap(near_part[rows:]).astype(f32)
    return near_sum + pair_swap(far_sum).astype(f32)


def pick(stacked, index, axis=0):
    return lax.dynamic_index_in_dim(stacked, index, axis, keepdims=False)


def reduce_over_z(stacked, z):
    halves = stacked.reshape((2, 2) + stacked.shape[1:])
    kept = pick(halves, z // 2) + far_swap(pick(halves, 1 - z // 2))
    return pick(kept, z % 2).astype(f32) + pair_swap(pick(kept, 1 - z % 2)).astype(f32)


def reduce_whole(parts, c, z):
    mine = pick(parts, c, 2).astype(f32) + core_swap(pick(parts, 1 - c, 2)).astype(f32)
    scattered = lax.psum_scatter(mine.astype(bf16), "a", scatter_dimension=1, tiled=True)
    return reduce_over_z(scattered[:, 0], z)


def body(
    tokens,
    cotangent,
    prefix_len,
    w_query,
    w_kv,
    w_out,
    w_gate_up,
    w_down,
    norm_gains,
    m_query,
    v_query,
    m_kv,
    v_kv,
    m_out,
    v_out,
    m_gate_up,
    v_gate_up,
    m_down,
    v_down,
    m_gains,
    v_gains,
):
    rows, width = tokens.shape
    c, z = lax.axis_index("c"), lax.axis_index("z")
    n_a, n_z = lax.axis_size("a"), lax.axis_size("z")
    n_dp = 2 * n_a
    w_rows, group_width = w_query.shape
    kv_rows = w_kv.shape[1]
    hidden_width = w_gate_up.shape[2]
    second = (z % (LEN // rows)) == 1
    seq_at = z // (LEN // rows)
    info = jnp.stack([second.astype(jnp.int32), pick(prefix_len, seq_at)])

    gain_row = jnp.zeros((1, group_width), f32).at[0, : 2 * kv_rows].set(norm_gains.reshape(-1))
    head_pack = jnp.concatenate([w_query, w_kv[0], w_kv[1], gain_row], 0).astype(bf16)
    head_all = lax.all_gather(head_pack, ("a", "c", "z"), axis=0, tiled=False)
    head_all = head_all.reshape(n_dp, n_z, head_pack.shape[0], group_width)
    query_groups = jnp.transpose(head_all[:, :, :w_rows], (1, 0, 2, 3)).reshape(
        n_z, width, group_width
    )
    w_key = head_all[:, :, w_rows : w_rows + kv_rows].reshape(width, group_width)
    w_value = head_all[:, :, w_rows + kv_rows : w_rows + 2 * kv_rows].reshape(width, group_width)
    gain_vals = (
        jnp.transpose(
            head_all[:, :, w_rows + 2 * kv_rows, : 2 * kv_rows].reshape(n_dp * n_z, 2, kv_rows),
            (1, 0, 2),
        )
        .reshape(2, width)
        .astype(f32)
    )
    out_all = lax.all_gather(w_out.T.astype(bf16), ("a", "c", "z"), axis=0, tiled=False)
    out_groups = jnp.transpose(
        out_all.reshape(n_dp, n_z, w_rows, group_width), (1, 0, 2, 3)
    ).reshape(n_z, width, group_width)

    ffn_own = jnp.concatenate([w_gate_up, w_down.T[None]], 0).astype(bf16)
    cross = [(n_z + zz, zz) for zz in range(n_z)] + [(zz, n_z + (zz ^ 2)) for zz in range(n_z)]
    crossed = lax.ppermute(ffn_own, ("c", "z"), cross)
    shifted = lax.ppermute(
        ffn_own, ("c", "z"), [(n_z + zz, n_z + (zz ^ 2)) for zz in range(n_z)]
    )
    ffn_first = jnp.where(c == 0, ffn_own, crossed)
    ffn_second = jnp.where(c == 0, crossed, shifted)
    ffn_w = lax.all_gather(
        jnp.concatenate([ffn_first, ffn_second], 1), "a", axis=1, tiled=True
    )

    cot_near, cot_far = spread_tokens(cotangent)

    inputs = tokens.astype(f32)
    normed_one = (inputs * rms_scale(inputs) * gain_vals[0]).astype(bf16)
    keys_values = jnp.concatenate([dot(normed_one, w_key), dot(normed_one, w_value)], 1).astype(bf16)
    before = lax.ppermute(keys_values, "z", [(i, i + 1) for i in range(0, n_z, 2)])
    kv_seq = jnp.concatenate([jnp.where(second, before, keys_values), keys_values], 0)
    k_seq, v_seq = kv_seq[:, :group_width], kv_seq[:, group_width:]
    queries = project_queries(normed_one, query_groups)
    attended, log_sums = attend_forward(info, queries, k_seq, v_seq)
    middle = project_back(attended, out_groups, tokens)
    normed_two = (middle * rms_scale(middle) * gain_vals[1]).astype(bf16)

    two_near, two_far = spread_tokens(normed_two)

    def feed_forward(normed, cot):
        gate = dot(normed, ffn_w[0])
        up = dot(normed, ffn_w[1])
        hidden_grad = dot(cot, ffn_w[2])
        sig = jax.nn.sigmoid(gate)
        silu = gate * sig
        hidden = (silu * up).astype(bf16)
        gate_grad = (hidden_grad * up * sig * (1.0 + gate * (1.0 - sig))).astype(bf16)
        up_grad = (hidden_grad * silu).astype(bf16)
        out_part = dot(hidden, ffn_w[2], NT).astype(bf16)
        back_part = (dot(gate_grad, ffn_w[0], NT) + dot(up_grad, ffn_w[1], NT)).astype(bf16)
        return hidden, gate_grad, up_grad, out_part, back_part

    hid_near, gg_near, ug_near, out_near, back_near = feed_forward(two_near, cot_near)
    hid_far, gg_far, ug_far, out_far, back_far = feed_forward(two_far, cot_far)
    normed_two_grad = collect_tokens(back_near, back_far, rows)
    two_all = jnp.concatenate([two_near, two_far], 0)
    cot_all = jnp.concatenate([cot_near, cot_far], 0)
    ffn_grad = jnp.stack(
        [
            dot(two_all, jnp.concatenate([gg_near, gg_far], 0), TN).astype(bf16),
            dot(two_all, jnp.concatenate([ug_near, ug_far], 0), TN).astype(bf16),
            dot(cot_all, jnp.concatenate([hid_near, hid_far], 0), TN).astype(bf16),
        ]
    )
    ffn_sum = lax.psum_scatter(ffn_grad, "a", scatter_dimension=1, tiled=True)
    ffn_sum = ffn_sum.reshape(3, 2, w_rows, hidden_width)
    back = [(dst, src) for src, dst in cross]
    crossed_back = lax.ppermute(
        jnp.where(c == 0, ffn_sum[:, 1], ffn_sum[:, 0]), ("c", "z"), back
    )
    shifted_back = lax.ppermute(
        ffn_sum[:, 1], ("c", "z"), [(n_z + zz, n_z + (zz ^ 2)) for zz in range(n_z)]
    )
    ffn_g = crossed_back.astype(f32) + jnp.where(c == 0, ffn_sum[:, 0], shifted_back).astype(f32)
    layer_out = (middle + collect_tokens(out_near, out_far, rows)).astype(bf16)

    middle_back, gain_two_grad = norm_back(middle, gain_vals[1], normed_two_grad)
    middle_grad = cotangent.astype(f32) + middle_back
    middle_low = middle_grad.astype(bf16)
    attended_grad, delta = project_attended_grad(middle_low, out_groups, attended)
    out_grad = jnp.stack([dot(middle_low, attended[r], TN) for r in range(n_z)]).astype(bf16)
    out_g = reduce_whole(out_grad.reshape(n_z, n_a, 2, w_rows, group_width), c, z)
    query_grads, key_grads, value_grads = attend_backward(
        info,
        queries,
        k_seq,
        v_seq,
        attended_grad,
        jnp.transpose(log_sums, (0, 2, 1)),
        jnp.transpose(delta, (0, 2, 1)),
    )
    kv_seq_grad = jnp.concatenate([key_grads, value_grads], 1)
    from_after = lax.ppermute(
        kv_seq_grad[:rows].astype(bf16), "z", [(i + 1, i) for i in range(0, n_z, 2)]
    )
    kv_parts = jnp.where(
        second, kv_seq_grad[rows:], kv_seq_grad[:rows] + from_after.astype(f32)
    ).astype(bf16)
    key_part, value_part = kv_parts[:, :group_width], kv_parts[:, group_width:]
    query_grad = jnp.stack([dot(normed_one, query_grads[r], TN) for r in range(n_z)]).astype(bf16)
    key_grad = dot(normed_one, key_part, TN).astype(bf16)
    value_grad = dot(normed_one, value_part, TN).astype(bf16)
    normed_one_grad = project_back(
        query_grads, query_groups, dot(key_part, w_key, NT) + dot(value_part, w_value, NT)
    )
    input_back, gain_one_grad = norm_back(inputs, gain_vals[0], normed_one_grad)
    input_grad = middle_grad + input_back

    def by_owner(matrix):
        return jnp.transpose(
            matrix.reshape(n_a, 2, n_z, kv_rows, -1), (2, 0, 1, 3, 4)
        )

    gain_parts = jnp.stack([gain_one_grad, gain_two_grad]).astype(bf16)
    gain_parts = jnp.transpose(gain_parts.reshape(2, n_a, 2, n_z, kv_rows), (3, 1, 2, 0, 4))
    gain_parts = gain_parts.reshape(n_z, n_a, 2, 1, 2 * kv_rows)
    gain_parts = jnp.pad(gain_parts, ((0, 0),) * 4 + ((0, group_width - 2 * kv_rows),))
    tail_pack = jnp.concatenate(
        [
            query_grad.reshape(n_z, n_a, 2, w_rows, group_width),
            by_owner(key_grad),
            by_owner(value_grad),
            gain_parts,
        ],
        3,
    )
    tail_g = reduce_whole(tail_pack, c, z)
    query_g = tail_g[:w_rows]
    kv_g = tail_g[w_rows : w_rows + 2 * kv_rows].reshape(2, kv_rows, group_width)
    gains_g = tail_g[w_rows + 2 * kv_rows, : 2 * kv_rows].reshape(2, kv_rows)

    first_query, second_query, new_query = adamw_step(
        w_query, query_g, m_query, v_query, rate_query, decay_rate
    )
    first_kv, second_kv, new_kv = adamw_step(w_kv, kv_g, m_kv, v_kv, rate_shared, decay_rate)
    first_out, second_out, new_out = adamw_step(
        w_out, out_g.T, m_out, v_out, rate_output, decay_rate
    )
    first_gate_up, second_gate_up, new_gate_up = adamw_step(
        w_gate_up, ffn_g[:2], m_gate_up, v_gate_up, rate_gate_up, decay_rate
    )
    first_down, second_down, new_down = adamw_step(
        w_down, ffn_g[2].T, m_down, v_down, rate_down, decay_rate
    )
    first_gains, second_gains, new_gains = adamw_step(
        norm_gains, gains_g, m_gains, v_gains, rate_gains, 0.0
    )
    return (
        layer_out,
        input_grad,
        first_query,
        second_query,
        new_query,
        first_kv,
        second_kv,
        new_kv,
        first_out,
        second_out,
        new_out,
        first_gate_up,
        second_gate_up,
        new_gate_up,
        first_down,
        second_down,
        new_down,
        first_gains,
        second_gains,
        new_gains,
    )


def solution(mesh):
    n_dp, n_tensor = mesh.shape["dp"], mesh.shape["tensor"]
    fine = Mesh(mesh.devices.reshape(n_dp // 2, 2, n_tensor), ("a", "c", "z"))
    dp, every = ("a", "c"), ("a", "c", "z")
    token = P(every, None)
    query = P(dp, "z")
    shared = P(None, every, None)
    output = P("z", dp)
    gate_up = P(None, dp, "z")
    gains = P(None, every)
    in_specs = (token, token, P(dp), query, shared, output, gate_up, output, gains)
    in_specs += (query, query, shared, shared, output, output, gate_up, gate_up)
    in_specs += (output, output, gains, gains)
    out_specs = (token, token) + (query,) * 3 + (shared,) * 3 + (output,) * 3
    out_specs += (gate_up,) * 3 + (output,) * 3 + (gains,) * 3
    return jax.shard_map(body, mesh=fine, in_specs=in_specs, out_specs=out_specs, check_vma=False)
```

```python
import functools

import jax
import jax.numpy as jnp
from jax import lax
from jax.experimental import pallas as pl
from jax.experimental.pallas import tpu as pltpu
from jax.sharding import Mesh, PartitionSpec as P

KV = 5
HD = 64
LEN = 1024
STEP = 10
RB = 256

beta_one = 0.9
beta_two = 0.95
adam_eps = 1e-08
decay_rate = 0.1
rate_query = 0.06
rate_shared = 0.06
rate_output = 0.8
rate_gate_up = 0.06
rate_down = 0.05
rate_gains = 0.6
norm_eps = 1e-05
neg_fill = -1e30

bf16 = jnp.bfloat16
f32 = jnp.float32
NN = (((1,), (0,)), ((), ()))
NT = (((1,), (1,)), ((), ()))
TN = (((0,), (0,)), ((), ()))
VMEM_LIMIT = 52 * 2**20
WIDE = 2 * KV * HD


def dot(a, b, dims=NN):
    return lax.dot_general(a, b, dims, preferred_element_type=f32)


def rms_scale(matrix):
    return lax.rsqrt(jnp.mean(matrix * matrix, axis=-1, keepdims=True) + norm_eps)


def norm_back(matrix, gain_row, upstream):
    scaling = rms_scale(matrix)
    unit_rows = matrix * scaling
    weighted = upstream * gain_row
    inner_mean = jnp.mean(weighted * unit_rows, axis=-1, keepdims=True)
    return (scaling * (weighted - unit_rows * inner_mean), jnp.sum(upstream * unit_rows, axis=0))


def adamw_step(weight, gradient, moment_one, moment_two, step_rate, decay_coef):
    moment_one = beta_one * moment_one + (1.0 - beta_one) * gradient
    moment_two = beta_two * moment_two + (1.0 - beta_two) * gradient * gradient
    unbiased_one = moment_one / (1.0 - beta_one**STEP)
    unbiased_two = moment_two / (1.0 - beta_two**STEP)
    updated = weight - step_rate * (
        unbiased_one / (jnp.sqrt(unbiased_two) + adam_eps) + decay_coef * weight
    )
    return (moment_one, moment_two, updated)


def columns_to_rows(columns):
    n = columns[0].shape[0]
    wide = jnp.concatenate(columns + [jnp.zeros((n, 128 - len(columns)), f32)], 1)
    return jnp.transpose(wide)[:8]


def params(flops, megabytes, transcendentals=0):
    return dict(
        compiler_params=pltpu.CompilerParams(vmem_limit_bytes=VMEM_LIMIT),
        cost_estimate=pl.CostEstimate(
            flops=int(flops), bytes_accessed=int(megabytes * 1e6), transcendentals=transcendentals
        ),
    )


def attend_forward_kernel(info, q_ref, before_ref, own_ref, o_ref, lse_ref, *, rows):
    second, prefix = info[0], info[1]
    width = KV * HD

    def run(is_second):
        for block in range(rows // RB):
            base = (rows if is_second else 0) + block * RB
            row_slice = slice(block * RB, (block + 1) * RB)
            if is_second:
                spans = [(before_ref, 0, rows, None)]
                if block:
                    spans.append((own_ref, 0, block * RB, None))
                spans.append((own_ref, block * RB, RB, rows + block * RB))
            else:
                spans = [(own_ref, 0, rows, 0)]
            masks = []
            for _, _, count, masked in spans:
                if masked is None:
                    masks.append(None)
                else:
                    at = lax.broadcasted_iota(jnp.int32, (RB, count), 1) + masked
                    row = lax.broadcasted_iota(jnp.int32, (RB, count), 0) + base
                    masks.append((at <= row) | (at < prefix))
            outs, logs = [], []
            for c in range(KV):
                cols = slice(c * HD, (c + 1) * HD)
                values = slice(width + c * HD, width + (c + 1) * HD)
                query = q_ref[0, row_slice, cols]
                scores = []
                for (ref, start, count, _), mask in zip(spans, masks):
                    part = dot(query, ref[start : start + count, cols], NT)
                    scores.append(part if mask is None else jnp.where(mask, part, neg_fill))
                highest = functools.reduce(
                    jnp.maximum, [jnp.max(s, axis=1, keepdims=True) for s in scores]
                )
                total, mixed = 0.0, 0.0
                for (ref, start, count, _), part in zip(spans, scores):
                    expo = jnp.exp(part - highest)
                    total = total + jnp.sum(expo, axis=1, keepdims=True)
                    mixed = mixed + dot(expo.astype(bf16), ref[start : start + count, values])
                outs.append((mixed / total).astype(bf16))
                logs.append(highest + jnp.log(total))
            o_ref[0, row_slice, :] = jnp.concatenate(outs, 1)
            lse_ref[0, :, row_slice] = columns_to_rows(logs)

    pl.when(second == 0)(lambda: run(False))
    pl.when(second == 1)(lambda: run(True))


def attend_forward(info, queries, before, own):
    groups, rows, width = queries.shape
    block = pl.BlockSpec((1, rows, width), lambda r, _: (r, 0, 0))
    whole = pl.BlockSpec(own.shape, lambda r, _: (0, 0))
    elements = groups * rows * KV * 2 * rows
    return pl.pallas_call(
        functools.partial(attend_forward_kernel, rows=rows),
        grid_spec=pltpu.PrefetchScalarGridSpec(
            num_scalar_prefetch=1,
            grid=(groups,),
            in_specs=[block, whole, whole],
            out_specs=[block, pl.BlockSpec((1, 8, rows), lambda r, _: (r, 0, 0))],
        ),
        out_shape=[
            jax.ShapeDtypeStruct(queries.shape, bf16),
            jax.ShapeDtypeStruct((groups, 8, rows), f32),
        ],
        name="attend_forward",
        **params(elements * 900, 4, elements),
    )(info, queries, before, own)


def attend_backward_kernel(
    info, q_ref, before_ref, own_ref, do_ref, lse_ref, delta_ref, dq_ref, first_ref, last_ref, dk_acc, dv_acc, *, rows
):
    second, prefix = info[0], info[1]
    group = pl.program_id(0)
    width = KV * HD

    @pl.when(group == 0)
    def _():
        dk_acc[...] = jnp.zeros_like(dk_acc)
        dv_acc[...] = jnp.zeros_like(dv_acc)

    def run(is_second):
        for block in range(rows // RB):
            base = (rows if is_second else 0) + block * RB
            row_slice = slice(block * RB, (block + 1) * RB)
            steps = rows // RB
            if is_second:
                spans = [(before_ref, i * RB, i * RB, False) for i in range(steps)]
                spans += [(own_ref, i * RB, rows + i * RB, i == block) for i in range(block + 1)]
            else:
                spans = [(own_ref, i * RB, i * RB, True) for i in range(steps)]
            query_grads = []
            for c in range(KV):
                cols = slice(c * HD, (c + 1) * HD)
                values = slice(width + c * HD, width + (c + 1) * HD)
                query, out_grad = q_ref[0, row_slice, cols], do_ref[0, row_slice, cols]
                log_sum = lse_ref[0, c : c + 1, row_slice]
                delta = delta_ref[0, c : c + 1, row_slice]
                query_grad = jnp.zeros((RB, HD), f32)
                for ref, start, position, masked in spans:
                    key, value = ref[start : start + RB, cols], ref[start : start + RB, values]
                    scores = dot(key, query, NT) - log_sum
                    if masked:
                        at = lax.broadcasted_iota(jnp.int32, (RB, RB), 0) + position
                        row = lax.broadcasted_iota(jnp.int32, (RB, RB), 1) + base
                        scores = jnp.where((at <= row) | (at < prefix), scores, neg_fill)
                    probs = jnp.exp(scores)
                    probs_grad = dot(value, out_grad, NT)
                    score_grad = (probs * (probs_grad - delta)).astype(bf16)
                    at_keys = slice(position, position + RB)
                    dv_acc[c, at_keys, :] += dot(probs.astype(bf16), out_grad)
                    dk_acc[c, at_keys, :] += dot(score_grad, query)
                    query_grad = query_grad + dot(score_grad, key, TN)
                query_grads.append((query_grad * HD**-0.5).astype(bf16))
            dq_ref[0, row_slice, :] = jnp.concatenate(query_grads, 1)

    pl.when(second == 0)(lambda: run(False))
    pl.when(second == 1)(lambda: run(True))

    @pl.when(group == pl.num_programs(0) - 1)
    def _():
        for ref, part in ((first_ref, slice(0, rows)), (last_ref, slice(rows, 2 * rows))):
            ref[...] = jnp.concatenate(
                [acc[c, part, :] for acc in (dk_acc, dv_acc) for c in range(KV)], 1
            )


def attend_backward(info, queries, before, own, out_grad, log_sums, delta):
    groups, rows, width = queries.shape
    block = pl.BlockSpec((1, rows, width), lambda r, _: (r, 0, 0))
    whole = pl.BlockSpec(own.shape, lambda r, _: (0, 0))
    stats = pl.BlockSpec((1, 8, rows), lambda r, _: (r, 0, 0))
    elements = groups * rows * KV * 2 * rows
    return pl.pallas_call(
        functools.partial(attend_backward_kernel, rows=rows),
        grid_spec=pltpu.PrefetchScalarGridSpec(
            num_scalar_prefetch=1,
            grid=(groups,),
            in_specs=[block, whole, whole, block, stats, stats],
            out_specs=[block, whole, whole],
            scratch_shapes=[pltpu.VMEM((KV, 2 * rows, HD), f32)] * 2,
        ),
        out_shape=[jax.ShapeDtypeStruct(queries.shape, bf16)]
        + [jax.ShapeDtypeStruct(own.shape, f32)] * 2,
        name="attend_backward",
        **params(elements * 2500, 8, elements),
    )(info, queries, before, own, out_grad, log_sums, delta)


BLOCKS = 4
SWAPPED = (0, 2, 1, 3)


def block_row(info, j, other):
    return (((info[2] ^ j) * 2) + (info[3] ^ other)) * 160


def pair_of(ref):
    return jnp.concatenate([ref[0], ref[1]], 1)


def put_together(info, refs, w_ref):
    width = KV * HD
    for i, ref in enumerate(refs):
        part, other = i // 2, i % 2
        for j in range(BLOCKS):
            at = block_row(info, SWAPPED[j] if part else j, other) + part * 80
            block = ref[j]
            w_ref[pl.ds(pl.multiple_of(at, 16), 80), :] = jnp.concatenate(
                [block[:80, :width], block[80:, :width]], 1
            )


def shared_kernel(info, tok_ref, ka, kb, va, vb, normed_ref, normed_t_ref, kv_ref, gain_ref, wkv_ref, gains):
    width = KV * HD
    for other, (k_ref, v_ref) in enumerate(((ka, va), (kb, vb))):
        for j in range(BLOCKS):
            at = pl.ds(pl.multiple_of(block_row(info, j, other), 160), 160)
            wkv_ref[at, :width] = k_ref[j][:, :width]
            gains[0, at, :] = k_ref[j][:, 256:].astype(f32)
            at = pl.ds(pl.multiple_of(block_row(info, SWAPPED[j], other), 160), 160)
            wkv_ref[at, width:] = v_ref[j][:, :width]
            gains[1, at, :] = v_ref[j][:, 256:].astype(f32)
    one = jnp.transpose(gains[0])[64:72]
    two = jnp.transpose(gains[1])[64:72]
    gain_ref[...] = jnp.concatenate([one[:1], two[:1], jnp.zeros((6, one.shape[1]), f32)], 0)
    tok = tok_ref[...].astype(f32)
    normed = (tok * rms_scale(tok) * one[:1]).astype(bf16)
    normed_ref[...] = normed
    normed_t_ref[...] = jnp.transpose(normed)
    kv_ref[...] = dot(normed, wkv_ref[...]).astype(bf16)


def project_shared(info, tokens, parts):
    rows, depth = tokens.shape
    width = 2 * KV * HD
    whole = lambda *shape: pl.BlockSpec(shape, lambda i, _: (0,) * len(shape))
    block = pl.BlockSpec((BLOCKS, 160, 384), lambda i, _: (0, 4, 0))
    return pl.pallas_call(
        shared_kernel,
        grid_spec=pltpu.PrefetchScalarGridSpec(
            num_scalar_prefetch=1,
            grid=(1,),
            in_specs=[whole(rows, depth)] + [block] * 4,
            out_specs=[
                whole(rows, depth),
                whole(depth, rows),
                whole(rows, width),
                whole(8, depth),
                whole(depth, width),
            ],
            scratch_shapes=[pltpu.VMEM((2, depth, 128), f32)],
        ),
        out_shape=[
            jax.ShapeDtypeStruct((rows, depth), bf16),
            jax.ShapeDtypeStruct((depth, rows), bf16),
            jax.ShapeDtypeStruct((rows, width), bf16),
            jax.ShapeDtypeStruct((8, depth), f32),
            jax.ShapeDtypeStruct((depth, width), bf16),
        ],
        name="project_shared",
        **params(2 * rows * depth * width, 8),
    )(info, tokens, *parts)


def query_kernel(info, x_ref, a0, b0, a1, b1, q_ref, w_ref):
    put_together(info, (a0, b0, a1, b1), w_ref)
    result = (dot(x_ref[...], w_ref[...]).astype(bf16) * HD**-0.5).astype(bf16)
    q_ref[0] = result[:, : KV * HD]
    q_ref[1] = result[:, KV * HD :]


def project_queries(info, normed, parts):
    rows, depth = normed.shape
    block = pl.BlockSpec((BLOCKS, 160, 384), lambda r, _: (0, r, 0))
    return pl.pallas_call(
        query_kernel,
        grid_spec=pltpu.PrefetchScalarGridSpec(
            num_scalar_prefetch=1,
            grid=(2,),
            in_specs=[pl.BlockSpec((rows, depth), lambda r, _: (0, 0))] + [block] * 4,
            out_specs=[
                pl.BlockSpec((2, rows, WIDE // 2), lambda r, _: (r, 0, 0)),
                pl.BlockSpec((depth, WIDE), lambda r, _: (0, r)),
            ],
        ),
        out_shape=[
            jax.ShapeDtypeStruct((4, rows, WIDE // 2), bf16),
            jax.ShapeDtypeStruct((depth, 2 * WIDE), bf16),
        ],
        name="project_queries",
        **params(4 * rows * depth * WIDE, 10),
    )(info, normed, *parts)


def output_kernel(
    info, att_ref, a0, b0, a1, b1, tok_ref, gain_ref, middle_ref, normed_ref, w_ref, acc
):
    put_together(info, (a0, b0, a1, b1), w_ref)
    part = dot(pair_of(att_ref), w_ref[...], NT)

    @pl.when(pl.program_id(0) == 0)
    def _():
        acc[...] = tok_ref[...].astype(f32) + part

    @pl.when(pl.program_id(0) == 1)
    def _():
        middle = acc[...] + part
        middle_ref[...] = middle
        normed_ref[...] = (middle * rms_scale(middle) * gain_ref[1:2]).astype(bf16)


def project_output(info, attended, parts, tokens, gains):
    rows, depth = tokens.shape
    block = pl.BlockSpec((BLOCKS, 160, 384), lambda r, _: (0, 2 + r, 0))
    whole = lambda *shape: pl.BlockSpec(shape, lambda r, _: (0,) * len(shape))
    return pl.pallas_call(
        output_kernel,
        grid_spec=pltpu.PrefetchScalarGridSpec(
            num_scalar_prefetch=1,
            grid=(2,),
            in_specs=[pl.BlockSpec((2, rows, WIDE // 2), lambda r, _: (r, 0, 0))]
            + [block] * 4
            + [whole(rows, depth), whole(8, depth)],
            out_specs=[
                whole(rows, depth),
                whole(rows, depth),
                pl.BlockSpec((depth, WIDE), lambda r, _: (0, r)),
            ],
            scratch_shapes=[pltpu.VMEM((rows, depth), f32)],
        ),
        out_shape=[
            jax.ShapeDtypeStruct((rows, depth), f32),
            jax.ShapeDtypeStruct((rows, depth), bf16),
            jax.ShapeDtypeStruct((depth, 2 * WIDE), bf16),
        ],
        name="project_output",
        **params(4 * rows * depth * WIDE, 14),
    )(info, attended, *parts, tokens, gains)


def feed_forward_kernel(xa, xb, ca, cb, w_ref, inner_ref, out_a, out_b, back_a, back_b):
    def run(x_ref, c_ref, out_ref, back_ref):
        x, cot = x_ref[...], c_ref[...]
        gate = dot(x, w_ref[0])
        up = dot(x, w_ref[1])
        hidden_grad = dot(cot, w_ref[2])
        sig = jax.nn.sigmoid(gate)
        silu = gate * sig
        hidden = (silu * up).astype(bf16)
        inner_ref[2] = hidden
        gate_grad = (hidden_grad * up * sig * (1.0 + gate * (1.0 - sig))).astype(bf16)
        inner_ref[0] = gate_grad
        up_grad = (hidden_grad * silu).astype(bf16)
        inner_ref[1] = up_grad
        out_ref[...] = dot(hidden, w_ref[2], NT).astype(bf16)
        back_ref[...] = (dot(gate_grad, w_ref[0], NT) + dot(up_grad, w_ref[1], NT)).astype(bf16)

    pl.when(pl.program_id(0) < pl.num_programs(0) // 2)(lambda: run(xa, ca, out_a, back_a))
    pl.when(pl.program_id(0) >= pl.num_programs(0) // 2)(lambda: run(xb, cb, out_b, back_b))


def feed_forward(normed, cots, weights):
    rows, depth = normed[0].shape
    width = weights.shape[2]
    tile = 256
    steps = rows // tile
    first = pl.BlockSpec((tile, depth), lambda i: (jnp.minimum(i, steps - 1), 0))
    last = pl.BlockSpec((tile, depth), lambda i: (jnp.maximum(i - steps, 0), 0))
    inner = pl.BlockSpec((3, tile, width), lambda i: (0, i, 0))
    whole = pl.BlockSpec(weights.shape, lambda i: (0, 0, 0), pipeline_mode=pl.Buffered(1))
    return pl.pallas_call(
        feed_forward_kernel,
        grid=(2 * steps,),
        in_specs=[first, last, first, last, whole],
        out_specs=[inner, first, last, first, last],
        out_shape=[jax.ShapeDtypeStruct((3, 2 * rows, width), bf16)]
        + [jax.ShapeDtypeStruct((rows, depth), bf16)] * 4,
        name="feed_forward",
        **params(24 * rows * depth * width, 24),
    )(*normed, *cots, weights)


def hidden_grad_kernel(x0, x1, x2, x3, c0, c1, c2, c3, near_ref, far_ref, out_ref):
    def run(lefts):
        rows = lefts[0].shape[0]
        total = 0.0
        for left, (right, at) in zip(lefts, ((near_ref, 0), (near_ref, 1), (far_ref, 0), (far_ref, 1))):
            total = total + dot(left[...], right[0, at * rows : (at + 1) * rows, :], TN)
        out_ref[0] = total.astype(bf16)

    pl.when(pl.program_id(0) < 2)(lambda: run((x0, x1, x2, x3)))
    pl.when(pl.program_id(0) == 2)(lambda: run((c0, c1, c2, c3)))


def hidden_grads(normed, cots, near, far):
    rows, depth = normed[0].shape
    width = near.shape[2]
    tile = 640
    last = depth // tile - 1
    left = pl.BlockSpec((rows, tile), lambda m, i: (0, jnp.where(m < 2, i, last)))
    cot = pl.BlockSpec((rows, tile), lambda m, i: (0, jnp.where(m < 2, 0, i)))
    right = pl.BlockSpec((1, 2 * rows, width), lambda m, i: (m, 0, 0))
    return pl.pallas_call(
        hidden_grad_kernel,
        grid=(3, depth // tile),
        in_specs=[left] * 4 + [cot] * 4 + [right] * 2,
        out_specs=pl.BlockSpec((1, tile, width), lambda m, i: (m, i, 0)),
        out_shape=jax.ShapeDtypeStruct((3, depth, width), bf16),
        name="hidden_grads",
        **params(24 * rows * depth * width, 28),
    )(*normed, *cots, near, far)


def middle_kernel(
    middle_ref, cot_ref, gain_ref, near_ref, core_ref, far_ref, w_ref, att_ref,
    grad_ref, low_t_ref, gain_grad_ref, do_ref, delta_ref, low,
):
    @pl.when(pl.program_id(0) == 0)
    def _():
        upstream = near_ref[...].astype(f32) + core_ref[...].astype(f32) + far_ref[...].astype(f32)
        middle = middle_ref[...]
        scaling = rms_scale(middle)
        unit_rows = middle * scaling
        gain_grad = jnp.sum(upstream * unit_rows, axis=0, keepdims=True)
        gain_grad_ref[...] = jnp.broadcast_to(gain_grad, gain_grad_ref.shape)
        weighted = upstream * gain_ref[1:2]
        inner_mean = jnp.mean(weighted * unit_rows, axis=-1, keepdims=True)
        grad = cot_ref[...].astype(f32) + scaling * (weighted - unit_rows * inner_mean)
        grad_ref[...] = grad
        low[...] = grad.astype(bf16)
        low_t_ref[...] = jnp.transpose(low[...])

    grad = dot(low[...], w_ref[...]).astype(bf16)
    do_ref[0] = grad[:, : WIDE // 2]
    do_ref[1] = grad[:, WIDE // 2 :]
    product = grad.astype(f32) * pair_of(att_ref).astype(f32)
    high = product.astype(bf16)
    rest = (product - high.astype(f32)).astype(bf16)
    row = lax.broadcasted_iota(jnp.int32, (16, WIDE), 0)
    head = jnp.where(row < 8, jnp.where(row < KV, row, -1), jnp.where(row < 8 + KV, row - 8 + KV, -1))
    column = lax.broadcasted_iota(jnp.int32, (16, WIDE), 1)
    member = ((column >= head * HD) & (column < (head + 1) * HD)).astype(f32).astype(bf16)
    delta = dot(member, high, NT) + dot(member, rest, NT)
    delta_ref[0] = delta[:8]
    delta_ref[1] = delta[8:]


def middle_backward(middle, cot, gains, near, core, far, w_out, attended):
    rows, depth = middle.shape
    block = pl.BlockSpec((2, rows, WIDE // 2), lambda r: (r, 0, 0))
    whole = lambda *shape: pl.BlockSpec(shape, lambda r: (0,) * len(shape))
    token = whole(rows, depth)
    return pl.pallas_call(
        middle_kernel,
        grid=(2,),
        in_specs=[token, token, whole(8, depth), token, token, token]
        + [pl.BlockSpec((depth, WIDE), lambda r: (0, r)), block],
        out_specs=[
            token,
            whole(depth, rows),
            whole(8, depth),
            block,
            pl.BlockSpec((2, 8, rows), lambda r: (r, 0, 0)),
        ],
        out_shape=[
            jax.ShapeDtypeStruct((rows, depth), f32),
            jax.ShapeDtypeStruct((depth, rows), bf16),
            jax.ShapeDtypeStruct((8, depth), f32),
            jax.ShapeDtypeStruct((4, rows, WIDE // 2), bf16),
            jax.ShapeDtypeStruct((4, 8, rows), f32),
        ],
        scratch_shapes=[pltpu.VMEM((rows, depth), bf16)],
        name="middle_backward",
        **params(4 * rows * depth * WIDE, 20),
    )(middle, cot, gains, near, core, far, w_out, attended)


def input_kernel(
    dq_ref, wq_ref, dkv_ref, wkv_ref, tok_ref, gain_ref, grad_ref, two_ref, out_ref, gain_grad_ref, acc
):
    group = pl.program_id(0)

    @pl.when(group == 0)
    def _():
        acc[...] = dot(dkv_ref[...], wkv_ref[...], NT)

    acc[...] += dot(pair_of(dq_ref), wq_ref[...], NT)

    @pl.when(group == pl.num_programs(0) - 1)
    def _():
        upstream = acc[...]
        tok = tok_ref[...].astype(f32)
        scaling = rms_scale(tok)
        unit_rows = tok * scaling
        one = jnp.sum(upstream * unit_rows, axis=0, keepdims=True)
        gain_grad_ref[...] = jnp.concatenate([one, two_ref[:7]], 0)
        weighted = upstream * gain_ref[0:1]
        inner_mean = jnp.mean(weighted * unit_rows, axis=-1, keepdims=True)
        out_ref[...] = grad_ref[...] + scaling * (weighted - unit_rows * inner_mean)


def input_backward(dq, wq, dkv, wkv, tokens, gains, middle_grad, gain_two):
    rows, depth = tokens.shape
    whole = lambda *shape: pl.BlockSpec(shape, lambda r: (0,) * len(shape))
    token = whole(rows, depth)
    return pl.pallas_call(
        input_kernel,
        grid=(2,),
        in_specs=[
            pl.BlockSpec((2, rows, WIDE // 2), lambda r: (r, 0, 0)),
            pl.BlockSpec((depth, WIDE), lambda r: (0, r)),
            whole(*dkv.shape),
            whole(*wkv.shape),
            token,
            whole(8, depth),
            token,
            whole(8, depth),
        ],
        out_specs=[token, whole(8, depth)],
        out_shape=[
            jax.ShapeDtypeStruct((rows, depth), f32),
            jax.ShapeDtypeStruct((8, depth), f32),
        ],
        scratch_shapes=[pltpu.VMEM((rows, depth), f32)],
        name="input_backward",
        **params(6 * rows * depth * WIDE, 20),
    )(dq, wq, dkv, wkv, tokens, gains, middle_grad, gain_two)


def group_grad_kernel(info, left_ref, right_ref, own_ref, other_ref, whole):
    width = KV * HD
    whole[...] = dot(left_ref[...], pair_of(right_ref)).astype(bf16)
    for other, ref in enumerate((own_ref, other_ref)):
        for j in range(BLOCKS):
            at = pl.multiple_of(block_row(info, j, other), 160)
            block = whole[pl.ds(at, 160), :]
            for low in range(2):
                ref[j, (info[4] & 1) ^ low] = block[:, low * width : (low + 1) * width]


def group_grads(info, left, right):
    groups, rows, width = right.shape
    depth = left.shape[0]
    block = pl.BlockSpec((BLOCKS, 2, 160, width), lambda r, _: (0, r, 0, 0))
    return pl.pallas_call(
        group_grad_kernel,
        grid_spec=pltpu.PrefetchScalarGridSpec(
            num_scalar_prefetch=1,
            grid=(2,),
            in_specs=[
                pl.BlockSpec((depth, rows), lambda r, _: (0, 0)),
                pl.BlockSpec((2, rows, width), lambda r, info: (r ^ (info[4] >> 1), 0, 0)),
            ],
            out_specs=[block] * 2,
            scratch_shapes=[pltpu.VMEM((depth, WIDE), bf16)],
        ),
        out_shape=[jax.ShapeDtypeStruct((BLOCKS, groups, 160, width), bf16)] * 2,
        name="group_grads",
        **params(4 * rows * depth * WIDE, 6),
    )(info, left, right)


def shared_grad_kernel(info, left_ref, right_ref, gain_ref, own_ref, other_ref, whole):
    wide = jnp.concatenate([gain_ref[...], jnp.zeros((120, gain_ref.shape[1]), f32)], 0)
    width = right_ref.shape[1]
    whole[:, width:] = jnp.transpose(wide).astype(bf16)
    whole[:, :width] = dot(left_ref[...], right_ref[...]).astype(bf16)
    for other, ref in enumerate((own_ref, other_ref)):
        for j in range(BLOCKS):
            at = pl.ds(pl.multiple_of(block_row(info, j, other), 160), 160)
            ref[j] = whole[at, :]


def shared_grads(info, left, right, gain_grads):
    rows, width = right.shape
    depth = left.shape[0]
    whole = lambda *shape: pl.BlockSpec(shape, lambda i, _: (0,) * len(shape))
    return pl.pallas_call(
        shared_grad_kernel,
        grid_spec=pltpu.PrefetchScalarGridSpec(
            num_scalar_prefetch=1,
            grid=(1,),
            in_specs=[whole(depth, rows), whole(rows, width), whole(8, depth)],
            out_specs=[whole(BLOCKS, 160, width + 128)] * 2,
            scratch_shapes=[pltpu.VMEM((depth, width + 128), bf16)],
        ),
        out_shape=[jax.ShapeDtypeStruct((BLOCKS, 160, width + 128), bf16)] * 2,
        name="shared_grads",
        **params(2 * rows * depth * width, 6),
    )(info, left, right, gain_grads)


def swap(value, axis, bit):
    size = lax.axis_size(axis)
    return lax.ppermute(value, axis, [(i, i ^ bit) for i in range(size)])


def core_swap(value):
    return swap(value, "c", 1)


def placed(own, other, bit, axis=0):
    return jnp.concatenate(
        [jnp.where(bit == 0, own, other), jnp.where(bit == 0, other, own)], axis
    )


def gather_line(own, z):
    pair = placed(own, swap(own, "z", 2), z // 2)
    size = own.shape[0]
    near = swap(pair, "z", 1)
    both = [jnp.where(z % 2 == 0, pair, near), jnp.where(z % 2 == 0, near, pair)]
    return jnp.concatenate(
        [part[i * size : (i + 1) * size] for i in range(2) for part in both], 0
    )


def gather_plane(own, bits):
    blocks = own[None]
    for bit in bits:
        blocks = jnp.concatenate([blocks, swap(blocks, "a", bit)], 0)
    return blocks


def add(one, two, kind=bf16):
    return (one.astype(f32) + two.astype(f32)).astype(kind)


def reduce_core(parts):
    own, other = parts
    return add(own, core_swap(other))


def reduce_plane(blocks, bits):
    if bits[0] == 1:
        blocks = blocks.reshape((2, 2) + blocks.shape[1:])
        blocks = add(blocks[:, 0], swap(blocks[:, 1], "a", 1))
    else:
        blocks = add(blocks[:2], swap(blocks[2:], "a", 2))
    return add(blocks[0], swap(blocks[1], "a", bits[1]))


def pick(stacked, index, axis=0):
    return lax.dynamic_index_in_dim(stacked, index, axis, keepdims=False)


def after(value, *earlier):
    return lax.optimization_barrier((value,) + earlier)[0]


def head_weights(w_query, w_kv, w_out, norm_gains, z):
    w_rows, group_width = w_query.shape
    kv_rows = w_kv.shape[1]
    n_a, n_z = lax.axis_size("a"), lax.axis_size("z")
    pad = lambda m: jnp.pad(m.astype(bf16), ((0, 0), (0, 384 - m.shape[1])))
    shared = [pad(jnp.concatenate([w_kv[i], norm_gains[i][:, None]], 1)) for i in range(2)]
    query, output = pad(w_query), pad(w_out.T)
    if n_a == BLOCKS:
        half = w_rows // 2
        line = gather_line(jnp.concatenate([query, output] + shared, 0)[None], z)
        packs = []
        for i, bits in enumerate(((1, 2), (2, 1))):
            starts = (i * half, w_rows + i * half, 2 * w_rows + i * kv_rows)
            counts = (half, half, kv_rows)
            own = [line[:, s : s + n].reshape(n_z * n, 384) for s, n in zip(starts, counts)]
            packs.append(gather_plane(jnp.concatenate(own, 0), bits))
        return packs, line
    every = ("a", "c", "z")

    def groups(own):
        got = lax.all_gather(own, every, axis=0).reshape(2 * n_a, n_z, w_rows, 384)
        return jnp.transpose(got, (1, 0, 2, 3)).reshape(n_z, BLOCKS, 2, 160, 384)

    query, output = groups(query), groups(output)
    result = []
    for i in range(2):
        kv = lax.all_gather(shared[i], every, axis=0).reshape(BLOCKS, 2, 160, 384)
        halves = [
            jnp.transpose(m[:, :, :, i * 80 : (i + 1) * 80], (1, 2, 0, 3, 4)).reshape(
                BLOCKS, 2, n_z * 80, 384
            )
            for m in (query, output)
        ]
        part = jnp.concatenate(halves + [kv], 2)
        if i:
            part = part[jnp.array(SWAPPED)]
        result += [part[:, 0], part[:, 1]]
    return result, query


def body(
    tokens,
    cotangent,
    prefix_len,
    w_query,
    w_kv,
    w_out,
    w_gate_up,
    w_down,
    norm_gains,
    m_query,
    v_query,
    m_kv,
    v_kv,
    m_out,
    v_out,
    m_gate_up,
    v_gate_up,
    m_down,
    v_down,
    m_gains,
    v_gains,
):
    rows, width = tokens.shape
    a, c, z = lax.axis_index("a"), lax.axis_index("c"), lax.axis_index("z")
    n_a, n_z = lax.axis_size("a"), lax.axis_size("z")
    plane = n_a == BLOCKS
    w_rows, group_width = w_query.shape
    kv_rows = w_kv.shape[1]
    hidden_width = w_gate_up.shape[2]
    second = (z % (LEN // rows)) == 1
    seq_at = z // (LEN // rows)
    at = [a, c, z] if plane else [0, 0, 0]
    info = jnp.stack([second, pick(prefix_len, seq_at)] + at).astype(jnp.int32)

    ffn_own = jnp.concatenate([w_gate_up, w_down.T[None]], 0).astype(bf16)
    cross = [(n_z + zz, zz) for zz in range(n_z)] + [(zz, n_z + (zz ^ 2)) for zz in range(n_z)]
    far_core = [(n_z + zz, n_z + (zz ^ 2)) for zz in range(n_z)]
    parts, line = head_weights(w_query, w_kv, w_out, norm_gains, z)
    ffn_own = after(ffn_own, line)
    crossed = lax.ppermute(ffn_own, ("c", "z"), cross)
    shifted = lax.ppermute(ffn_own, ("c", "z"), far_core)
    ffn_first = jnp.where(c == 0, ffn_own, crossed)
    ffn_second = jnp.where(c == 0, crossed, shifted)
    ffn_blocks = jnp.concatenate([ffn_first, ffn_second], 1)
    if plane:
        ffn_blocks = after(ffn_blocks, *parts)
        parts = parts[0], core_swap(parts[0]), parts[1], core_swap(parts[1])
    ffn_w = lax.all_gather(ffn_blocks, "a", axis=1, tiled=True)

    normed_one, normed_one_t, kv_own, gains, w_shared = project_shared(info, tokens, parts)
    before = lax.ppermute(kv_own, "z", [(i, i + 1) for i in range(0, n_z, 2)])
    queries, w_groups = project_queries(info, normed_one, parts)
    before = after(before, queries)
    cot_core = core_swap(after(cotangent, before))
    cot_pair = swap(after(cotangent, before), "z", 1)
    attended, log_sums = attend_forward(info, queries, before, kv_own)
    cot_pair = after(cot_pair, attended)
    cots = cotangent, cot_core, cot_pair, core_swap(cot_pair)
    middle, normed_two, out_groups = project_output(
        info, attended, parts, after(tokens, cots[3]), gains
    )

    two_core, two_pair = core_swap(normed_two), swap(normed_two, "z", 1)
    inner_near, out_own, out_core, back_own, back_core = feed_forward(
        (normed_two, two_core), cots[:2], ffn_w
    )
    back_core = core_swap(back_core)
    two_pair = after(two_pair, inner_near)
    twos = (normed_two, two_core, two_pair, core_swap(two_pair))
    inner_far, out_far, out_far_core, back_far, back_far_core = feed_forward(
        twos[2:], cots[2:], ffn_w
    )
    back_sum = add(back_far, core_swap(back_far_core))
    back_pair = swap(back_sum, "z", 1)
    ffn_grad = hidden_grads(twos, cots, inner_near, after(inner_far, back_sum))
    ffn_sum = lax.psum_scatter(ffn_grad, "a", scatter_dimension=1, tiled=True)

    middle_grad, middle_low_t, gain_two_grad, attended_grad, delta = middle_backward(
        middle, cotangent, gains, back_own, back_core, after(back_pair, ffn_grad), out_groups, attended
    )
    out_parts = group_grads(info, middle_low_t, attended)
    if plane:
        out_sum = reduce_core(out_parts)
        out_keep, out_send = out_sum[:2], out_sum[2:]
        out_recv = swap(out_send, "a", 2)
        attended_grad = after(attended_grad, out_sum)
    out_pair = swap(after(add(out_far, core_swap(out_far_core)), attended_grad), "z", 1)
    out_core = core_swap(out_core)
    dq, first_grad, last_grad = attend_backward(
        info, queries, before, kv_own, attended_grad, log_sums, delta
    )
    from_after = lax.ppermute(
        first_grad.astype(bf16), "z", [(i + 1, i) for i in range(0, n_z, 2)]
    )
    query_parts = group_grads(info, normed_one_t, dq)
    if plane:
        query_sum = reduce_core(query_parts)
        first = query_sum[:, :2].reshape((2, 2, 2) + query_sum.shape[2:])
        last = query_sum[:, 2:]
        first_send, last_send = first[:, 1], last[2:]
        from_after = after(from_after, first_send, last_send)
        first_recv, last_recv = swap(first_send, "a", 1), swap(last_send, "a", 2)
    dkv = jnp.where(second, last_grad, first_grad + from_after.astype(f32)).astype(bf16)
    input_grad, gain_grads = input_backward(
        dq, w_groups, dkv, w_shared, tokens, gains, middle_grad, gain_two_grad
    )
    shared_parts = shared_grads(info, normed_one_t, dkv, gain_grads)

    ffn_sum = ffn_sum.reshape(3, 2, w_rows, hidden_width)
    crossed_back = lax.ppermute(
        jnp.where(c == 0, ffn_sum[:, 1], ffn_sum[:, 0]), ("c", "z"), [(d, s) for s, d in cross]
    )
    shifted_back = lax.ppermute(ffn_sum[:, 1], ("c", "z"), far_core)
    if plane:
        shared_own, shared_other = shared_parts
        shared_recv = core_swap(shared_other)
        first = add(first[:, 0], after(first_recv, shared_other))
        last = add(last[:2], after(last_recv, shared_other))
        out_sum = add(out_keep, after(out_recv, shared_other))
        first_recv, last_recv = swap(first[1], "a", 2), swap(last[1], "a", 1)
        out_recv = swap(out_sum[1], "a", 1)
        shared_sum = add(shared_own, after(shared_recv, first, last))
        keys, values = shared_sum[..., :group_width], shared_sum[..., group_width:]
        keys = keys.reshape((2, 2) + keys.shape[1:])
        keys, keys_send, values, values_send = keys[:, 0], keys[:, 1], values[:2], values[2:]
        keys_recv, values_recv = swap(keys_send, "a", 1), swap(values_send, "a", 2)
        first_recv, last_recv, out_recv = (
            after(r, keys_send, values_send) for r in (first_recv, last_recv, out_recv)
        )
        both = jnp.stack(
            [
                jnp.concatenate([add(first[0], first_recv), add(last[0], last_recv)], 0),
                add(out_sum[0], out_recv),
            ]
        ).reshape((2, 2, 2) + first.shape[2:])
        both_send = both[:, :, 1]
        both_recv = swap(both_send, "z", 1)
        keys = add(keys, after(keys_recv, both_send))
        values = add(values, after(values_recv, both_send))
        keys_recv, values_recv = swap(keys[1], "a", 2), swap(values[1], "a", 1)
        both = add(both[:, :, 0], after(both_recv, keys, values))
        both_recv = swap(both[:, 1], "z", 2)
        shared_sum = jnp.concatenate(
            [
                add(keys[0], after(keys_recv, both)),
                add(values[0], after(values_recv, both)),
            ],
            1,
        )
        quarters = shared_sum.reshape(2, 2, kv_rows, -1)
        kept = add(pick(quarters, z % 2, 1), swap(pick(quarters, 1 - z % 2, 1), "z", 1))
        shared_g = add(pick(kept, z // 2), swap(pick(kept, 1 - z // 2), "z", 2), f32)
        both = add(both[:, 0], after(both_recv, kept), f32)
        query_g, out_g = both[0], both[1]
    else:

        def whole_sum(blocks):
            blocks = jnp.stack(blocks, 1)
            blocks = jnp.moveaxis(blocks, 2, 0) if blocks.ndim == 5 else blocks[None]
            blocks = blocks.reshape(blocks.shape[0], width, blocks.shape[-1])
            mine = lax.psum_scatter(blocks, ("a", "c"), scatter_dimension=1, tiled=True)
            return mine.astype(f32)

        query_g = lax.psum_scatter(whole_sum(query_parts), "z", scatter_dimension=0)
        out_g = lax.psum_scatter(whole_sum(out_parts), "z", scatter_dimension=0)
        shared_g = lax.psum_scatter(
            whole_sum(shared_parts)[0], "z", scatter_dimension=0, tiled=True
        )
    ffn_g = add(crossed_back, jnp.where(c == 0, ffn_sum[:, 0], shifted_back), f32)
    kv_g = jnp.stack([shared_g[:, :group_width], shared_g[:, group_width : 2 * group_width]])
    gains_g = shared_g[:, 2 * group_width : 2 * group_width + 2].T

    layer_out = (middle + add(add(out_own, out_core, f32), after(out_pair, shared_parts[0]), f32)).astype(bf16)

    first_query, second_query, new_query = adamw_step(
        w_query, query_g, m_query, v_query, rate_query, decay_rate
    )
    first_kv, second_kv, new_kv = adamw_step(w_kv, kv_g, m_kv, v_kv, rate_shared, decay_rate)
    first_out, second_out, new_out = adamw_step(
        w_out, out_g.T, m_out, v_out, rate_output, decay_rate
    )
    first_gate_up, second_gate_up, new_gate_up = adamw_step(
        w_gate_up, ffn_g[:2], m_gate_up, v_gate_up, rate_gate_up, decay_rate
    )
    first_down, second_down, new_down = adamw_step(
        w_down, ffn_g[2].T, m_down, v_down, rate_down, decay_rate
    )
    first_gains, second_gains, new_gains = adamw_step(
        norm_gains, gains_g, m_gains, v_gains, rate_gains, 0.0
    )
    return (
        layer_out,
        input_grad,
        first_query,
        second_query,
        new_query,
        first_kv,
        second_kv,
        new_kv,
        first_out,
        second_out,
        new_out,
        first_gate_up,
        second_gate_up,
        new_gate_up,
        first_down,
        second_down,
        new_down,
        first_gains,
        second_gains,
        new_gains,
    )


def solution(mesh):
    n_dp, n_tensor = mesh.shape["dp"], mesh.shape["tensor"]
    fine = Mesh(mesh.devices.reshape(n_dp // 2, 2, n_tensor), ("a", "c", "z"))
    dp, every = ("a", "c"), ("a", "c", "z")
    token = P(every, None)
    query = P(dp, "z")
    shared = P(None, every, None)
    output = P("z", dp)
    gate_up = P(None, dp, "z")
    gains = P(None, every)
    in_specs = (token, token, P(dp), query, shared, output, gate_up, output, gains)
    in_specs += (query, query, shared, shared, output, output, gate_up, gate_up)
    in_specs += (output, output, gains, gains)
    out_specs = (token, token) + (query,) * 3 + (shared,) * 3 + (output,) * 3
    out_specs += (gate_up,) * 3 + (output,) * 3 + (gains,) * 3
    return jax.shard_map(body, mesh=fine, in_specs=in_specs, out_specs=out_specs, check_vma=False)
```

```python
import functools

import jax
import jax.numpy as jnp
from jax import lax
from jax.experimental import pallas as pl
from jax.experimental.pallas import tpu as pltpu
from jax.sharding import Mesh, PartitionSpec as P

KV = 5
HD = 64
LEN = 1024
STEP = 10
RB = 256

beta_one = 0.9
beta_two = 0.95
adam_eps = 1e-08
decay_rate = 0.1
rate_query = 0.06
rate_shared = 0.06
rate_output = 0.8
rate_gate_up = 0.06
rate_down = 0.05
rate_gains = 0.6
norm_eps = 1e-05
neg_fill = -1e30

bf16 = jnp.bfloat16
f32 = jnp.float32
NN = (((1,), (0,)), ((), ()))
NT = (((1,), (1,)), ((), ()))
TN = (((0,), (0,)), ((), ()))
VMEM_LIMIT = 42 * 2**20
WIDE = 2 * KV * HD


def dot(a, b, dims=NN):
    return lax.dot_general(a, b, dims, preferred_element_type=f32)


def rms_scale(matrix):
    return lax.rsqrt(jnp.mean(matrix * matrix, axis=-1, keepdims=True) + norm_eps)


def norm_back(matrix, gain_row, upstream):
    scaling = rms_scale(matrix)
    unit_rows = matrix * scaling
    weighted = upstream * gain_row
    inner_mean = jnp.mean(weighted * unit_rows, axis=-1, keepdims=True)
    return (scaling * (weighted - unit_rows * inner_mean), jnp.sum(upstream * unit_rows, axis=0))


def adamw_step(weight, gradient, moment_one, moment_two, step_rate, decay_coef):
    moment_one = beta_one * moment_one + (1.0 - beta_one) * gradient
    moment_two = beta_two * moment_two + (1.0 - beta_two) * gradient * gradient
    unbiased_one = moment_one / (1.0 - beta_one**STEP)
    unbiased_two = moment_two / (1.0 - beta_two**STEP)
    updated = weight - step_rate * (
        unbiased_one / (jnp.sqrt(unbiased_two) + adam_eps) + decay_coef * weight
    )
    return (moment_one, moment_two, updated)


def columns_to_rows(columns):
    n = columns[0].shape[0]
    wide = jnp.concatenate(columns + [jnp.zeros((n, 128 - len(columns)), f32)], 1)
    return jnp.transpose(wide)[:8]


def params(flops, megabytes, transcendentals=0, weight=2.5):
    return dict(
        compiler_params=pltpu.CompilerParams(vmem_limit_bytes=VMEM_LIMIT),
        cost_estimate=pl.CostEstimate(
            flops=int(flops * weight), bytes_accessed=int(megabytes * weight * 1e6), transcendentals=transcendentals
        ),
    )


def attend_forward_kernel(info, q_ref, before_ref, own_ref, o_ref, lse_ref, *, rows):
    second, prefix = info[0], info[1]
    width = KV * HD

    def run(is_second):
        for block in range(rows // RB):
            base = (rows if is_second else 0) + block * RB
            row_slice = slice(block * RB, (block + 1) * RB)
            if is_second:
                spans = [(before_ref, 0, rows, None)]
                if block:
                    spans.append((own_ref, 0, block * RB, None))
                spans.append((own_ref, block * RB, RB, rows + block * RB))
            else:
                spans = [(own_ref, 0, rows, 0)]
            masks = []
            for _, _, count, masked in spans:
                if masked is None:
                    masks.append(None)
                else:
                    at = lax.broadcasted_iota(jnp.int32, (RB, count), 1) + masked
                    row = lax.broadcasted_iota(jnp.int32, (RB, count), 0) + base
                    masks.append((at <= row) | (at < prefix))
            outs, logs = [], []
            for c in range(KV):
                cols = slice(c * HD, (c + 1) * HD)
                values = slice(width + c * HD, width + (c + 1) * HD)
                query = q_ref[0, row_slice, cols]
                scores = []
                for (ref, start, count, _), mask in zip(spans, masks):
                    part = dot(query, ref[start : start + count, cols], NT)
                    scores.append(part if mask is None else jnp.where(mask, part, neg_fill))
                highest = functools.reduce(
                    jnp.maximum, [jnp.max(s, axis=1, keepdims=True) for s in scores]
                )
                total, mixed = 0.0, 0.0
                for (ref, start, count, _), part in zip(spans, scores):
                    expo = jnp.exp(part - highest)
                    total = total + jnp.sum(expo, axis=1, keepdims=True)
                    mixed = mixed + dot(expo.astype(bf16), ref[start : start + count, values])
                outs.append((mixed / total).astype(bf16))
                logs.append(highest + jnp.log(total))
            o_ref[0, row_slice, :] = jnp.concatenate(outs, 1)
            lse_ref[0, :, row_slice] = columns_to_rows(logs)

    pl.when(second == 0)(lambda: run(False))
    pl.when(second == 1)(lambda: run(True))


def attend_forward(info, queries, before, own):
    groups, rows, width = queries.shape
    block = pl.BlockSpec((1, rows, width), lambda r, _: (r, 0, 0))
    whole = pl.BlockSpec(own.shape, lambda r, _: (0, 0))
    elements = groups * rows * KV * 2 * rows
    return pl.pallas_call(
        functools.partial(attend_forward_kernel, rows=rows),
        grid_spec=pltpu.PrefetchScalarGridSpec(
            num_scalar_prefetch=1,
            grid=(groups,),
            in_specs=[block, whole, whole],
            out_specs=[block, pl.BlockSpec((1, 8, rows), lambda r, _: (r, 0, 0))],
        ),
        out_shape=[
            jax.ShapeDtypeStruct(queries.shape, bf16),
            jax.ShapeDtypeStruct((groups, 8, rows), f32),
        ],
        name="attend_forward",
        **params(elements * 900, 4, elements),
    )(info, queries, before, own)


def attend_backward_kernel(
    info, q_ref, before_ref, own_ref, do_ref, lse_ref, delta_ref, dq_ref, first_ref, last_ref, dk_acc, dv_acc, *, rows
):
    second, prefix = info[0], info[1]
    group = pl.program_id(0)
    width = KV * HD

    @pl.when(group == 0)
    def _():
        dk_acc[...] = jnp.zeros_like(dk_acc)
        dv_acc[...] = jnp.zeros_like(dv_acc)

    def run(is_second):
        for block in range(rows // RB):
            base = (rows if is_second else 0) + block * RB
            row_slice = slice(block * RB, (block + 1) * RB)
            steps = rows // RB
            if is_second:
                spans = [(before_ref, i * RB, i * RB, False) for i in range(steps)]
                spans += [(own_ref, i * RB, rows + i * RB, i == block) for i in range(block + 1)]
            else:
                spans = [(own_ref, i * RB, i * RB, True) for i in range(steps)]
            query_grads = []
            for c in range(KV):
                cols = slice(c * HD, (c + 1) * HD)
                values = slice(width + c * HD, width + (c + 1) * HD)
                query, out_grad = q_ref[0, row_slice, cols], do_ref[0, row_slice, cols]
                log_sum = lse_ref[0, c : c + 1, row_slice]
                delta = delta_ref[0, c : c + 1, row_slice]
                query_grad = jnp.zeros((RB, HD), f32)
                for ref, start, position, masked in spans:
                    key, value = ref[start : start + RB, cols], ref[start : start + RB, values]
                    scores = dot(key, query, NT) - log_sum
                    if masked:
                        at = lax.broadcasted_iota(jnp.int32, (RB, RB), 0) + position
                        row = lax.broadcasted_iota(jnp.int32, (RB, RB), 1) + base
                        scores = jnp.where((at <= row) | (at < prefix), scores, neg_fill)
                    probs = jnp.exp(scores)
                    probs_grad = dot(value, out_grad, NT)
                    score_grad = (probs * (probs_grad - delta)).astype(bf16)
                    at_keys = slice(position, position + RB)
                    dv_acc[c, at_keys, :] += dot(probs.astype(bf16), out_grad)
                    dk_acc[c, at_keys, :] += dot(score_grad, query)
                    query_grad = query_grad + dot(score_grad, key, TN)
                query_grads.append((query_grad * HD**-0.5).astype(bf16))
            dq_ref[0, row_slice, :] = jnp.concatenate(query_grads, 1)

    pl.when(second == 0)(lambda: run(False))
    pl.when(second == 1)(lambda: run(True))

    @pl.when(group == pl.num_programs(0) - 1)
    def _():
        for ref, part in ((first_ref, slice(0, rows)), (last_ref, slice(rows, 2 * rows))):
            ref[...] = jnp.concatenate(
                [acc[c, part, :] for acc in (dk_acc, dv_acc) for c in range(KV)], 1
            )


def attend_backward(info, queries, before, own, out_grad, log_sums, delta):
    groups, rows, width = queries.shape
    block = pl.BlockSpec((1, rows, width), lambda r, _: (r, 0, 0))
    whole = pl.BlockSpec(own.shape, lambda r, _: (0, 0))
    stats = pl.BlockSpec((1, 8, rows), lambda r, _: (r, 0, 0))
    elements = groups * rows * KV * 2 * rows
    return pl.pallas_call(
        functools.partial(attend_backward_kernel, rows=rows),
        grid_spec=pltpu.PrefetchScalarGridSpec(
            num_scalar_prefetch=1,
            grid=(groups,),
            in_specs=[block, whole, whole, block, stats, stats],
            out_specs=[block, whole, whole],
            scratch_shapes=[pltpu.VMEM((KV, 2 * rows, HD), f32)] * 2,
        ),
        out_shape=[jax.ShapeDtypeStruct(queries.shape, bf16)]
        + [jax.ShapeDtypeStruct(own.shape, f32)] * 2,
        name="attend_backward",
        **params(elements * 2500, 8, elements),
    )(info, queries, before, own, out_grad, log_sums, delta)


BLOCKS = 4
SWAPPED = (0, 2, 1, 3)


def block_row(info, j, other):
    return (((info[2] ^ j) * 2) + (info[3] ^ other)) * 160


def pair_of(ref):
    return jnp.concatenate([ref[0], ref[1]], 1)


def put_together(info, refs, w_ref):
    width = KV * HD
    for i, ref in enumerate(refs):
        part, other = i // 2, i % 2
        for j in range(BLOCKS):
            at = block_row(info, SWAPPED[j] if part else j, other) + part * 80
            block = ref[j]
            w_ref[pl.ds(pl.multiple_of(at, 16), 80), :] = jnp.concatenate(
                [block[:80, :width], block[80:, :width]], 1
            )


def shared_kernel(info, tok_ref, ka, kb, va, vb, normed_ref, normed_t_ref, kv_ref, gain_ref, wkv_ref, gains):
    width = KV * HD
    for other, (k_ref, v_ref) in enumerate(((ka, va), (kb, vb))):
        for j in range(BLOCKS):
            at = pl.ds(pl.multiple_of(block_row(info, j, other), 160), 160)
            wkv_ref[at, :width] = k_ref[j][:, :width]
            gains[0, at, :] = k_ref[j][:, 256:].astype(f32)
            at = pl.ds(pl.multiple_of(block_row(info, SWAPPED[j], other), 160), 160)
            wkv_ref[at, width:] = v_ref[j][:, :width]
            gains[1, at, :] = v_ref[j][:, 256:].astype(f32)
    one = jnp.transpose(gains[0])[64:72]
    two = jnp.transpose(gains[1])[64:72]
    gain_ref[...] = jnp.concatenate([one[:1], two[:1], jnp.zeros((6, one.shape[1]), f32)], 0)
    tok = tok_ref[...].astype(f32)
    normed = (tok * rms_scale(tok) * one[:1]).astype(bf16)
    normed_ref[...] = normed
    normed_t_ref[...] = jnp.transpose(normed)
    kv_ref[...] = dot(normed, wkv_ref[...]).astype(bf16)


def project_shared(info, tokens, parts):
    rows, depth = tokens.shape
    width = 2 * KV * HD
    whole = lambda *shape: pl.BlockSpec(shape, lambda i, _: (0,) * len(shape))
    block = pl.BlockSpec((BLOCKS, 160, 384), lambda i, _: (0, 4, 0))
    return pl.pallas_call(
        shared_kernel,
        grid_spec=pltpu.PrefetchScalarGridSpec(
            num_scalar_prefetch=1,
            grid=(1,),
            in_specs=[whole(rows, depth)] + [block] * 4,
            out_specs=[
                whole(rows, depth),
                whole(depth, rows),
                whole(rows, width),
                whole(8, depth),
                whole(depth, width),
            ],
            scratch_shapes=[pltpu.VMEM((2, depth, 128), f32)],
        ),
        out_shape=[
            jax.ShapeDtypeStruct((rows, depth), bf16),
            jax.ShapeDtypeStruct((depth, rows), bf16),
            jax.ShapeDtypeStruct((rows, width), bf16),
            jax.ShapeDtypeStruct((8, depth), f32),
            jax.ShapeDtypeStruct((depth, width), bf16),
        ],
        name="project_shared",
        **params(2 * rows * depth * width, 8),
    )(info, tokens, *parts)


def query_kernel(info, x_ref, a0, b0, a1, b1, q_ref, w_ref):
    put_together(info, (a0, b0, a1, b1), w_ref)
    result = (dot(x_ref[...], w_ref[...]).astype(bf16) * HD**-0.5).astype(bf16)
    q_ref[0] = result[:, : KV * HD]
    q_ref[1] = result[:, KV * HD :]


def project_queries(info, normed, parts):
    rows, depth = normed.shape
    block = pl.BlockSpec((BLOCKS, 160, 384), lambda r, _: (0, r, 0))
    return pl.pallas_call(
        query_kernel,
        grid_spec=pltpu.PrefetchScalarGridSpec(
            num_scalar_prefetch=1,
            grid=(2,),
            in_specs=[pl.BlockSpec((rows, depth), lambda r, _: (0, 0))] + [block] * 4,
            out_specs=[
                pl.BlockSpec((2, rows, WIDE // 2), lambda r, _: (r, 0, 0)),
                pl.BlockSpec((depth, WIDE), lambda r, _: (0, r)),
            ],
        ),
        out_shape=[
            jax.ShapeDtypeStruct((4, rows, WIDE // 2), bf16),
            jax.ShapeDtypeStruct((depth, 2 * WIDE), bf16),
        ],
        name="project_queries",
        **params(4 * rows * depth * WIDE, 10),
    )(info, normed, *parts)


def output_kernel(
    info, att_ref, a0, b0, a1, b1, tok_ref, gain_ref, middle_ref, normed_ref, w_ref, acc
):
    put_together(info, (a0, b0, a1, b1), w_ref)
    part = dot(pair_of(att_ref), w_ref[...], NT)

    @pl.when(pl.program_id(0) == 0)
    def _():
        acc[...] = tok_ref[...].astype(f32) + part

    @pl.when(pl.program_id(0) == 1)
    def _():
        middle = acc[...] + part
        middle_ref[...] = middle
        normed_ref[...] = (middle * rms_scale(middle) * gain_ref[1:2]).astype(bf16)


def project_output(info, attended, parts, tokens, gains):
    rows, depth = tokens.shape
    block = pl.BlockSpec((BLOCKS, 160, 384), lambda r, _: (0, 2 + r, 0))
    whole = lambda *shape: pl.BlockSpec(shape, lambda r, _: (0,) * len(shape))
    return pl.pallas_call(
        output_kernel,
        grid_spec=pltpu.PrefetchScalarGridSpec(
            num_scalar_prefetch=1,
            grid=(2,),
            in_specs=[pl.BlockSpec((2, rows, WIDE // 2), lambda r, _: (r, 0, 0))]
            + [block] * 4
            + [whole(rows, depth), whole(8, depth)],
            out_specs=[
                whole(rows, depth),
                whole(rows, depth),
                pl.BlockSpec((depth, WIDE), lambda r, _: (0, r)),
            ],
            scratch_shapes=[pltpu.VMEM((rows, depth), f32)],
        ),
        out_shape=[
            jax.ShapeDtypeStruct((rows, depth), f32),
            jax.ShapeDtypeStruct((rows, depth), bf16),
            jax.ShapeDtypeStruct((depth, 2 * WIDE), bf16),
        ],
        name="project_output",
        **params(4 * rows * depth * WIDE, 14),
    )(info, attended, *parts, tokens, gains)


def feed_forward_kernel(xa, xb, ca, cb, w_ref, inner_ref, out_a, out_b, back_a, back_b):
    def run(x_ref, c_ref, out_ref, back_ref):
        x, cot = x_ref[...], c_ref[...]
        gate = dot(x, w_ref[0])
        up = dot(x, w_ref[1])
        hidden_grad = dot(cot, w_ref[2])
        sig = jax.nn.sigmoid(gate)
        silu = gate * sig
        hidden = (silu * up).astype(bf16)
        inner_ref[2] = hidden
        gate_grad = (hidden_grad * up * sig * (1.0 + gate * (1.0 - sig))).astype(bf16)
        inner_ref[0] = gate_grad
        up_grad = (hidden_grad * silu).astype(bf16)
        inner_ref[1] = up_grad
        out_ref[...] = dot(hidden, w_ref[2], NT).astype(bf16)
        back_ref[...] = (dot(gate_grad, w_ref[0], NT) + dot(up_grad, w_ref[1], NT)).astype(bf16)

    pl.when(pl.program_id(0) < pl.num_programs(0) // 2)(lambda: run(xa, ca, out_a, back_a))
    pl.when(pl.program_id(0) >= pl.num_programs(0) // 2)(lambda: run(xb, cb, out_b, back_b))


def feed_forward(normed, cots, weights):
    rows, depth = normed[0].shape
    width = weights.shape[2]
    tile = 256
    steps = rows // tile
    first = pl.BlockSpec((tile, depth), lambda i: (jnp.minimum(i, steps - 1), 0))
    last = pl.BlockSpec((tile, depth), lambda i: (jnp.maximum(i - steps, 0), 0))
    inner = pl.BlockSpec((3, tile, width), lambda i: (0, i, 0))
    whole = pl.BlockSpec(weights.shape, lambda i: (0, 0, 0), pipeline_mode=pl.Buffered(1))
    return pl.pallas_call(
        feed_forward_kernel,
        grid=(2 * steps,),
        in_specs=[first, last, first, last, whole],
        out_specs=[inner, first, last, first, last],
        out_shape=[jax.ShapeDtypeStruct((3, 2 * rows, width), bf16)]
        + [jax.ShapeDtypeStruct((rows, depth), bf16)] * 4,
        name="feed_forward",
        **params(24 * rows * depth * width, 24),
    )(*normed, *cots, weights)


def hidden_grad_kernel(x0, x1, x2, x3, c0, c1, c2, c3, near_ref, far_ref, out_ref):
    def run(lefts):
        rows = lefts[0].shape[0]
        total = 0.0
        for left, (right, at) in zip(lefts, ((near_ref, 0), (near_ref, 1), (far_ref, 0), (far_ref, 1))):
            total = total + dot(left[...], right[0, at * rows : (at + 1) * rows, :], TN)
        out_ref[0] = total.astype(bf16)

    pl.when(pl.program_id(0) < 2)(lambda: run((x0, x1, x2, x3)))
    pl.when(pl.program_id(0) == 2)(lambda: run((c0, c1, c2, c3)))


def hidden_grads(normed, cots, near, far):
    rows, depth = normed[0].shape
    width = near.shape[2]
    tile = 640
    last = depth // tile - 1
    left = pl.BlockSpec((rows, tile), lambda m, i: (0, jnp.where(m < 2, i, last)))
    cot = pl.BlockSpec((rows, tile), lambda m, i: (0, jnp.where(m < 2, 0, i)))
    right = pl.BlockSpec((1, 2 * rows, width), lambda m, i: (m, 0, 0))
    return pl.pallas_call(
        hidden_grad_kernel,
        grid=(3, depth // tile),
        in_specs=[left] * 4 + [cot] * 4 + [right] * 2,
        out_specs=pl.BlockSpec((1, tile, width), lambda m, i: (m, i, 0)),
        out_shape=jax.ShapeDtypeStruct((3, depth, width), bf16),
        name="hidden_grads",
        **params(24 * rows * depth * width, 28),
    )(*normed, *cots, near, far)


def middle_kernel(
    middle_ref, cot_ref, gain_ref, near_ref, core_ref, far_ref, w_ref, att_ref,
    grad_ref, low_t_ref, gain_grad_ref, do_ref, delta_ref, low,
):
    @pl.when(pl.program_id(0) == 0)
    def _():
        upstream = near_ref[...].astype(f32) + core_ref[...].astype(f32) + far_ref[...].astype(f32)
        middle = middle_ref[...]
        scaling = rms_scale(middle)
        unit_rows = middle * scaling
        gain_grad = jnp.sum(upstream * unit_rows, axis=0, keepdims=True)
        gain_grad_ref[...] = jnp.broadcast_to(gain_grad, gain_grad_ref.shape)
        weighted = upstream * gain_ref[1:2]
        inner_mean = jnp.mean(weighted * unit_rows, axis=-1, keepdims=True)
        grad = cot_ref[...].astype(f32) + scaling * (weighted - unit_rows * inner_mean)
        grad_ref[...] = grad
        low[...] = grad.astype(bf16)
        low_t_ref[...] = jnp.transpose(low[...])

    grad = dot(low[...], w_ref[...]).astype(bf16)
    do_ref[0] = grad[:, : WIDE // 2]
    do_ref[1] = grad[:, WIDE // 2 :]
    product = grad.astype(f32) * pair_of(att_ref).astype(f32)
    high = product.astype(bf16)
    rest = (product - high.astype(f32)).astype(bf16)
    row = lax.broadcasted_iota(jnp.int32, (16, WIDE), 0)
    head = jnp.where(row < 8, jnp.where(row < KV, row, -1), jnp.where(row < 8 + KV, row - 8 + KV, -1))
    column = lax.broadcasted_iota(jnp.int32, (16, WIDE), 1)
    member = ((column >= head * HD) & (column < (head + 1) * HD)).astype(f32).astype(bf16)
    delta = dot(member, high, NT) + dot(member, rest, NT)
    delta_ref[0] = delta[:8]
    delta_ref[1] = delta[8:]


def middle_backward(middle, cot, gains, near, core, far, w_out, attended):
    rows, depth = middle.shape
    block = pl.BlockSpec((2, rows, WIDE // 2), lambda r: (r, 0, 0))
    whole = lambda *shape: pl.BlockSpec(shape, lambda r: (0,) * len(shape))
    token = whole(rows, depth)
    return pl.pallas_call(
        middle_kernel,
        grid=(2,),
        in_specs=[token, token, whole(8, depth), token, token, token]
        + [pl.BlockSpec((depth, WIDE), lambda r: (0, r)), block],
        out_specs=[
            token,
            whole(depth, rows),
            whole(8, depth),
            block,
            pl.BlockSpec((2, 8, rows), lambda r: (r, 0, 0)),
        ],
        out_shape=[
            jax.ShapeDtypeStruct((rows, depth), f32),
            jax.ShapeDtypeStruct((depth, rows), bf16),
            jax.ShapeDtypeStruct((8, depth), f32),
            jax.ShapeDtypeStruct((4, rows, WIDE // 2), bf16),
            jax.ShapeDtypeStruct((4, 8, rows), f32),
        ],
        scratch_shapes=[pltpu.VMEM((rows, depth), bf16)],
        name="middle_backward",
        **params(4 * rows * depth * WIDE, 20),
    )(middle, cot, gains, near, core, far, w_out, attended)


def input_kernel(
    dq_ref, wq_ref, dkv_ref, wkv_ref, tok_ref, gain_ref, grad_ref, two_ref, out_ref, gain_grad_ref, acc
):
    group = pl.program_id(0)

    @pl.when(group == 0)
    def _():
        acc[...] = dot(dkv_ref[...], wkv_ref[...], NT)

    acc[...] += dot(pair_of(dq_ref), wq_ref[...], NT)

    @pl.when(group == pl.num_programs(0) - 1)
    def _():
        upstream = acc[...]
        tok = tok_ref[...].astype(f32)
        scaling = rms_scale(tok)
        unit_rows = tok * scaling
        one = jnp.sum(upstream * unit_rows, axis=0, keepdims=True)
        gain_grad_ref[...] = jnp.concatenate([one, two_ref[:7]], 0)
        weighted = upstream * gain_ref[0:1]
        inner_mean = jnp.mean(weighted * unit_rows, axis=-1, keepdims=True)
        out_ref[...] = grad_ref[...] + scaling * (weighted - unit_rows * inner_mean)


def input_backward(dq, wq, dkv, wkv, tokens, gains, middle_grad, gain_two):
    rows, depth = tokens.shape
    whole = lambda *shape: pl.BlockSpec(shape, lambda r: (0,) * len(shape))
    token = whole(rows, depth)
    return pl.pallas_call(
        input_kernel,
        grid=(2,),
        in_specs=[
            pl.BlockSpec((2, rows, WIDE // 2), lambda r: (r, 0, 0)),
            pl.BlockSpec((depth, WIDE), lambda r: (0, r)),
            whole(*dkv.shape),
            whole(*wkv.shape),
            token,
            whole(8, depth),
            token,
            whole(8, depth),
        ],
        out_specs=[token, whole(8, depth)],
        out_shape=[
            jax.ShapeDtypeStruct((rows, depth), f32),
            jax.ShapeDtypeStruct((8, depth), f32),
        ],
        scratch_shapes=[pltpu.VMEM((rows, depth), f32)],
        name="input_backward",
        **params(6 * rows * depth * WIDE, 20),
    )(dq, wq, dkv, wkv, tokens, gains, middle_grad, gain_two)


def group_grad_kernel(info, left_a, right_a, left_b, right_b, own_ref, other_ref, whole):
    width = KV * HD

    @pl.when(pl.program_id(1) == 0)
    def _():
        whole[...] = dot(left_a[...], pair_of(right_a)).astype(bf16)

    @pl.when(pl.program_id(1) == 1)
    def _():
        whole[...] = dot(left_b[...], pair_of(right_b)).astype(bf16)

    for other, ref in enumerate((own_ref, other_ref)):
        for j in range(BLOCKS):
            at = pl.multiple_of(block_row(info, j, other), 160)
            block = whole[pl.ds(at, 160), :]
            for low in range(2):
                ref[j, (info[4] & 1) ^ low] = block[:, low * width : (low + 1) * width]


def group_grads(info, left_a, right_a, left_b, right_b):
    groups, rows, width = right_a.shape
    depth = left_a.shape[0]
    left = pl.BlockSpec((depth, rows), lambda r, w, _: (0, 0))
    right = pl.BlockSpec((2, rows, width), lambda r, w, info: (r ^ (info[4] >> 1), 0, 0))
    block = pl.BlockSpec((BLOCKS, 2, 160, width), lambda r, w, _: (0, 2 * r + w, 0, 0))
    return pl.pallas_call(
        group_grad_kernel,
        grid_spec=pltpu.PrefetchScalarGridSpec(
            num_scalar_prefetch=1,
            grid=(2, 2),
            in_specs=[left, right] * 2,
            out_specs=[block] * 2,
            scratch_shapes=[pltpu.VMEM((depth, WIDE), bf16)],
        ),
        out_shape=[jax.ShapeDtypeStruct((BLOCKS, 2 * groups, 160, width), bf16)] * 2,
        name="group_grads",
        **params(8 * rows * depth * WIDE, 12),
    )(info, left_a, right_a, left_b, right_b)


def shared_grad_kernel(info, left_ref, right_ref, gain_ref, own_ref, other_ref, whole):
    wide = jnp.concatenate([gain_ref[...], jnp.zeros((120, gain_ref.shape[1]), f32)], 0)
    width = right_ref.shape[1]
    whole[:, width:] = jnp.transpose(wide).astype(bf16)
    whole[:, :width] = dot(left_ref[...], right_ref[...]).astype(bf16)
    for other, ref in enumerate((own_ref, other_ref)):
        for j in range(BLOCKS):
            at = pl.ds(pl.multiple_of(block_row(info, j, other), 160), 160)
            ref[j] = whole[at, :]


def shared_grads(info, left, right, gain_grads):
    rows, width = right.shape
    depth = left.shape[0]
    whole = lambda *shape: pl.BlockSpec(shape, lambda i, _: (0,) * len(shape))
    return pl.pallas_call(
        shared_grad_kernel,
        grid_spec=pltpu.PrefetchScalarGridSpec(
            num_scalar_prefetch=1,
            grid=(1,),
            in_specs=[whole(depth, rows), whole(rows, width), whole(8, depth)],
            out_specs=[whole(BLOCKS, 160, width + 128)] * 2,
            scratch_shapes=[pltpu.VMEM((depth, width + 128), bf16)],
        ),
        out_shape=[jax.ShapeDtypeStruct((BLOCKS, 160, width + 128), bf16)] * 2,
        name="shared_grads",
        **params(2 * rows * depth * width, 6),
    )(info, left, right, gain_grads)


def swap(value, axis, bit):
    size = lax.axis_size(axis)
    return lax.ppermute(value, axis, [(i, i ^ bit) for i in range(size)])


def core_swap(value):
    return swap(value, "c", 1)


def placed(own, other, bit, axis=0):
    return jnp.concatenate(
        [jnp.where(bit == 0, own, other), jnp.where(bit == 0, other, own)], axis
    )


def gather_line(own, z):
    pair = placed(own, swap(own, "z", 2), z // 2)
    size = own.shape[0]
    near = swap(pair, "z", 1)
    both = [jnp.where(z % 2 == 0, pair, near), jnp.where(z % 2 == 0, near, pair)]
    return jnp.concatenate(
        [part[i * size : (i + 1) * size] for i in range(2) for part in both], 0
    )


def gather_plane(blocks, bit):
    return jnp.concatenate([blocks, swap(blocks, "a", bit)], 0)


def add(one, two, kind=bf16):
    return (one.astype(f32) + two.astype(f32)).astype(kind)


def reduce_core(parts):
    own, other = parts
    return add(own, core_swap(other))


def reduce_plane(blocks, bits):
    if bits[0] == 1:
        blocks = blocks.reshape((2, 2) + blocks.shape[1:])
        blocks = add(blocks[:, 0], swap(blocks[:, 1], "a", 1))
    else:
        blocks = add(blocks[:2], swap(blocks[2:], "a", 2))
    return add(blocks[0], swap(blocks[1], "a", bits[1]))


def pick(stacked, index, axis=0):
    return lax.dynamic_index_in_dim(stacked, index, axis, keepdims=False)


def after(value, *earlier):
    return lax.optimization_barrier((value,) + earlier)[0]


def head_weights(w_query, w_kv, w_out, norm_gains, z, beside):
    w_rows, group_width = w_query.shape
    kv_rows = w_kv.shape[1]
    n_a, n_z = lax.axis_size("a"), lax.axis_size("z")
    pad = lambda m: jnp.pad(m.astype(bf16), ((0, 0), (0, 384 - m.shape[1])))
    shared = [pad(jnp.concatenate([w_kv[i], norm_gains[i][:, None]], 1)) for i in range(2)]
    query, output = pad(w_query), pad(w_out.T)
    if n_a == BLOCKS:
        half = w_rows // 2
        line = gather_line(jnp.concatenate([query, output] + shared, 0)[None], z)
        moved = beside(line)
        packs = []
        for i, bits in enumerate(((1, 2), (2, 1))):
            starts = (i * half, w_rows + i * half, 2 * w_rows + i * kv_rows)
            counts = (half, half, kv_rows)
            own = [line[:, s : s + n].reshape(n_z * n, 384) for s, n in zip(starts, counts)]
            blocks = gather_plane(jnp.concatenate(own, 0)[None], bits[0])
            packs.append(gather_plane(blocks, bits[1]))
        return packs, moved
    every = ("a", "c", "z")

    def groups(own):
        got = lax.all_gather(own, every, axis=0).reshape(2 * n_a, n_z, w_rows, 384)
        return jnp.transpose(got, (1, 0, 2, 3)).reshape(n_z, BLOCKS, 2, 160, 384)

    query, output = groups(query), groups(output)
    result = []
    for i in range(2):
        kv = lax.all_gather(shared[i], every, axis=0).reshape(BLOCKS, 2, 160, 384)
        halves = [
            jnp.transpose(m[:, :, :, i * 80 : (i + 1) * 80], (1, 2, 0, 3, 4)).reshape(
                BLOCKS, 2, n_z * 80, 384
            )
            for m in (query, output)
        ]
        part = jnp.concatenate(halves + [kv], 2)
        if i:
            part = part[jnp.array(SWAPPED)]
        result += [part[:, 0], part[:, 1]]
    return result, beside(query)


def body(
    tokens,
    cotangent,
    prefix_len,
    w_query,
    w_kv,
    w_out,
    w_gate_up,
    w_down,
    norm_gains,
    m_query,
    v_query,
    m_kv,
    v_kv,
    m_out,
    v_out,
    m_gate_up,
    v_gate_up,
    m_down,
    v_down,
    m_gains,
    v_gains,
):
    rows, width = tokens.shape
    a, c, z = lax.axis_index("a"), lax.axis_index("c"), lax.axis_index("z")
    n_a, n_z = lax.axis_size("a"), lax.axis_size("z")
    plane = n_a == BLOCKS
    w_rows, group_width = w_query.shape
    kv_rows = w_kv.shape[1]
    hidden_width = w_gate_up.shape[2]
    second = (z % (LEN // rows)) == 1
    seq_at = z // (LEN // rows)
    at = [a, c, z] if plane else [0, 0, 0]
    info = jnp.stack([second, pick(prefix_len, seq_at)] + at).astype(jnp.int32)

    ffn_own = jnp.concatenate([w_gate_up, w_down.T[None]], 0).astype(bf16)
    cross = [(n_z + zz, zz) for zz in range(n_z)] + [(zz, n_z + (zz ^ 2)) for zz in range(n_z)]
    far_core = [(n_z + zz, n_z + (zz ^ 2)) for zz in range(n_z)]

    def cross_line(line):
        block = after(ffn_own, line)
        return lax.ppermute(block, ("c", "z"), cross), lax.ppermute(block, ("c", "z"), far_core)

    parts, moved = head_weights(w_query, w_kv, w_out, norm_gains, z, cross_line)
    crossed, shifted = moved
    ffn_blocks = jnp.concatenate(
        [jnp.where(c == 0, ffn_own, crossed), jnp.where(c == 0, crossed, shifted)], 1
    )
    if plane:
        ffn_blocks = after(ffn_blocks, *parts)
        parts = parts[0], core_swap(parts[0]), parts[1], core_swap(parts[1])
    ffn_w = lax.all_gather(ffn_blocks, "a", axis=1, tiled=True)

    normed_one, normed_one_t, kv_own, gains, w_shared = project_shared(info, tokens, parts)
    before = lax.ppermute(kv_own, "z", [(i, i + 1) for i in range(0, n_z, 2)])
    queries, w_groups = project_queries(info, normed_one, parts)
    before = after(before, queries)
    cot_core = core_swap(after(cotangent, before))
    cot_pair = swap(after(cotangent, before), "z", 1)
    attended, log_sums = attend_forward(info, queries, before, kv_own)
    cot_pair = after(cot_pair, attended)
    cots = cotangent, cot_core, cot_pair, core_swap(cot_pair)
    middle, normed_two, out_groups = project_output(
        info, attended, parts, after(tokens, cots[3]), gains
    )

    two_core, two_pair = core_swap(normed_two), swap(normed_two, "z", 1)
    inner_near, out_own, out_core, back_own, back_core = feed_forward(
        (normed_two, two_core), cots[:2], ffn_w
    )
    back_core = core_swap(back_core)
    two_pair = after(two_pair, inner_near)
    twos = (normed_two, two_core, two_pair, core_swap(two_pair))
    inner_far, out_far, out_far_core, back_far, back_far_core = feed_forward(
        twos[2:], cots[2:], ffn_w
    )
    back_sum = add(back_far, core_swap(back_far_core))
    back_pair = swap(back_sum, "z", 1)
    ffn_grad = hidden_grads(twos, cots, inner_near, after(inner_far, back_sum, back_core))
    ffn_sum = lax.psum_scatter(
        after(ffn_grad, back_pair), "a", scatter_dimension=1, tiled=True
    )

    middle_grad, middle_low_t, gain_two_grad, attended_grad, delta = middle_backward(
        middle, cotangent, gains, back_own, back_core, after(back_pair, ffn_grad), out_groups, attended
    )
    out_pair = swap(after(add(out_far, core_swap(out_far_core)), attended_grad), "z", 1)
    out_core = core_swap(out_core)
    dq, first_grad, last_grad = attend_backward(
        info, queries, before, kv_own, attended_grad, log_sums, delta
    )
    to_before = first_grad.astype(bf16)
    dq = after(dq, out_core, out_pair, to_before)
    from_after = lax.ppermute(to_before, "z", [(i + 1, i) for i in range(0, n_z, 2)])
    parts = group_grads(info, normed_one_t, dq, middle_low_t, attended)
    if plane:
        parts = parts[0], core_swap(parts[1])
        first = [m[:, :4].reshape((2, 2, 4) + m.shape[2:]) for m in parts]
        last = [m[:, 4:] for m in parts]
        first_send = add(first[0][:, 1], first[1][:, 1])
        last_send = add(last[0][2:], last[1][2:])
        from_after = after(from_after, first_send, last_send, ffn_sum)
        first_recv, last_recv = swap(first_send, "a", 1), swap(last_send, "a", 2)
    dkv = jnp.where(second, last_grad, first_grad + from_after.astype(f32)).astype(bf16)
    input_grad, gain_grads = input_backward(
        dq, w_groups, dkv, w_shared, tokens, gains, middle_grad, gain_two_grad
    )
    shared_parts = shared_grads(info, normed_one_t, dkv, gain_grads)

    ffn_sum = ffn_sum.reshape(3, 2, w_rows, hidden_width)
    ffn_g = []
    for part in ffn_sum:
        crossed_back = lax.ppermute(
            jnp.where(c == 0, part[1], part[0]), ("c", "z"), [(d, s) for s, d in cross]
        )
        shifted_back = lax.ppermute(part[1], ("c", "z"), far_core)
        ffn_g.append(add(crossed_back, jnp.where(c == 0, part[0], shifted_back), f32))
    if plane:
        shared_own, shared_other = shared_parts
        shared_recv = core_swap(shared_other)
        first_recv = after(first_recv, shared_other, ffn_g[0])
        last_recv = after(last_recv, shared_other)
        first = add(add(first[0][:, 0], first[1][:, 0], f32), first_recv)
        last = add(add(last[0][:2], last[1][:2], f32), last_recv)
        first_recv, last_recv = swap(first[1], "a", 2), swap(last[1], "a", 1)
        shared_sum = add(shared_own, after(shared_recv, first, last))
        keys, values = shared_sum[..., :group_width], shared_sum[..., group_width:]
        keys = keys.reshape((2, 2) + keys.shape[1:])
        keys, keys_send, values, values_send = keys[:, 0], keys[:, 1], values[:2], values[2:]
        keys_recv, values_recv = swap(keys_send, "a", 1), swap(values_send, "a", 2)
        first_recv, last_recv = (after(r, keys_send, values_send) for r in (first_recv, last_recv))
        both = jnp.stack([add(first[0], first_recv), add(last[0], last_recv)])
        both = both.reshape((2, 2, 2) + both.shape[2:])
        both_send = after(both[:, :, 1], ffn_g[1])
        both_recv = swap(both_send, "z", 1)
        keys = add(keys, after(keys_recv, both_send))
        values = add(values, after(values_recv, both_send))
        keys_recv, values_recv = swap(keys[1], "a", 2), swap(values[1], "a", 1)
        both = add(both[:, :, 0], both_recv)
        both_recv = swap(both[1], "z", 2)
        shared_sum = jnp.concatenate(
            [
                add(keys[0], after(keys_recv, both)),
                add(values[0], after(values_recv, both)),
            ],
            1,
        )
        quarters = shared_sum.reshape(2, 2, kv_rows, -1)
        kept = add(pick(quarters, z % 2, 1), swap(pick(quarters, 1 - z % 2, 1), "z", 1))
        both = add(both[0], both_recv, f32)
        kept = after(kept, both)
        shared_g = add(pick(kept, z // 2), swap(pick(kept, 1 - z // 2), "z", 2), f32)
        query_g, out_g = both[0], both[1]
    else:

        def whole_sum(blocks):
            blocks = jnp.stack(blocks, 1)
            blocks = jnp.moveaxis(blocks, 2, 0) if blocks.ndim == 5 else blocks[None]
            blocks = blocks.reshape(blocks.shape[0], width, blocks.shape[-1])
            mine = lax.psum_scatter(blocks, ("a", "c"), scatter_dimension=1, tiled=True)
            return mine.astype(f32)

        query_g, out_g = (
            lax.psum_scatter(
                whole_sum(
                    [
                        m.reshape((BLOCKS, 2, 2, 2) + m.shape[2:])[:, :, i].reshape(
                            (BLOCKS, 4) + m.shape[2:]
                        )
                        for m in parts
                    ]
                ),
                "z",
                scatter_dimension=0,
            )
            for i in range(2)
        )
        shared_g = lax.psum_scatter(
            whole_sum(shared_parts)[0], "z", scatter_dimension=0, tiled=True
        )
    gate_up_g = jnp.stack(ffn_g[:2])
    kv_g = jnp.stack([shared_g[:, :group_width], shared_g[:, group_width : 2 * group_width]])
    gains_g = shared_g[:, 2 * group_width : 2 * group_width + 2].T

    layer_out = (middle + add(add(out_own, out_core, f32), after(out_pair, shared_parts[0]), f32)).astype(bf16)

    first_query, second_query, new_query = adamw_step(
        w_query, query_g, m_query, v_query, rate_query, decay_rate
    )
    first_kv, second_kv, new_kv = adamw_step(w_kv, kv_g, m_kv, v_kv, rate_shared, decay_rate)
    first_out, second_out, new_out = adamw_step(
        w_out, out_g.T, m_out, v_out, rate_output, decay_rate
    )
    first_gate_up, second_gate_up, new_gate_up = adamw_step(
        w_gate_up, gate_up_g, m_gate_up, v_gate_up, rate_gate_up, decay_rate
    )
    first_down, second_down, new_down = adamw_step(
        w_down, ffn_g[2].T, m_down, v_down, rate_down, decay_rate
    )
    first_gains, second_gains, new_gains = adamw_step(
        norm_gains, gains_g, m_gains, v_gains, rate_gains, 0.0
    )
    return (
        layer_out,
        input_grad,
        first_query,
        second_query,
        new_query,
        first_kv,
        second_kv,
        new_kv,
        first_out,
        second_out,
        new_out,
        first_gate_up,
        second_gate_up,
        new_gate_up,
        first_down,
        second_down,
        new_down,
        first_gains,
        second_gains,
        new_gains,
    )


def solution(mesh):
    n_dp, n_tensor = mesh.shape["dp"], mesh.shape["tensor"]
    fine = Mesh(mesh.devices.reshape(n_dp // 2, 2, n_tensor), ("a", "c", "z"))
    dp, every = ("a", "c"), ("a", "c", "z")
    token = P(every, None)
    query = P(dp, "z")
    shared = P(None, every, None)
    output = P("z", dp)
    gate_up = P(None, dp, "z")
    gains = P(None, every)
    in_specs = (token, token, P(dp), query, shared, output, gate_up, output, gains)
    in_specs += (query, query, shared, shared, output, output, gate_up, gate_up)
    in_specs += (output, output, gains, gains)
    out_specs = (token, token) + (query,) * 3 + (shared,) * 3 + (output,) * 3
    out_specs += (gate_up,) * 3 + (output,) * 3 + (gains,) * 3
    return jax.shard_map(body, mesh=fine, in_specs=in_specs, out_specs=out_specs, check_vma=False)
```

```python
import functools

import jax
import jax.numpy as jnp
from jax import lax
from jax.experimental import pallas as pl
from jax.experimental.pallas import tpu as pltpu
from jax.sharding import Mesh, PartitionSpec as P

KV = 5
HD = 64
LEN = 1024
STEP = 10
RB = 256

beta_one = 0.9
beta_two = 0.95
adam_eps = 1e-08
decay_rate = 0.1
rate_query = 0.06
rate_shared = 0.06
rate_output = 0.8
rate_gate_up = 0.06
rate_down = 0.05
rate_gains = 0.6
norm_eps = 1e-05
neg_fill = -1e30

bf16 = jnp.bfloat16
f32 = jnp.float32
NN = (((1,), (0,)), ((), ()))
NT = (((1,), (1,)), ((), ()))
TN = (((0,), (0,)), ((), ()))
VMEM_LIMIT = 46 * 2**20
WIDE = 2 * KV * HD


def dot(a, b, dims=NN):
    return lax.dot_general(a, b, dims, preferred_element_type=f32)


def rms_scale(matrix):
    return lax.rsqrt(jnp.mean(matrix * matrix, axis=-1, keepdims=True) + norm_eps)


def norm_back(matrix, gain_row, upstream):
    scaling = rms_scale(matrix)
    unit_rows = matrix * scaling
    weighted = upstream * gain_row
    inner_mean = jnp.mean(weighted * unit_rows, axis=-1, keepdims=True)
    return (scaling * (weighted - unit_rows * inner_mean), jnp.sum(upstream * unit_rows, axis=0))


def adamw_step(weight, gradient, moment_one, moment_two, step_rate, decay_coef):
    moment_one = beta_one * moment_one + (1.0 - beta_one) * gradient
    moment_two = beta_two * moment_two + (1.0 - beta_two) * gradient * gradient
    unbiased_one = moment_one / (1.0 - beta_one**STEP)
    unbiased_two = moment_two / (1.0 - beta_two**STEP)
    updated = weight - step_rate * (
        unbiased_one / (jnp.sqrt(unbiased_two) + adam_eps) + decay_coef * weight
    )
    return (moment_one, moment_two, updated)


def columns_to_rows(columns):
    n = columns[0].shape[0]
    wide = jnp.concatenate(columns + [jnp.zeros((n, 128 - len(columns)), f32)], 1)
    return jnp.transpose(wide)[:8]


def params(flops, megabytes, transcendentals=0, weight=2.5):
    return dict(
        compiler_params=pltpu.CompilerParams(vmem_limit_bytes=VMEM_LIMIT),
        cost_estimate=pl.CostEstimate(
            flops=int(flops * weight), bytes_accessed=int(megabytes * weight * 1e6), transcendentals=transcendentals
        ),
    )


def attend_forward_kernel(info, q_ref, before_ref, own_ref, o_ref, lse_ref, *, rows):
    second, prefix = info[0], info[1]
    width = KV * HD

    def run(is_second):
        for block in range(rows // RB):
            base = (rows if is_second else 0) + block * RB
            row_slice = slice(block * RB, (block + 1) * RB)
            if is_second:
                spans = [(before_ref, 0, rows, None)]
                if block:
                    spans.append((own_ref, 0, block * RB, None))
                spans.append((own_ref, block * RB, RB, rows + block * RB))
            else:
                spans = [(own_ref, 0, rows, 0)]
            masks = []
            for _, _, count, masked in spans:
                if masked is None:
                    masks.append(None)
                else:
                    at = lax.broadcasted_iota(jnp.int32, (RB, count), 1) + masked
                    row = lax.broadcasted_iota(jnp.int32, (RB, count), 0) + base
                    masks.append((at <= row) | (at < prefix))
            outs, logs = [], []
            for c in range(KV):
                cols = slice(c * HD, (c + 1) * HD)
                values = slice(width + c * HD, width + (c + 1) * HD)
                query = q_ref[0, row_slice, cols]
                scores = []
                for (ref, start, count, _), mask in zip(spans, masks):
                    part = dot(query, ref[start : start + count, cols], NT)
                    scores.append(part if mask is None else jnp.where(mask, part, neg_fill))
                highest = functools.reduce(
                    jnp.maximum, [jnp.max(s, axis=1, keepdims=True) for s in scores]
                )
                total, mixed = 0.0, 0.0
                for (ref, start, count, _), part in zip(spans, scores):
                    expo = jnp.exp(part - highest)
                    total = total + jnp.sum(expo, axis=1, keepdims=True)
                    mixed = mixed + dot(expo.astype(bf16), ref[start : start + count, values])
                outs.append((mixed / total).astype(bf16))
                logs.append(highest + jnp.log(total))
            o_ref[0, row_slice, :] = jnp.concatenate(outs, 1)
            lse_ref[0, :, row_slice] = columns_to_rows(logs)

    pl.when(second == 0)(lambda: run(False))
    pl.when(second == 1)(lambda: run(True))


def attend_forward(info, queries, before, own):
    groups, rows, width = queries.shape
    block = pl.BlockSpec((1, rows, width), lambda r, _: (r, 0, 0))
    whole = pl.BlockSpec(own.shape, lambda r, _: (0, 0))
    elements = groups * rows * KV * 2 * rows
    return pl.pallas_call(
        functools.partial(attend_forward_kernel, rows=rows),
        grid_spec=pltpu.PrefetchScalarGridSpec(
            num_scalar_prefetch=1,
            grid=(groups,),
            in_specs=[block, whole, whole],
            out_specs=[block, pl.BlockSpec((1, 8, rows), lambda r, _: (r, 0, 0))],
        ),
        out_shape=[
            jax.ShapeDtypeStruct(queries.shape, bf16),
            jax.ShapeDtypeStruct((groups, 8, rows), f32),
        ],
        name="attend_forward",
        **params(elements * 900, 4, elements),
    )(info, queries, before, own)


def attend_backward_kernel(
    info, q_ref, before_ref, own_ref, do_ref, lse_ref, delta_ref, dq_ref, first_ref, last_ref, dk_acc, dv_acc, *, rows
):
    second, prefix = info[0], info[1]
    group = pl.program_id(0)
    width = KV * HD

    @pl.when(group == 0)
    def _():
        dk_acc[...] = jnp.zeros_like(dk_acc)
        dv_acc[...] = jnp.zeros_like(dv_acc)

    def run(is_second):
        for block in range(rows // RB):
            base = (rows if is_second else 0) + block * RB
            row_slice = slice(block * RB, (block + 1) * RB)
            steps = rows // RB
            if is_second:
                spans = [(before_ref, i * RB, i * RB, False) for i in range(steps)]
                spans += [(own_ref, i * RB, rows + i * RB, i == block) for i in range(block + 1)]
            else:
                spans = [(own_ref, i * RB, i * RB, True) for i in range(steps)]
            query_grads = []
            for c in range(KV):
                cols = slice(c * HD, (c + 1) * HD)
                values = slice(width + c * HD, width + (c + 1) * HD)
                query, out_grad = q_ref[0, row_slice, cols], do_ref[0, row_slice, cols]
                log_sum = lse_ref[0, c : c + 1, row_slice]
                delta = delta_ref[0, c : c + 1, row_slice]
                query_grad = jnp.zeros((RB, HD), f32)
                for ref, start, position, masked in spans:
                    key, value = ref[start : start + RB, cols], ref[start : start + RB, values]
                    scores = dot(key, query, NT) - log_sum
                    if masked:
                        at = lax.broadcasted_iota(jnp.int32, (RB, RB), 0) + position
                        row = lax.broadcasted_iota(jnp.int32, (RB, RB), 1) + base
                        scores = jnp.where((at <= row) | (at < prefix), scores, neg_fill)
                    probs = jnp.exp(scores)
                    probs_grad = dot(value, out_grad, NT)
                    score_grad = (probs * (probs_grad - delta)).astype(bf16)
                    at_keys = slice(position, position + RB)
                    dv_acc[c, at_keys, :] += dot(probs.astype(bf16), out_grad)
                    dk_acc[c, at_keys, :] += dot(score_grad, query)
                    query_grad = query_grad + dot(score_grad, key, TN)
                query_grads.append((query_grad * HD**-0.5).astype(bf16))
            dq_ref[0, row_slice, :] = jnp.concatenate(query_grads, 1)

    pl.when(second == 0)(lambda: run(False))
    pl.when(second == 1)(lambda: run(True))

    @pl.when(group == pl.num_programs(0) - 1)
    def _():
        for ref, part in ((first_ref, slice(0, rows)), (last_ref, slice(rows, 2 * rows))):
            ref[...] = jnp.concatenate(
                [acc[c, part, :] for acc in (dk_acc, dv_acc) for c in range(KV)], 1
            )


def attend_backward(info, queries, before, own, out_grad, log_sums, delta):
    groups, rows, width = queries.shape
    block = pl.BlockSpec((1, rows, width), lambda r, _: (r, 0, 0))
    whole = pl.BlockSpec(own.shape, lambda r, _: (0, 0))
    stats = pl.BlockSpec((1, 8, rows), lambda r, _: (r, 0, 0))
    elements = groups * rows * KV * 2 * rows
    return pl.pallas_call(
        functools.partial(attend_backward_kernel, rows=rows),
        grid_spec=pltpu.PrefetchScalarGridSpec(
            num_scalar_prefetch=1,
            grid=(groups,),
            in_specs=[block, whole, whole, block, stats, stats],
            out_specs=[block, whole, whole],
            scratch_shapes=[pltpu.VMEM((KV, 2 * rows, HD), f32)] * 2,
        ),
        out_shape=[jax.ShapeDtypeStruct(queries.shape, bf16)]
        + [jax.ShapeDtypeStruct(own.shape, f32)] * 2,
        name="attend_backward",
        **params(elements * 2500, 8, elements),
    )(info, queries, before, own, out_grad, log_sums, delta)


BLOCKS = 4
SWAPPED = (0, 2, 1, 3)


def block_row(info, j, other):
    return (((info[2] ^ j) * 2) + (info[3] ^ other)) * 160


def pair_of(ref):
    return jnp.concatenate([ref[0], ref[1]], 1)


def put_together(info, refs, w_ref):
    width = KV * HD
    for i, ref in enumerate(refs):
        part, other = i // 2, i % 2
        for j in range(BLOCKS):
            at = block_row(info, SWAPPED[j] if part else j, other) + part * 80
            block = ref[j]
            w_ref[pl.ds(pl.multiple_of(at, 16), 80), :] = jnp.concatenate(
                [block[:80, :width], block[80:, :width]], 1
            )


def shared_kernel(info, tok_ref, ka, kb, va, vb, normed_ref, normed_t_ref, kv_ref, gain_ref, wkv_ref, gains):
    width = KV * HD
    for other, (k_ref, v_ref) in enumerate(((ka, va), (kb, vb))):
        for j in range(BLOCKS):
            at = pl.ds(pl.multiple_of(block_row(info, j, other), 160), 160)
            wkv_ref[at, :width] = k_ref[j][:, :width]
            gains[0, at, :] = k_ref[j][:, 256:].astype(f32)
            at = pl.ds(pl.multiple_of(block_row(info, SWAPPED[j], other), 160), 160)
            wkv_ref[at, width:] = v_ref[j][:, :width]
            gains[1, at, :] = v_ref[j][:, 256:].astype(f32)
    one = jnp.transpose(gains[0])[64:72]
    two = jnp.transpose(gains[1])[64:72]
    gain_ref[...] = jnp.concatenate([one[:1], two[:1], jnp.zeros((6, one.shape[1]), f32)], 0)
    tok = tok_ref[...].astype(f32)
    normed = (tok * rms_scale(tok) * one[:1]).astype(bf16)
    normed_ref[...] = normed
    normed_t_ref[...] = jnp.transpose(normed)
    kv_ref[...] = dot(normed, wkv_ref[...]).astype(bf16)


def project_shared(info, tokens, parts):
    rows, depth = tokens.shape
    width = 2 * KV * HD
    whole = lambda *shape: pl.BlockSpec(shape, lambda i, _: (0,) * len(shape))
    block = pl.BlockSpec((BLOCKS, 160, 384), lambda i, _: (0, 4, 0))
    return pl.pallas_call(
        shared_kernel,
        grid_spec=pltpu.PrefetchScalarGridSpec(
            num_scalar_prefetch=1,
            grid=(1,),
            in_specs=[whole(rows, depth)] + [block] * 4,
            out_specs=[
                whole(rows, depth),
                whole(depth, rows),
                whole(rows, width),
                whole(8, depth),
                whole(depth, width),
            ],
            scratch_shapes=[pltpu.VMEM((2, depth, 128), f32)],
        ),
        out_shape=[
            jax.ShapeDtypeStruct((rows, depth), bf16),
            jax.ShapeDtypeStruct((depth, rows), bf16),
            jax.ShapeDtypeStruct((rows, width), bf16),
            jax.ShapeDtypeStruct((8, depth), f32),
            jax.ShapeDtypeStruct((depth, width), bf16),
        ],
        name="project_shared",
        **params(2 * rows * depth * width, 8),
    )(info, tokens, *parts)


def query_kernel(info, x_ref, a0, b0, a1, b1, c0, d0, c1, d1, q_ref, w_ref, wo_ref):
    put_together(info, (a0, b0, a1, b1), w_ref)
    put_together(info, (c0, d0, c1, d1), wo_ref)
    result = (dot(x_ref[...], w_ref[...]).astype(bf16) * HD**-0.5).astype(bf16)
    q_ref[0] = result[:, : KV * HD]
    q_ref[1] = result[:, KV * HD :]


def project_queries(info, normed, parts):
    rows, depth = normed.shape
    query = pl.BlockSpec((BLOCKS, 160, 384), lambda r, _: (0, r, 0))
    output = pl.BlockSpec((BLOCKS, 160, 384), lambda r, _: (0, 2 + r, 0))
    weights = pl.BlockSpec((depth, WIDE), lambda r, _: (0, r))
    return pl.pallas_call(
        query_kernel,
        grid_spec=pltpu.PrefetchScalarGridSpec(
            num_scalar_prefetch=1,
            grid=(2,),
            in_specs=[pl.BlockSpec((rows, depth), lambda r, _: (0, 0))] + [query] * 4 + [output] * 4,
            out_specs=[
                pl.BlockSpec((2, rows, WIDE // 2), lambda r, _: (r, 0, 0)),
                weights,
                weights,
            ],
        ),
        out_shape=[jax.ShapeDtypeStruct((4, rows, WIDE // 2), bf16)]
        + [jax.ShapeDtypeStruct((depth, 2 * WIDE), bf16)] * 2,
        name="project_queries",
        **params(4 * rows * depth * WIDE, 14),
    )(info, normed, *parts, *parts)


def output_kernel(att_ref, w_ref, tok_ref, gain_ref, middle_ref, normed_ref, acc):
    part = dot(pair_of(att_ref), w_ref[...], NT)

    @pl.when(pl.program_id(0) == 0)
    def _():
        acc[...] = tok_ref[...].astype(f32) + part

    @pl.when(pl.program_id(0) == 1)
    def _():
        middle = acc[...] + part
        middle_ref[...] = middle
        normed_ref[...] = (middle * rms_scale(middle) * gain_ref[1:2]).astype(bf16)


def project_output(attended, w_out, tokens, gains):
    rows, depth = tokens.shape
    whole = lambda *shape: pl.BlockSpec(shape, lambda r: (0,) * len(shape))
    return pl.pallas_call(
        output_kernel,
        grid=(2,),
        in_specs=[
            pl.BlockSpec((2, rows, WIDE // 2), lambda r: (r, 0, 0)),
            pl.BlockSpec((depth, WIDE), lambda r: (0, r)),
            whole(rows, depth),
            whole(8, depth),
        ],
        out_specs=[whole(rows, depth)] * 2,
        out_shape=[
            jax.ShapeDtypeStruct((rows, depth), f32),
            jax.ShapeDtypeStruct((rows, depth), bf16),
        ],
        scratch_shapes=[pltpu.VMEM((rows, depth), f32)],
        name="project_output",
        **params(4 * rows * depth * WIDE, 12),
    )(attended, w_out, tokens, gains)


def feed_forward_kernel(xa, xb, ca, cb, w_ref, inner_ref, out_a, out_b, back_a, back_b):
    def run(x_ref, c_ref, out_ref, back_ref):
        x, cot = x_ref[...], c_ref[...]
        gate = dot(x, w_ref[0])
        up = dot(x, w_ref[1])
        hidden_grad = dot(cot, w_ref[2])
        sig = jax.nn.sigmoid(gate)
        silu = gate * sig
        hidden = (silu * up).astype(bf16)
        inner_ref[2] = hidden
        gate_grad = (hidden_grad * up * sig * (1.0 + gate * (1.0 - sig))).astype(bf16)
        inner_ref[0] = gate_grad
        up_grad = (hidden_grad * silu).astype(bf16)
        inner_ref[1] = up_grad
        out_ref[...] = dot(hidden, w_ref[2], NT).astype(bf16)
        back_ref[...] = (dot(gate_grad, w_ref[0], NT) + dot(up_grad, w_ref[1], NT)).astype(bf16)

    pl.when(pl.program_id(0) < pl.num_programs(0) // 2)(lambda: run(xa, ca, out_a, back_a))
    pl.when(pl.program_id(0) >= pl.num_programs(0) // 2)(lambda: run(xb, cb, out_b, back_b))


def feed_forward(normed, cots, weights):
    rows, depth = normed[0].shape
    width = weights.shape[2]
    tile = 256
    steps = rows // tile
    first = pl.BlockSpec((tile, depth), lambda i: (jnp.minimum(i, steps - 1), 0))
    last = pl.BlockSpec((tile, depth), lambda i: (jnp.maximum(i - steps, 0), 0))
    inner = pl.BlockSpec((3, tile, width), lambda i: (0, i, 0))
    whole = pl.BlockSpec(weights.shape, lambda i: (0, 0, 0), pipeline_mode=pl.Buffered(1))
    return pl.pallas_call(
        feed_forward_kernel,
        grid=(2 * steps,),
        in_specs=[first, last, first, last, whole],
        out_specs=[inner, first, last, first, last],
        out_shape=[jax.ShapeDtypeStruct((3, 2 * rows, width), bf16)]
        + [jax.ShapeDtypeStruct((rows, depth), bf16)] * 4,
        name="feed_forward",
        **params(24 * rows * depth * width, 24),
    )(*normed, *cots, weights)


def hidden_grad_kernel(x0, x1, x2, x3, c0, c1, c2, c3, near_ref, far_ref, out_ref):
    def run(lefts):
        rows = lefts[0].shape[0]
        total = 0.0
        for left, (right, at) in zip(lefts, ((near_ref, 0), (near_ref, 1), (far_ref, 0), (far_ref, 1))):
            total = total + dot(left[...], right[0, at * rows : (at + 1) * rows, :], TN)
        out_ref[0] = total.astype(bf16)

    pl.when(pl.program_id(0) < 2)(lambda: run((x0, x1, x2, x3)))
    pl.when(pl.program_id(0) == 2)(lambda: run((c0, c1, c2, c3)))


def hidden_grads(normed, cots, near, far):
    rows, depth = normed[0].shape
    width = near.shape[2]
    tile = 640
    last = depth // tile - 1
    left = pl.BlockSpec((rows, tile), lambda m, i: (0, jnp.where(m < 2, i, last)))
    cot = pl.BlockSpec((rows, tile), lambda m, i: (0, jnp.where(m < 2, 0, i)))
    right = pl.BlockSpec((1, 2 * rows, width), lambda m, i: (m, 0, 0))
    return pl.pallas_call(
        hidden_grad_kernel,
        grid=(3, depth // tile),
        in_specs=[left] * 4 + [cot] * 4 + [right] * 2,
        out_specs=pl.BlockSpec((1, tile, width), lambda m, i: (m, i, 0)),
        out_shape=jax.ShapeDtypeStruct((3, depth, width), bf16),
        name="hidden_grads",
        **params(24 * rows * depth * width, 28),
    )(*normed, *cots, near, far)


def middle_kernel(
    middle_ref, cot_ref, gain_ref, near_ref, core_ref, far_ref, w_ref, att_ref,
    grad_ref, low_t_ref, gain_grad_ref, do_ref, delta_ref, low,
):
    @pl.when(pl.program_id(0) == 0)
    def _():
        upstream = near_ref[...].astype(f32) + core_ref[...].astype(f32) + far_ref[...].astype(f32)
        middle = middle_ref[...]
        scaling = rms_scale(middle)
        unit_rows = middle * scaling
        gain_grad = jnp.sum(upstream * unit_rows, axis=0, keepdims=True)
        gain_grad_ref[...] = jnp.broadcast_to(gain_grad, gain_grad_ref.shape)
        weighted = upstream * gain_ref[1:2]
        inner_mean = jnp.mean(weighted * unit_rows, axis=-1, keepdims=True)
        grad = cot_ref[...].astype(f32) + scaling * (weighted - unit_rows * inner_mean)
        grad_ref[...] = grad
        low[...] = grad.astype(bf16)
        low_t_ref[...] = jnp.transpose(low[...])

    grad = dot(low[...], w_ref[...]).astype(bf16)
    do_ref[0] = grad[:, : WIDE // 2]
    do_ref[1] = grad[:, WIDE // 2 :]
    product = grad.astype(f32) * pair_of(att_ref).astype(f32)
    high = product.astype(bf16)
    rest = (product - high.astype(f32)).astype(bf16)
    row = lax.broadcasted_iota(jnp.int32, (16, WIDE), 0)
    head = jnp.where(row < 8, jnp.where(row < KV, row, -1), jnp.where(row < 8 + KV, row - 8 + KV, -1))
    column = lax.broadcasted_iota(jnp.int32, (16, WIDE), 1)
    member = ((column >= head * HD) & (column < (head + 1) * HD)).astype(f32).astype(bf16)
    delta = dot(member, high, NT) + dot(member, rest, NT)
    delta_ref[0] = delta[:8]
    delta_ref[1] = delta[8:]


def middle_backward(middle, cot, gains, near, core, far, w_out, attended):
    rows, depth = middle.shape
    block = pl.BlockSpec((2, rows, WIDE // 2), lambda r: (r, 0, 0))
    whole = lambda *shape: pl.BlockSpec(shape, lambda r: (0,) * len(shape))
    token = whole(rows, depth)
    return pl.pallas_call(
        middle_kernel,
        grid=(2,),
        in_specs=[token, token, whole(8, depth), token, token, token]
        + [pl.BlockSpec((depth, WIDE), lambda r: (0, r)), block],
        out_specs=[
            token,
            whole(depth, rows),
            whole(8, depth),
            block,
            pl.BlockSpec((2, 8, rows), lambda r: (r, 0, 0)),
        ],
        out_shape=[
            jax.ShapeDtypeStruct((rows, depth), f32),
            jax.ShapeDtypeStruct((depth, rows), bf16),
            jax.ShapeDtypeStruct((8, depth), f32),
            jax.ShapeDtypeStruct((4, rows, WIDE // 2), bf16),
            jax.ShapeDtypeStruct((4, 8, rows), f32),
        ],
        scratch_shapes=[pltpu.VMEM((rows, depth), bf16)],
        name="middle_backward",
        **params(4 * rows * depth * WIDE, 20),
    )(middle, cot, gains, near, core, far, w_out, attended)


def input_kernel(
    dq_ref, wq_ref, dkv_ref, wkv_ref, tok_ref, gain_ref, grad_ref, two_ref, out_ref, gain_grad_ref, acc
):
    group = pl.program_id(0)

    @pl.when(group == 0)
    def _():
        acc[...] = dot(dkv_ref[...], wkv_ref[...], NT)

    acc[...] += dot(pair_of(dq_ref), wq_ref[...], NT)

    @pl.when(group == pl.num_programs(0) - 1)
    def _():
        upstream = acc[...]
        tok = tok_ref[...].astype(f32)
        scaling = rms_scale(tok)
        unit_rows = tok * scaling
        one = jnp.sum(upstream * unit_rows, axis=0, keepdims=True)
        gain_grad_ref[...] = jnp.concatenate([one, two_ref[:7]], 0)
        weighted = upstream * gain_ref[0:1]
        inner_mean = jnp.mean(weighted * unit_rows, axis=-1, keepdims=True)
        out_ref[...] = grad_ref[...] + scaling * (weighted - unit_rows * inner_mean)


def input_backward(dq, wq, dkv, wkv, tokens, gains, middle_grad, gain_two):
    rows, depth = tokens.shape
    whole = lambda *shape: pl.BlockSpec(shape, lambda r: (0,) * len(shape))
    token = whole(rows, depth)
    return pl.pallas_call(
        input_kernel,
        grid=(2,),
        in_specs=[
            pl.BlockSpec((2, rows, WIDE // 2), lambda r: (r, 0, 0)),
            pl.BlockSpec((depth, WIDE), lambda r: (0, r)),
            whole(*dkv.shape),
            whole(*wkv.shape),
            token,
            whole(8, depth),
            token,
            whole(8, depth),
        ],
        out_specs=[token, whole(8, depth)],
        out_shape=[
            jax.ShapeDtypeStruct((rows, depth), f32),
            jax.ShapeDtypeStruct((8, depth), f32),
        ],
        scratch_shapes=[pltpu.VMEM((rows, depth), f32)],
        name="input_backward",
        **params(6 * rows * depth * WIDE, 20),
    )(dq, wq, dkv, wkv, tokens, gains, middle_grad, gain_two)


def group_grad_kernel(info, left_a, right_a, left_b, right_b, own_ref, other_ref, whole):
    @pl.when(pl.program_id(1) == 0)
    def _():
        whole[...] = dot(left_a[...], pair_of(right_a)).astype(bf16)

    @pl.when(pl.program_id(1) == 1)
    def _():
        whole[...] = dot(left_b[...], pair_of(right_b)).astype(bf16)

    for other, ref in enumerate((own_ref, other_ref)):
        for j in range(BLOCKS):
            ref[j, 0] = whole[pl.ds(pl.multiple_of(block_row(info, j, other), 160), 160), :]


def group_grads(info, left_a, right_a, left_b, right_b):
    groups, rows, width = right_a.shape
    depth = left_a.shape[0]
    left = pl.BlockSpec((depth, rows), lambda r, w, _: (0, 0))
    right = pl.BlockSpec((2, rows, width), lambda r, w, info: (r ^ (info[4] >> 1), 0, 0))
    block = pl.BlockSpec((BLOCKS, 1, 160, WIDE), lambda r, w, _: (0, 2 * r + w, 0, 0))
    return pl.pallas_call(
        group_grad_kernel,
        grid_spec=pltpu.PrefetchScalarGridSpec(
            num_scalar_prefetch=1,
            grid=(2, 2),
            in_specs=[left, right] * 2,
            out_specs=[block] * 2,
            scratch_shapes=[pltpu.VMEM((depth, WIDE), bf16)],
        ),
        out_shape=[jax.ShapeDtypeStruct((BLOCKS, groups, 160, WIDE), bf16)] * 2,
        name="group_grads",
        **params(8 * rows * depth * WIDE, 12),
    )(info, left_a, right_a, left_b, right_b)


def shared_grad_kernel(info, left_ref, right_ref, gain_ref, own_ref, other_ref, whole):
    wide = jnp.concatenate([gain_ref[...], jnp.zeros((120, gain_ref.shape[1]), f32)], 0)
    width = right_ref.shape[1]
    whole[:, width:] = jnp.transpose(wide).astype(bf16)
    whole[:, :width] = dot(left_ref[...], right_ref[...]).astype(bf16)
    for other, ref in enumerate((own_ref, other_ref)):
        for j in range(BLOCKS):
            at = pl.ds(pl.multiple_of(block_row(info, j, other), 160), 160)
            ref[j] = whole[at, :]


def shared_grads(info, left, right, gain_grads):
    rows, width = right.shape
    depth = left.shape[0]
    whole = lambda *shape: pl.BlockSpec(shape, lambda i, _: (0,) * len(shape))
    return pl.pallas_call(
        shared_grad_kernel,
        grid_spec=pltpu.PrefetchScalarGridSpec(
            num_scalar_prefetch=1,
            grid=(1,),
            in_specs=[whole(depth, rows), whole(rows, width), whole(8, depth)],
            out_specs=[whole(BLOCKS, 160, width + 128)] * 2,
            scratch_shapes=[pltpu.VMEM((depth, width + 128), bf16)],
        ),
        out_shape=[jax.ShapeDtypeStruct((BLOCKS, 160, width + 128), bf16)] * 2,
        name="shared_grads",
        **params(2 * rows * depth * width, 6),
    )(info, left, right, gain_grads)


def swap(value, axis, bit):
    size = lax.axis_size(axis)
    return lax.ppermute(value, axis, [(i, i ^ bit) for i in range(size)])


def core_swap(value):
    return swap(value, "c", 1)


def placed(own, other, bit, axis=0):
    return jnp.concatenate(
        [jnp.where(bit == 0, own, other), jnp.where(bit == 0, other, own)], axis
    )


def gather_line(own, z):
    pair = placed(own, swap(own, "z", 2), z // 2)
    size = own.shape[0]
    near = swap(pair, "z", 1)
    both = [jnp.where(z % 2 == 0, pair, near), jnp.where(z % 2 == 0, near, pair)]
    return jnp.concatenate(
        [part[i * size : (i + 1) * size] for i in range(2) for part in both], 0
    )


def gather_plane(blocks, bit):
    return jnp.concatenate([blocks, swap(blocks, "a", bit)], 0)


def add(one, two, kind=bf16):
    return (one.astype(f32) + two.astype(f32)).astype(kind)


def reduce_core(parts):
    own, other = parts
    return add(own, core_swap(other))


def reduce_plane(blocks, bits):
    if bits[0] == 1:
        blocks = blocks.reshape((2, 2) + blocks.shape[1:])
        blocks = add(blocks[:, 0], swap(blocks[:, 1], "a", 1))
    else:
        blocks = add(blocks[:2], swap(blocks[2:], "a", 2))
    return add(blocks[0], swap(blocks[1], "a", bits[1]))


def pick(stacked, index, axis=0):
    return lax.dynamic_index_in_dim(stacked, index, axis, keepdims=False)


def after(value, *earlier):
    return lax.optimization_barrier((value,) + earlier)[0]


def head_weights(w_query, w_kv, w_out, norm_gains, z, beside):
    w_rows, group_width = w_query.shape
    kv_rows = w_kv.shape[1]
    n_a, n_z = lax.axis_size("a"), lax.axis_size("z")
    pad = lambda m: jnp.pad(m.astype(bf16), ((0, 0), (0, 384 - m.shape[1])))
    shared = [pad(jnp.concatenate([w_kv[i], norm_gains[i][:, None]], 1)) for i in range(2)]
    query, output = pad(w_query), pad(w_out.T)
    if n_a == BLOCKS:
        half = w_rows // 2
        line = gather_line(jnp.concatenate([query, output] + shared, 0)[None], z)
        moved = beside(line)
        packs = []
        for i, bits in enumerate(((1, 2), (2, 1))):
            starts = (i * half, w_rows + i * half, 2 * w_rows + i * kv_rows)
            counts = (half, half, kv_rows)
            own = [line[:, s : s + n].reshape(n_z * n, 384) for s, n in zip(starts, counts)]
            blocks = gather_plane(jnp.concatenate(own, 0)[None], bits[0])
            packs.append((blocks, swap(blocks, "a", bits[1])))
        return packs, moved
    every = ("a", "c", "z")

    def groups(own):
        got = lax.all_gather(own, every, axis=0).reshape(2 * n_a, n_z, w_rows, 384)
        return jnp.transpose(got, (1, 0, 2, 3)).reshape(n_z, BLOCKS, 2, 160, 384)

    query, output = groups(query), groups(output)
    result = []
    for i in range(2):
        kv = lax.all_gather(shared[i], every, axis=0).reshape(BLOCKS, 2, 160, 384)
        halves = [
            jnp.transpose(m[:, :, :, i * 80 : (i + 1) * 80], (1, 2, 0, 3, 4)).reshape(
                BLOCKS, 2, n_z * 80, 384
            )
            for m in (query, output)
        ]
        part = jnp.concatenate(halves + [kv], 2)
        if i:
            part = part[jnp.array(SWAPPED)]
        result += [part[:, 0], part[:, 1]]
    return result, beside(query)


def body(
    tokens,
    cotangent,
    prefix_len,
    w_query,
    w_kv,
    w_out,
    w_gate_up,
    w_down,
    norm_gains,
    m_query,
    v_query,
    m_kv,
    v_kv,
    m_out,
    v_out,
    m_gate_up,
    v_gate_up,
    m_down,
    v_down,
    m_gains,
    v_gains,
):
    rows, width = tokens.shape
    a, c, z = lax.axis_index("a"), lax.axis_index("c"), lax.axis_index("z")
    n_a, n_z = lax.axis_size("a"), lax.axis_size("z")
    plane = n_a == BLOCKS
    w_rows, group_width = w_query.shape
    kv_rows = w_kv.shape[1]
    hidden_width = w_gate_up.shape[2]
    second = (z % (LEN // rows)) == 1
    seq_at = z // (LEN // rows)
    at = [a, c, z] if plane else [0, 0, 0]
    info = jnp.stack([second, pick(prefix_len, seq_at)] + at).astype(jnp.int32)

    ffn_own = jnp.concatenate([w_gate_up, w_down.T[None]], 0).astype(bf16)
    cross = [(n_z + zz, zz) for zz in range(n_z)] + [(zz, n_z + (zz ^ 2)) for zz in range(n_z)]
    far_core = [(n_z + zz, n_z + (zz ^ 2)) for zz in range(n_z)]

    def cross_line(line):
        block = after(ffn_own, line)
        return lax.ppermute(block, ("c", "z"), cross), lax.ppermute(block, ("c", "z"), far_core)

    parts, moved = head_weights(w_query, w_kv, w_out, norm_gains, z, cross_line)
    crossed, shifted = moved
    ffn_blocks = jnp.concatenate(
        [jnp.where(c == 0, ffn_own, crossed), jnp.where(c == 0, crossed, shifted)], 1
    )
    if plane:
        ffn_blocks = after(ffn_blocks, *(received for _, received in parts))
        first, last = (jnp.concatenate(pair, 0) for pair in parts)
        parts = first, core_swap(first), last, core_swap(last)
    ffn_w = lax.all_gather(ffn_blocks, "a", axis=1, tiled=True)

    normed_one, normed_one_t, kv_own, gains, w_shared = project_shared(info, tokens, parts)
    before = lax.ppermute(kv_own, "z", [(i, i + 1) for i in range(0, n_z, 2)])
    queries, w_groups, out_groups = project_queries(info, normed_one, parts)
    before = after(before, queries)
    cot_core = core_swap(after(cotangent, before))
    cot_pair = swap(after(cotangent, before), "z", 1)
    attended, log_sums = attend_forward(info, queries, before, kv_own)
    cot_pair = after(cot_pair, attended)
    cots = cotangent, cot_core, cot_pair, core_swap(cot_pair)
    middle, normed_two = project_output(attended, out_groups, after(tokens, cots[3]), gains)

    two_core, two_pair = core_swap(normed_two), swap(normed_two, "z", 1)
    inner_near, out_own, out_core, back_own, back_core = feed_forward(
        (normed_two, two_core), cots[:2], ffn_w
    )
    back_core = core_swap(back_core)
    two_pair = after(two_pair, inner_near)
    twos = (normed_two, two_core, two_pair, core_swap(two_pair))
    inner_far, out_far, out_far_core, back_far, back_far_core = feed_forward(
        twos[2:], cots[2:], ffn_w
    )
    back_sum = add(back_far, core_swap(back_far_core))
    back_pair = swap(back_sum, "z", 1)
    ffn_grad = hidden_grads(twos, cots, inner_near, after(inner_far, back_sum, back_core))
    ffn_sum = lax.psum_scatter(
        after(ffn_grad, back_pair), "a", scatter_dimension=1, tiled=True
    )

    middle_grad, middle_low_t, gain_two_grad, attended_grad, delta = middle_backward(
        middle, cotangent, gains, back_own, back_core, after(back_pair, ffn_grad), out_groups, attended
    )
    out_pair = swap(after(add(out_far, core_swap(out_far_core)), attended_grad), "z", 1)
    out_core = core_swap(out_core)
    dq, first_grad, last_grad = attend_backward(
        info, queries, before, kv_own, attended_grad, log_sums, delta
    )
    to_before = first_grad.astype(bf16)
    dq = after(dq, out_core, out_pair, to_before)
    from_after = lax.ppermute(to_before, "z", [(i + 1, i) for i in range(0, n_z, 2)])
    parts = group_grads(info, normed_one_t, dq, middle_low_t, attended)
    if plane:
        parts = parts[0], core_swap(parts[1])
        first = [m[:, :2].reshape((2, 2, 2) + m.shape[2:]) for m in parts]
        last = [m[:, 2:] for m in parts]
        first_send = add(first[0][:, 1], first[1][:, 1])
        last_send = add(last[0][2:], last[1][2:])
        from_after = after(from_after, first_send, last_send, ffn_sum)
        first_recv, last_recv = swap(first_send, "a", 1), swap(last_send, "a", 2)
    dkv = jnp.where(second, last_grad, first_grad + from_after.astype(f32)).astype(bf16)
    input_grad, gain_grads = input_backward(
        dq, w_groups, dkv, w_shared, tokens, gains, middle_grad, gain_two_grad
    )
    ffn_sum = ffn_sum.reshape(3, 2, w_rows, hidden_width)
    crossed = [
        lax.ppermute(jnp.where(c == 0, m[1], m[0]), ("c", "z"), [(d, s) for s, d in cross])
        for m in ffn_sum
    ]
    shifted = [lax.ppermute(m[1], ("c", "z"), far_core) for m in ffn_sum]
    shared_parts = shared_grads(info, normed_one_t, dkv, after(gain_grads, crossed[0]))

    if plane:
        shared_own, shared_other = shared_parts
        shared_recv = core_swap(shared_other)
        first_recv = after(first_recv, shared_other, shifted[0], crossed[1])
        last_recv = after(last_recv, shared_other)
        first = add(add(first[0][:, 0], first[1][:, 0], f32), first_recv)
        last = add(add(last[0][:2], last[1][:2], f32), last_recv)
        first_recv, last_recv = swap(first[1], "a", 2), swap(last[1], "a", 1)
        shared_sum = add(shared_own, after(shared_recv, first, last))
        keys, values = shared_sum[..., :group_width], shared_sum[..., group_width:]
        keys = keys.reshape((2, 2) + keys.shape[1:])
        keys, keys_send, values, values_send = keys[:, 0], keys[:, 1], values[:2], values[2:]
        keys_recv, values_recv = swap(keys_send, "a", 1), swap(values_send, "a", 2)
        first_recv, last_recv = (
            after(r, keys_send, values_send, shifted[1], crossed[2]) for r in (first_recv, last_recv)
        )
        both = jnp.stack([add(first[0], first_recv), add(last[0], last_recv)])
        halves = both[..., :group_width], both[..., group_width:]
        both_send = after(jnp.where(z % 2 == 0, halves[1], halves[0]), shifted[2])
        both = jnp.where(z % 2 == 0, halves[0], halves[1])
        both_recv = swap(both_send, "z", 1)
        keys = add(keys, after(keys_recv, both_send))
        values = add(values, after(values_recv, both_send))
        keys_recv, values_recv = swap(keys[1], "a", 2), swap(values[1], "a", 1)
        both = add(both, both_recv)
        both_recv = swap(both[1], "z", 2)
        shared_sum = jnp.concatenate(
            [
                add(keys[0], after(keys_recv, both)),
                add(values[0], after(values_recv, both)),
            ],
            1,
        )
        quarters = shared_sum.reshape(2, 2, kv_rows, -1)
        kept = add(pick(quarters, z % 2, 1), swap(pick(quarters, 1 - z % 2, 1), "z", 1))
        both = add(both[0], both_recv, f32)
        kept = after(kept, both)
        shared_g = add(pick(kept, z // 2), swap(pick(kept, 1 - z // 2), "z", 2), f32)
        query_g, out_g = both[0], both[1]
    else:

        def whole_sum(blocks):
            blocks = jnp.stack(blocks, 1)
            blocks = jnp.moveaxis(blocks, 2, 0) if blocks.ndim == 5 else blocks[None]
            blocks = blocks.reshape(blocks.shape[0], width, blocks.shape[-1])
            mine = lax.psum_scatter(blocks, ("a", "c"), scatter_dimension=1, tiled=True)
            return mine.astype(f32)

        query_g, out_g = (
            lax.psum_scatter(
                whole_sum(
                    [
                        jnp.stack(
                            [
                                m[:, 2 * r + i, :, k * group_width : (k + 1) * group_width]
                                for r in range(2)
                                for k in range(2)
                            ],
                            1,
                        )
                        for m in parts
                    ]
                ),
                "z",
                scatter_dimension=0,
            )
            for i in range(2)
        )
        shared_g = lax.psum_scatter(
            whole_sum(shared_parts)[0], "z", scatter_dimension=0, tiled=True
        )
    ffn_g = [
        add(got, jnp.where(c == 0, m[0], moved), f32)
        for m, got, moved in zip(ffn_sum, crossed, shifted)
    ]
    gate_up_g = jnp.stack(ffn_g[:2])
    kv_g = jnp.stack([shared_g[:, :group_width], shared_g[:, group_width : 2 * group_width]])
    gains_g = shared_g[:, 2 * group_width : 2 * group_width + 2].T

    layer_out = (middle + add(add(out_own, out_core, f32), after(out_pair, shared_parts[0]), f32)).astype(bf16)

    first_query, second_query, new_query = adamw_step(
        w_query, query_g, m_query, v_query, rate_query, decay_rate
    )
    first_kv, second_kv, new_kv = adamw_step(w_kv, kv_g, m_kv, v_kv, rate_shared, decay_rate)
    first_out, second_out, new_out = adamw_step(
        w_out, out_g.T, m_out, v_out, rate_output, decay_rate
    )
    first_gate_up, second_gate_up, new_gate_up = adamw_step(
        w_gate_up, gate_up_g, m_gate_up, v_gate_up, rate_gate_up, decay_rate
    )
    first_down, second_down, new_down = adamw_step(
        w_down, ffn_g[2].T, m_down, v_down, rate_down, decay_rate
    )
    first_gains, second_gains, new_gains = adamw_step(
        norm_gains, gains_g, m_gains, v_gains, rate_gains, 0.0
    )
    return (
        layer_out,
        input_grad,
        first_query,
        second_query,
        new_query,
        first_kv,
        second_kv,
        new_kv,
        first_out,
        second_out,
        new_out,
        first_gate_up,
        second_gate_up,
        new_gate_up,
        first_down,
        second_down,
        new_down,
        first_gains,
        second_gains,
        new_gains,
    )


def solution(mesh):
    n_dp, n_tensor = mesh.shape["dp"], mesh.shape["tensor"]
    fine = Mesh(mesh.devices.reshape(n_dp // 2, 2, n_tensor), ("a", "c", "z"))
    dp, every = ("a", "c"), ("a", "c", "z")
    token = P(every, None)
    query = P(dp, "z")
    shared = P(None, every, None)
    output = P("z", dp)
    gate_up = P(None, dp, "z")
    gains = P(None, every)
    in_specs = (token, token, P(dp), query, shared, output, gate_up, output, gains)
    in_specs += (query, query, shared, shared, output, output, gate_up, gate_up)
    in_specs += (output, output, gains, gains)
    out_specs = (token, token) + (query,) * 3 + (shared,) * 3 + (output,) * 3
    out_specs += (gate_up,) * 3 + (output,) * 3 + (gains,) * 3
    return jax.shard_map(body, mesh=fine, in_specs=in_specs, out_specs=out_specs, check_vma=False)
```

```python
import functools

import jax
import jax.numpy as jnp
from jax import lax
from jax.experimental import pallas as pl
from jax.experimental.pallas import tpu as pltpu
from jax.sharding import Mesh, PartitionSpec as P

KV = 5
HD = 64
LEN = 1024
STEP = 10
RB = 256

beta_one = 0.9
beta_two = 0.95
adam_eps = 1e-08
decay_rate = 0.1
rate_query = 0.06
rate_shared = 0.06
rate_output = 0.8
rate_gate_up = 0.06
rate_down = 0.05
rate_gains = 0.6
norm_eps = 1e-05
neg_fill = -1e30

bf16 = jnp.bfloat16
f32 = jnp.float32
NN = (((1,), (0,)), ((), ()))
NT = (((1,), (1,)), ((), ()))
TN = (((0,), (0,)), ((), ()))
VMEM_LIMIT = 46 * 2**20
WIDE = 2 * KV * HD


def dot(a, b, dims=NN):
    return lax.dot_general(a, b, dims, preferred_element_type=f32)


def rms_scale(matrix):
    return lax.rsqrt(jnp.mean(matrix * matrix, axis=-1, keepdims=True) + norm_eps)


def norm_back(matrix, gain_row, upstream):
    scaling = rms_scale(matrix)
    unit_rows = matrix * scaling
    weighted = upstream * gain_row
    inner_mean = jnp.mean(weighted * unit_rows, axis=-1, keepdims=True)
    return (scaling * (weighted - unit_rows * inner_mean), jnp.sum(upstream * unit_rows, axis=0))


def adamw_step(weight, gradient, moment_one, moment_two, step_rate, decay_coef):
    moment_one = beta_one * moment_one + (1.0 - beta_one) * gradient
    moment_two = beta_two * moment_two + (1.0 - beta_two) * gradient * gradient
    unbiased_one = moment_one / (1.0 - beta_one**STEP)
    unbiased_two = moment_two / (1.0 - beta_two**STEP)
    updated = weight - step_rate * (
        unbiased_one / (jnp.sqrt(unbiased_two) + adam_eps) + decay_coef * weight
    )
    return (moment_one, moment_two, updated)


def columns_to_rows(columns):
    n = columns[0].shape[0]
    wide = jnp.concatenate(columns + [jnp.zeros((n, 128 - len(columns)), f32)], 1)
    return jnp.transpose(wide)[:8]


def params(flops, megabytes, transcendentals=0, weight=2.5):
    return dict(
        compiler_params=pltpu.CompilerParams(vmem_limit_bytes=VMEM_LIMIT),
        cost_estimate=pl.CostEstimate(
            flops=int(flops * weight), bytes_accessed=int(megabytes * weight * 1e6), transcendentals=transcendentals
        ),
    )


def attend_forward_kernel(info, q_ref, before_ref, own_ref, o_ref, lse_ref, *, rows):
    second, prefix = info[0], info[1]
    width = KV * HD

    def run(is_second):
        for block in range(rows // RB):
            base = (rows if is_second else 0) + block * RB
            row_slice = slice(block * RB, (block + 1) * RB)
            if is_second:
                spans = [(before_ref, 0, rows, None)]
                if block:
                    spans.append((own_ref, 0, block * RB, None))
                spans.append((own_ref, block * RB, RB, rows + block * RB))
            else:
                spans = [(own_ref, 0, rows, 0)]
            masks = []
            for _, _, count, masked in spans:
                if masked is None:
                    masks.append(None)
                else:
                    at = lax.broadcasted_iota(jnp.int32, (RB, count), 1) + masked
                    row = lax.broadcasted_iota(jnp.int32, (RB, count), 0) + base
                    masks.append((at <= row) | (at < prefix))
            outs, logs = [], []
            for c in range(KV):
                cols = slice(c * HD, (c + 1) * HD)
                values = slice(width + c * HD, width + (c + 1) * HD)
                query = q_ref[0, row_slice, cols]
                scores = []
                for (ref, start, count, _), mask in zip(spans, masks):
                    part = dot(query, ref[start : start + count, cols], NT)
                    scores.append(part if mask is None else jnp.where(mask, part, neg_fill))
                highest = functools.reduce(
                    jnp.maximum, [jnp.max(s, axis=1, keepdims=True) for s in scores]
                )
                total, mixed = 0.0, 0.0
                for (ref, start, count, _), part in zip(spans, scores):
                    expo = jnp.exp(part - highest)
                    total = total + jnp.sum(expo, axis=1, keepdims=True)
                    mixed = mixed + dot(expo.astype(bf16), ref[start : start + count, values])
                outs.append((mixed / total).astype(bf16))
                logs.append(highest + jnp.log(total))
            o_ref[0, row_slice, :] = jnp.concatenate(outs, 1)
            lse_ref[0, :, row_slice] = columns_to_rows(logs)

    pl.when(second == 0)(lambda: run(False))
    pl.when(second == 1)(lambda: run(True))


def attend_forward(info, queries, before, own):
    groups, rows, width = queries.shape
    block = pl.BlockSpec((1, rows, width), lambda r, _: (r, 0, 0))
    whole = pl.BlockSpec(own.shape, lambda r, _: (0, 0))
    elements = groups * rows * KV * 2 * rows
    return pl.pallas_call(
        functools.partial(attend_forward_kernel, rows=rows),
        grid_spec=pltpu.PrefetchScalarGridSpec(
            num_scalar_prefetch=1,
            grid=(groups,),
            in_specs=[block, whole, whole],
            out_specs=[block, pl.BlockSpec((1, 8, rows), lambda r, _: (r, 0, 0))],
        ),
        out_shape=[
            jax.ShapeDtypeStruct(queries.shape, bf16),
            jax.ShapeDtypeStruct((groups, 8, rows), f32),
        ],
        name="attend_forward",
        **params(elements * 900, 4, elements),
    )(info, queries, before, own)


def attend_backward_kernel(
    info, q_ref, before_ref, own_ref, do_ref, lse_ref, delta_ref, dq_ref, first_ref, last_ref, dk_acc, dv_acc, *, rows
):
    second, prefix = info[0], info[1]
    group = pl.program_id(0)
    width = KV * HD

    @pl.when(group == 0)
    def _():
        dk_acc[...] = jnp.zeros_like(dk_acc)
        dv_acc[...] = jnp.zeros_like(dv_acc)

    def run(is_second):
        for block in range(rows // RB):
            base = (rows if is_second else 0) + block * RB
            row_slice = slice(block * RB, (block + 1) * RB)
            steps = rows // RB
            if is_second:
                spans = [(before_ref, i * RB, i * RB, False) for i in range(steps)]
                spans += [(own_ref, i * RB, rows + i * RB, i == block) for i in range(block + 1)]
            else:
                spans = [(own_ref, i * RB, i * RB, True) for i in range(steps)]
            query_grads = []
            for c in range(KV):
                cols = slice(c * HD, (c + 1) * HD)
                values = slice(width + c * HD, width + (c + 1) * HD)
                query, out_grad = q_ref[0, row_slice, cols], do_ref[0, row_slice, cols]
                log_sum = lse_ref[0, c : c + 1, row_slice]
                delta = delta_ref[0, c : c + 1, row_slice]
                query_grad = jnp.zeros((RB, HD), f32)
                for ref, start, position, masked in spans:
                    key, value = ref[start : start + RB, cols], ref[start : start + RB, values]
                    scores = dot(key, query, NT) - log_sum
                    if masked:
                        at = lax.broadcasted_iota(jnp.int32, (RB, RB), 0) + position
                        row = lax.broadcasted_iota(jnp.int32, (RB, RB), 1) + base
                        scores = jnp.where((at <= row) | (at < prefix), scores, neg_fill)
                    probs = jnp.exp(scores)
                    probs_grad = dot(value, out_grad, NT)
                    score_grad = (probs * (probs_grad - delta)).astype(bf16)
                    at_keys = slice(position, position + RB)
                    dv_acc[c, at_keys, :] += dot(probs.astype(bf16), out_grad)
                    dk_acc[c, at_keys, :] += dot(score_grad, query)
                    query_grad = query_grad + dot(score_grad, key, TN)
                query_grads.append((query_grad * HD**-0.5).astype(bf16))
            dq_ref[0, row_slice, :] = jnp.concatenate(query_grads, 1)

    pl.when(second == 0)(lambda: run(False))
    pl.when(second == 1)(lambda: run(True))

    @pl.when(group == pl.num_programs(0) - 1)
    def _():
        for ref, part in ((first_ref, slice(0, rows)), (last_ref, slice(rows, 2 * rows))):
            ref[...] = jnp.concatenate(
                [acc[c, part, :] for acc in (dk_acc, dv_acc) for c in range(KV)], 1
            )


def attend_backward(info, queries, before, own, out_grad, log_sums, delta):
    groups, rows, width = queries.shape
    block = pl.BlockSpec((1, rows, width), lambda r, _: (r, 0, 0))
    whole = pl.BlockSpec(own.shape, lambda r, _: (0, 0))
    stats = pl.BlockSpec((1, 8, rows), lambda r, _: (r, 0, 0))
    elements = groups * rows * KV * 2 * rows
    return pl.pallas_call(
        functools.partial(attend_backward_kernel, rows=rows),
        grid_spec=pltpu.PrefetchScalarGridSpec(
            num_scalar_prefetch=1,
            grid=(groups,),
            in_specs=[block, whole, whole, block, stats, stats],
            out_specs=[block, whole, whole],
            scratch_shapes=[pltpu.VMEM((KV, 2 * rows, HD), f32)] * 2,
        ),
        out_shape=[jax.ShapeDtypeStruct(queries.shape, bf16)]
        + [jax.ShapeDtypeStruct(own.shape, f32)] * 2,
        name="attend_backward",
        **params(elements * 2500, 8, elements),
    )(info, queries, before, own, out_grad, log_sums, delta)


BLOCKS = 4
SWAPPED = (0, 2, 1, 3)


def block_row(info, j, other):
    return (((info[2] ^ j) * 2) + (info[3] ^ other)) * 160


def pair_of(ref):
    return jnp.concatenate([ref[0], ref[1]], 1)


def put_together(info, refs, w_ref):
    width = KV * HD
    for i, ref in enumerate(refs):
        part, other = i // 2, i % 2
        for j in range(BLOCKS):
            at = block_row(info, SWAPPED[j] if part else j, other) + part * 80
            block = ref[j]
            w_ref[pl.ds(pl.multiple_of(at, 16), 80), :] = jnp.concatenate(
                [block[:80, :width], block[80:, :width]], 1
            )


def shared_kernel(info, tok_ref, ka, kb, va, vb, normed_ref, normed_t_ref, kv_ref, gain_ref, wkv_ref, gains):
    width = KV * HD
    for other, (k_ref, v_ref) in enumerate(((ka, va), (kb, vb))):
        for j in range(BLOCKS):
            at = pl.ds(pl.multiple_of(block_row(info, j, other), 160), 160)
            wkv_ref[at, :width] = k_ref[j][:, :width]
            gains[0, at, :] = k_ref[j][:, 256:].astype(f32)
            at = pl.ds(pl.multiple_of(block_row(info, SWAPPED[j], other), 160), 160)
            wkv_ref[at, width:] = v_ref[j][:, :width]
            gains[1, at, :] = v_ref[j][:, 256:].astype(f32)
    one = jnp.transpose(gains[0])[64:72]
    two = jnp.transpose(gains[1])[64:72]
    gain_ref[...] = jnp.concatenate([one[:1], two[:1], jnp.zeros((6, one.shape[1]), f32)], 0)
    tok = tok_ref[...].astype(f32)
    normed = (tok * rms_scale(tok) * one[:1]).astype(bf16)
    normed_ref[...] = normed
    normed_t_ref[...] = jnp.transpose(normed)
    kv_ref[...] = dot(normed, wkv_ref[...]).astype(bf16)


def project_shared(info, tokens, parts):
    rows, depth = tokens.shape
    width = 2 * KV * HD
    whole = lambda *shape: pl.BlockSpec(shape, lambda i, _: (0,) * len(shape))
    block = pl.BlockSpec((BLOCKS, 160, 384), lambda i, _: (0, 4, 0))
    return pl.pallas_call(
        shared_kernel,
        grid_spec=pltpu.PrefetchScalarGridSpec(
            num_scalar_prefetch=1,
            grid=(1,),
            in_specs=[whole(rows, depth)] + [block] * 4,
            out_specs=[
                whole(rows, depth),
                whole(depth, rows),
                whole(rows, width),
                whole(8, depth),
                whole(depth, width),
            ],
            scratch_shapes=[pltpu.VMEM((2, depth, 128), f32)],
        ),
        out_shape=[
            jax.ShapeDtypeStruct((rows, depth), bf16),
            jax.ShapeDtypeStruct((depth, rows), bf16),
            jax.ShapeDtypeStruct((rows, width), bf16),
            jax.ShapeDtypeStruct((8, depth), f32),
            jax.ShapeDtypeStruct((depth, width), bf16),
        ],
        name="project_shared",
        **params(2 * rows * depth * width, 8),
    )(info, tokens, *parts)


def query_kernel(info, x_ref, a0, b0, a1, b1, c0, d0, c1, d1, q_ref, w_ref, wo_ref):
    put_together(info, (a0, b0, a1, b1), w_ref)
    put_together(info, (c0, d0, c1, d1), wo_ref)
    result = (dot(x_ref[...], w_ref[...]).astype(bf16) * HD**-0.5).astype(bf16)
    q_ref[0] = result[:, : KV * HD]
    q_ref[1] = result[:, KV * HD :]


def project_queries(info, normed, parts):
    rows, depth = normed.shape
    query = pl.BlockSpec((BLOCKS, 160, 384), lambda r, _: (0, r, 0))
    output = pl.BlockSpec((BLOCKS, 160, 384), lambda r, _: (0, 2 + r, 0))
    weights = pl.BlockSpec((depth, WIDE), lambda r, _: (0, r))
    return pl.pallas_call(
        query_kernel,
        grid_spec=pltpu.PrefetchScalarGridSpec(
            num_scalar_prefetch=1,
            grid=(2,),
            in_specs=[pl.BlockSpec((rows, depth), lambda r, _: (0, 0))] + [query] * 4 + [output] * 4,
            out_specs=[
                pl.BlockSpec((2, rows, WIDE // 2), lambda r, _: (r, 0, 0)),
                weights,
                weights,
            ],
        ),
        out_shape=[jax.ShapeDtypeStruct((4, rows, WIDE // 2), bf16)]
        + [jax.ShapeDtypeStruct((depth, 2 * WIDE), bf16)] * 2,
        name="project_queries",
        **params(4 * rows * depth * WIDE, 14),
    )(info, normed, *parts, *parts)


def output_kernel(att_ref, w_ref, tok_ref, gain_ref, middle_ref, normed_ref, acc):
    part = dot(pair_of(att_ref), w_ref[...], NT)

    @pl.when(pl.program_id(0) == 0)
    def _():
        acc[...] = tok_ref[...].astype(f32) + part

    @pl.when(pl.program_id(0) == 1)
    def _():
        middle = acc[...] + part
        middle_ref[...] = middle
        normed_ref[...] = (middle * rms_scale(middle) * gain_ref[1:2]).astype(bf16)


def project_output(attended, w_out, tokens, gains):
    rows, depth = tokens.shape
    whole = lambda *shape: pl.BlockSpec(shape, lambda r: (0,) * len(shape))
    return pl.pallas_call(
        output_kernel,
        grid=(2,),
        in_specs=[
            pl.BlockSpec((2, rows, WIDE // 2), lambda r: (r, 0, 0)),
            pl.BlockSpec((depth, WIDE), lambda r: (0, r)),
            whole(rows, depth),
            whole(8, depth),
        ],
        out_specs=[whole(rows, depth)] * 2,
        out_shape=[
            jax.ShapeDtypeStruct((rows, depth), f32),
            jax.ShapeDtypeStruct((rows, depth), bf16),
        ],
        scratch_shapes=[pltpu.VMEM((rows, depth), f32)],
        name="project_output",
        **params(4 * rows * depth * WIDE, 12),
    )(attended, w_out, tokens, gains)


def feed_forward_kernel(xa, xb, ca, cb, w_ref, inner_ref, out_a, out_b, back_a, back_b):
    def run(x_ref, c_ref, out_ref, back_ref):
        x, cot = x_ref[...], c_ref[...]
        gate = dot(x, w_ref[0])
        up = dot(x, w_ref[1])
        hidden_grad = dot(cot, w_ref[2])
        sig = jax.nn.sigmoid(gate)
        silu = gate * sig
        hidden = (silu * up).astype(bf16)
        inner_ref[2] = hidden
        gate_grad = (hidden_grad * up * sig * (1.0 + gate * (1.0 - sig))).astype(bf16)
        inner_ref[0] = gate_grad
        up_grad = (hidden_grad * silu).astype(bf16)
        inner_ref[1] = up_grad
        out_ref[...] = dot(hidden, w_ref[2], NT).astype(bf16)
        back_ref[...] = (dot(gate_grad, w_ref[0], NT) + dot(up_grad, w_ref[1], NT)).astype(bf16)

    pl.when(pl.program_id(0) < pl.num_programs(0) // 2)(lambda: run(xa, ca, out_a, back_a))
    pl.when(pl.program_id(0) >= pl.num_programs(0) // 2)(lambda: run(xb, cb, out_b, back_b))


def feed_forward(normed, cots, weights):
    rows, depth = normed[0].shape
    width = weights.shape[2]
    tile = 256
    steps = rows // tile
    first = pl.BlockSpec((tile, depth), lambda i: (jnp.minimum(i, steps - 1), 0))
    last = pl.BlockSpec((tile, depth), lambda i: (jnp.maximum(i - steps, 0), 0))
    inner = pl.BlockSpec((3, tile, width), lambda i: (0, i, 0))
    whole = pl.BlockSpec(weights.shape, lambda i: (0, 0, 0), pipeline_mode=pl.Buffered(1))
    return pl.pallas_call(
        feed_forward_kernel,
        grid=(2 * steps,),
        in_specs=[first, last, first, last, whole],
        out_specs=[inner, first, last, first, last],
        out_shape=[jax.ShapeDtypeStruct((3, 2 * rows, width), bf16)]
        + [jax.ShapeDtypeStruct((rows, depth), bf16)] * 4,
        name="feed_forward",
        **params(24 * rows * depth * width, 24),
    )(*normed, *cots, weights)


def hidden_grad_kernel(x0, x1, x2, x3, c0, c1, c2, c3, near_ref, far_ref, out_ref):
    def run(lefts):
        rows = lefts[0].shape[0]
        total = 0.0
        for left, (right, at) in zip(lefts, ((near_ref, 0), (near_ref, 1), (far_ref, 0), (far_ref, 1))):
            total = total + dot(left[...], right[0, at * rows : (at + 1) * rows, :], TN)
        out_ref[0] = total.astype(bf16)

    pl.when(pl.program_id(0) < 2)(lambda: run((x0, x1, x2, x3)))
    pl.when(pl.program_id(0) == 2)(lambda: run((c0, c1, c2, c3)))


def hidden_grads(normed, cots, near, far):
    rows, depth = normed[0].shape
    width = near.shape[2]
    tile = 640
    last = depth // tile - 1
    left = pl.BlockSpec((rows, tile), lambda m, i: (0, jnp.where(m < 2, i, last)))
    cot = pl.BlockSpec((rows, tile), lambda m, i: (0, jnp.where(m < 2, 0, i)))
    right = pl.BlockSpec((1, 2 * rows, width), lambda m, i: (m, 0, 0))
    return pl.pallas_call(
        hidden_grad_kernel,
        grid=(3, depth // tile),
        in_specs=[left] * 4 + [cot] * 4 + [right] * 2,
        out_specs=pl.BlockSpec((1, tile, width), lambda m, i: (m, i, 0)),
        out_shape=jax.ShapeDtypeStruct((3, depth, width), bf16),
        name="hidden_grads",
        **params(24 * rows * depth * width, 28),
    )(*normed, *cots, near, far)


def middle_kernel(
    middle_ref, cot_ref, gain_ref, near_ref, core_ref, far_ref, w_ref, att_ref,
    grad_ref, low_t_ref, gain_grad_ref, do_ref, delta_ref, low,
):
    @pl.when(pl.program_id(0) == 0)
    def _():
        upstream = near_ref[...].astype(f32) + core_ref[...].astype(f32) + far_ref[...].astype(f32)
        middle = middle_ref[...]
        scaling = rms_scale(middle)
        unit_rows = middle * scaling
        gain_grad = jnp.sum(upstream * unit_rows, axis=0, keepdims=True)
        gain_grad_ref[...] = jnp.broadcast_to(gain_grad, gain_grad_ref.shape)
        weighted = upstream * gain_ref[1:2]
        inner_mean = jnp.mean(weighted * unit_rows, axis=-1, keepdims=True)
        grad = cot_ref[...].astype(f32) + scaling * (weighted - unit_rows * inner_mean)
        grad_ref[...] = grad
        low[...] = grad.astype(bf16)
        low_t_ref[...] = jnp.transpose(low[...])

    grad = dot(low[...], w_ref[...]).astype(bf16)
    do_ref[0] = grad[:, : WIDE // 2]
    do_ref[1] = grad[:, WIDE // 2 :]
    product = grad.astype(f32) * pair_of(att_ref).astype(f32)
    high = product.astype(bf16)
    rest = (product - high.astype(f32)).astype(bf16)
    row = lax.broadcasted_iota(jnp.int32, (16, WIDE), 0)
    head = jnp.where(row < 8, jnp.where(row < KV, row, -1), jnp.where(row < 8 + KV, row - 8 + KV, -1))
    column = lax.broadcasted_iota(jnp.int32, (16, WIDE), 1)
    member = ((column >= head * HD) & (column < (head + 1) * HD)).astype(f32).astype(bf16)
    delta = dot(member, high, NT) + dot(member, rest, NT)
    delta_ref[0] = delta[:8]
    delta_ref[1] = delta[8:]


def middle_backward(middle, cot, gains, near, core, far, w_out, attended):
    rows, depth = middle.shape
    block = pl.BlockSpec((2, rows, WIDE // 2), lambda r: (r, 0, 0))
    whole = lambda *shape: pl.BlockSpec(shape, lambda r: (0,) * len(shape))
    token = whole(rows, depth)
    return pl.pallas_call(
        middle_kernel,
        grid=(2,),
        in_specs=[token, token, whole(8, depth), token, token, token]
        + [pl.BlockSpec((depth, WIDE), lambda r: (0, r)), block],
        out_specs=[
            token,
            whole(depth, rows),
            whole(8, depth),
            block,
            pl.BlockSpec((2, 8, rows), lambda r: (r, 0, 0)),
        ],
        out_shape=[
            jax.ShapeDtypeStruct((rows, depth), f32),
            jax.ShapeDtypeStruct((depth, rows), bf16),
            jax.ShapeDtypeStruct((8, depth), f32),
            jax.ShapeDtypeStruct((4, rows, WIDE // 2), bf16),
            jax.ShapeDtypeStruct((4, 8, rows), f32),
        ],
        scratch_shapes=[pltpu.VMEM((rows, depth), bf16)],
        name="middle_backward",
        **params(4 * rows * depth * WIDE, 20),
    )(middle, cot, gains, near, core, far, w_out, attended)


def input_kernel(
    dq_ref, wq_ref, dkv_ref, wkv_ref, tok_ref, gain_ref, grad_ref, two_ref, out_ref, gain_grad_ref, acc
):
    group = pl.program_id(0)

    @pl.when(group == 0)
    def _():
        acc[...] = dot(dkv_ref[...], wkv_ref[...], NT)

    acc[...] += dot(pair_of(dq_ref), wq_ref[...], NT)

    @pl.when(group == pl.num_programs(0) - 1)
    def _():
        upstream = acc[...]
        tok = tok_ref[...].astype(f32)
        scaling = rms_scale(tok)
        unit_rows = tok * scaling
        one = jnp.sum(upstream * unit_rows, axis=0, keepdims=True)
        gain_grad_ref[...] = jnp.concatenate([one, two_ref[:7]], 0)
        weighted = upstream * gain_ref[0:1]
        inner_mean = jnp.mean(weighted * unit_rows, axis=-1, keepdims=True)
        out_ref[...] = grad_ref[...] + scaling * (weighted - unit_rows * inner_mean)


def input_backward(dq, wq, dkv, wkv, tokens, gains, middle_grad, gain_two):
    rows, depth = tokens.shape
    whole = lambda *shape: pl.BlockSpec(shape, lambda r: (0,) * len(shape))
    token = whole(rows, depth)
    return pl.pallas_call(
        input_kernel,
        grid=(2,),
        in_specs=[
            pl.BlockSpec((2, rows, WIDE // 2), lambda r: (r, 0, 0)),
            pl.BlockSpec((depth, WIDE), lambda r: (0, r)),
            whole(*dkv.shape),
            whole(*wkv.shape),
            token,
            whole(8, depth),
            token,
            whole(8, depth),
        ],
        out_specs=[token, whole(8, depth)],
        out_shape=[
            jax.ShapeDtypeStruct((rows, depth), f32),
            jax.ShapeDtypeStruct((8, depth), f32),
        ],
        scratch_shapes=[pltpu.VMEM((rows, depth), f32)],
        name="input_backward",
        **params(6 * rows * depth * WIDE, 20),
    )(dq, wq, dkv, wkv, tokens, gains, middle_grad, gain_two)


def group_grad_kernel(info, left_a, right_a, left_b, right_b, own_ref, other_ref, whole):
    @pl.when(pl.program_id(1) == 0)
    def _():
        whole[...] = dot(left_a[...], pair_of(right_a)).astype(bf16)

    @pl.when(pl.program_id(1) == 1)
    def _():
        whole[...] = dot(left_b[...], pair_of(right_b)).astype(bf16)

    for other, ref in enumerate((own_ref, other_ref)):
        for j in range(BLOCKS):
            ref[j, 0] = whole[pl.ds(pl.multiple_of(block_row(info, j, other), 160), 160), :]


def group_grads(info, left_a, right_a, left_b, right_b):
    groups, rows, width = right_a.shape
    depth = left_a.shape[0]
    left = pl.BlockSpec((depth, rows), lambda r, w, _: (0, 0))
    right = pl.BlockSpec((2, rows, width), lambda r, w, info: (r ^ (info[4] >> 1), 0, 0))
    block = pl.BlockSpec((BLOCKS, 1, 160, WIDE), lambda r, w, _: (0, 2 * r + w, 0, 0))
    return pl.pallas_call(
        group_grad_kernel,
        grid_spec=pltpu.PrefetchScalarGridSpec(
            num_scalar_prefetch=1,
            grid=(2, 2),
            in_specs=[left, right] * 2,
            out_specs=[block] * 2,
            scratch_shapes=[pltpu.VMEM((depth, WIDE), bf16)],
        ),
        out_shape=[jax.ShapeDtypeStruct((BLOCKS, groups, 160, WIDE), bf16)] * 2,
        name="group_grads",
        **params(8 * rows * depth * WIDE, 12),
    )(info, left_a, right_a, left_b, right_b)


def shared_grad_kernel(info, left_ref, right_ref, gain_ref, own_ref, other_ref, whole):
    wide = jnp.concatenate([gain_ref[...], jnp.zeros((120, gain_ref.shape[1]), f32)], 0)
    width = right_ref.shape[1]
    whole[:, width:] = jnp.transpose(wide).astype(bf16)
    whole[:, :width] = dot(left_ref[...], right_ref[...]).astype(bf16)
    for other, ref in enumerate((own_ref, other_ref)):
        for j in range(BLOCKS):
            at = pl.ds(pl.multiple_of(block_row(info, j, other), 160), 160)
            ref[j] = whole[at, :]


def shared_grads(info, left, right, gain_grads):
    rows, width = right.shape
    depth = left.shape[0]
    whole = lambda *shape: pl.BlockSpec(shape, lambda i, _: (0,) * len(shape))
    return pl.pallas_call(
        shared_grad_kernel,
        grid_spec=pltpu.PrefetchScalarGridSpec(
            num_scalar_prefetch=1,
            grid=(1,),
            in_specs=[whole(depth, rows), whole(rows, width), whole(8, depth)],
            out_specs=[whole(BLOCKS, 160, width + 128)] * 2,
            scratch_shapes=[pltpu.VMEM((depth, width + 128), bf16)],
        ),
        out_shape=[jax.ShapeDtypeStruct((BLOCKS, 160, width + 128), bf16)] * 2,
        name="shared_grads",
        **params(2 * rows * depth * width, 6),
    )(info, left, right, gain_grads)


def swap(value, axis, bit):
    size = lax.axis_size(axis)
    return lax.ppermute(value, axis, [(i, i ^ bit) for i in range(size)])


def core_swap(value):
    return swap(value, "c", 1)


def placed(own, other, bit, axis=0):
    return jnp.concatenate(
        [jnp.where(bit == 0, own, other), jnp.where(bit == 0, other, own)], axis
    )


def gather_line(own, z):
    pair = placed(own, swap(own, "z", 2), z // 2)
    size = own.shape[0]
    near = swap(pair, "z", 1)
    both = [jnp.where(z % 2 == 0, pair, near), jnp.where(z % 2 == 0, near, pair)]
    return jnp.concatenate(
        [part[i * size : (i + 1) * size] for i in range(2) for part in both], 0
    )


def gather_plane(blocks, bit):
    return jnp.concatenate([blocks, swap(blocks, "a", bit)], 0)


def add(one, two, kind=bf16):
    return (one.astype(f32) + two.astype(f32)).astype(kind)


def reduce_core(parts):
    own, other = parts
    return add(own, core_swap(other))


def reduce_plane(blocks, bits):
    if bits[0] == 1:
        blocks = blocks.reshape((2, 2) + blocks.shape[1:])
        blocks = add(blocks[:, 0], swap(blocks[:, 1], "a", 1))
    else:
        blocks = add(blocks[:2], swap(blocks[2:], "a", 2))
    return add(blocks[0], swap(blocks[1], "a", bits[1]))


def pick(stacked, index, axis=0):
    return lax.dynamic_index_in_dim(stacked, index, axis, keepdims=False)


def after(value, *earlier):
    return lax.optimization_barrier((value,) + earlier)[0]


def head_weights(w_query, w_kv, w_out, norm_gains, z, beside):
    w_rows, group_width = w_query.shape
    kv_rows = w_kv.shape[1]
    n_a, n_z = lax.axis_size("a"), lax.axis_size("z")
    pad = lambda m: jnp.pad(m.astype(bf16), ((0, 0), (0, 384 - m.shape[1])))
    shared = [pad(jnp.concatenate([w_kv[i], norm_gains[i][:, None]], 1)) for i in range(2)]
    query, output = pad(w_query), pad(w_out.T)
    if n_a == BLOCKS:
        half = w_rows // 2
        line = gather_line(jnp.concatenate([query, output] + shared, 0)[None], z)
        moved = beside(line)
        packs = []
        for i, bits in enumerate(((1, 2), (2, 1))):
            starts = (i * half, w_rows + i * half, 2 * w_rows + i * kv_rows)
            counts = (half, half, kv_rows)
            own = [line[:, s : s + n].reshape(n_z * n, 384) for s, n in zip(starts, counts)]
            blocks = gather_plane(jnp.concatenate(own, 0)[None], bits[0])
            packs.append((blocks, swap(blocks, "a", bits[1])))
        return packs, moved
    every = ("a", "c", "z")

    def groups(own):
        got = lax.all_gather(own, every, axis=0).reshape(2 * n_a, n_z, w_rows, 384)
        return jnp.transpose(got, (1, 0, 2, 3)).reshape(n_z, BLOCKS, 2, 160, 384)

    query, output = groups(query), groups(output)
    result = []
    for i in range(2):
        kv = lax.all_gather(shared[i], every, axis=0).reshape(BLOCKS, 2, 160, 384)
        halves = [
            jnp.transpose(m[:, :, :, i * 80 : (i + 1) * 80], (1, 2, 0, 3, 4)).reshape(
                BLOCKS, 2, n_z * 80, 384
            )
            for m in (query, output)
        ]
        part = jnp.concatenate(halves + [kv], 2)
        if i:
            part = part[jnp.array(SWAPPED)]
        result += [part[:, 0], part[:, 1]]
    return result, beside(query)


def body(
    tokens,
    cotangent,
    prefix_len,
    w_query,
    w_kv,
    w_out,
    w_gate_up,
    w_down,
    norm_gains,
    m_query,
    v_query,
    m_kv,
    v_kv,
    m_out,
    v_out,
    m_gate_up,
    v_gate_up,
    m_down,
    v_down,
    m_gains,
    v_gains,
):
    rows, width = tokens.shape
    a, c, z = lax.axis_index("a"), lax.axis_index("c"), lax.axis_index("z")
    n_a, n_z = lax.axis_size("a"), lax.axis_size("z")
    plane = n_a == BLOCKS
    w_rows, group_width = w_query.shape
    kv_rows = w_kv.shape[1]
    hidden_width = w_gate_up.shape[2]
    second = (z % (LEN // rows)) == 1
    seq_at = z // (LEN // rows)
    at = [a, c, z] if plane else [0, 0, 0]
    info = jnp.stack([second, pick(prefix_len, seq_at)] + at).astype(jnp.int32)

    ffn_own = jnp.concatenate([w_gate_up, w_down.T[None]], 0).astype(bf16)
    cross = [(n_z + zz, zz) for zz in range(n_z)] + [(zz, n_z + (zz ^ 2)) for zz in range(n_z)]
    far_core = [(n_z + zz, n_z + (zz ^ 2)) for zz in range(n_z)]

    def cross_line(line):
        block = after(ffn_own, line)
        return lax.ppermute(block, ("c", "z"), cross), lax.ppermute(block, ("c", "z"), far_core)

    parts, moved = head_weights(w_query, w_kv, w_out, norm_gains, z, cross_line)
    crossed, shifted = moved
    ffn_blocks = jnp.concatenate(
        [jnp.where(c == 0, ffn_own, crossed), jnp.where(c == 0, crossed, shifted)], 1
    )
    if plane:
        ffn_blocks = after(ffn_blocks, *(received for _, received in parts))
        first, last = (jnp.concatenate(pair, 0) for pair in parts)
        parts = first, core_swap(first), last, core_swap(last)
    ffn_w = lax.all_gather(ffn_blocks, "a", axis=1, tiled=True)

    normed_one, normed_one_t, kv_own, gains, w_shared = project_shared(info, tokens, parts)
    before = lax.ppermute(kv_own, "z", [(i, i + 1) for i in range(0, n_z, 2)])
    queries, w_groups, out_groups = project_queries(info, normed_one, parts)
    before = after(before, queries)
    cot_core = core_swap(after(cotangent, before))
    cot_pair = swap(after(cotangent, crossed, shifted), "z", 1)
    attended, log_sums = attend_forward(info, queries, before, kv_own)
    cot_pair = after(cot_pair, attended)
    cots = cotangent, cot_core, cot_pair, core_swap(cot_pair)
    middle, normed_two = project_output(attended, out_groups, after(tokens, cots[3]), gains)

    two_core, two_pair = core_swap(normed_two), swap(normed_two, "z", 1)
    inner_near, out_own, out_core, back_own, back_core = feed_forward(
        (normed_two, two_core), cots[:2], ffn_w
    )
    back_core = core_swap(back_core)
    two_pair = after(two_pair, inner_near)
    twos = (normed_two, two_core, two_pair, core_swap(two_pair))
    inner_far, out_far, out_far_core, back_far, back_far_core = feed_forward(
        twos[2:], cots[2:], ffn_w
    )
    back_sum = add(back_far, core_swap(back_far_core))
    back_pair = swap(back_sum, "z", 1)
    ffn_grad = hidden_grads(twos, cots, inner_near, after(inner_far, back_sum, back_core))
    out_sum = add(out_far, core_swap(out_far_core))
    ffn_sum = lax.psum_scatter(
        after(ffn_grad, back_pair, out_sum), "a", scatter_dimension=1, tiled=True
    )

    middle_grad, middle_low_t, gain_two_grad, attended_grad, delta = middle_backward(
        middle, cotangent, gains, back_own, back_core, after(back_pair, ffn_grad), out_groups, attended
    )
    out_pair = swap(after(out_sum, attended_grad), "z", 1)
    out_core = core_swap(out_core)
    dq, first_grad, last_grad = attend_backward(
        info, queries, before, kv_own, attended_grad, log_sums, delta
    )
    to_before = first_grad.astype(bf16)
    dq = after(dq, out_core, out_pair, to_before)
    from_after = lax.ppermute(to_before, "z", [(i + 1, i) for i in range(0, n_z, 2)])
    parts = group_grads(info, normed_one_t, dq, middle_low_t, attended)
    if plane:
        parts = parts[0], core_swap(parts[1])
        first = [m[:, :2].reshape((2, 2, 2) + m.shape[2:]) for m in parts]
        last = [m[:, 2:] for m in parts]
        first_send = add(first[0][:, 1], first[1][:, 1])
        last_send = add(last[0][2:], last[1][2:])
        from_after = after(from_after, first_send, last_send, ffn_sum)
        first_recv, last_recv = swap(first_send, "a", 1), swap(last_send, "a", 2)
    dkv = jnp.where(second, last_grad, first_grad + from_after.astype(f32)).astype(bf16)
    input_grad, gain_grads = input_backward(
        dq, w_groups, dkv, w_shared, tokens, gains, middle_grad, gain_two_grad
    )
    ffn_sum = ffn_sum.reshape(3, 2, w_rows, hidden_width)
    crossed = [
        lax.ppermute(jnp.where(c == 0, m[1], m[0]), ("c", "z"), [(d, s) for s, d in cross])
        for m in ffn_sum
    ]
    shifted = [lax.ppermute(m[1], ("c", "z"), far_core) for m in ffn_sum]
    shared_parts = shared_grads(info, normed_one_t, dkv, after(gain_grads, crossed[0]))

    if plane:
        shared_own, shared_other = shared_parts
        shared_recv = core_swap(shared_other)
        first_recv = after(first_recv, shared_other, shifted[0], crossed[1])
        last_recv = after(last_recv, shared_other)
        first = add(add(first[0][:, 0], first[1][:, 0], f32), first_recv)
        last = add(add(last[0][:2], last[1][:2], f32), last_recv)
        first_recv, last_recv = swap(first[1], "a", 2), swap(last[1], "a", 1)
        shared_sum = add(shared_own, after(shared_recv, first, last))
        keys, values = shared_sum[..., :group_width], shared_sum[..., group_width:]
        keys = keys.reshape((2, 2) + keys.shape[1:])
        keys, keys_send, values, values_send = keys[:, 0], keys[:, 1], values[:2], values[2:]
        keys_recv, values_recv = swap(keys_send, "a", 1), swap(values_send, "a", 2)
        first_recv, last_recv = (
            after(r, keys_send, values_send, shifted[1], crossed[2]) for r in (first_recv, last_recv)
        )
        both = jnp.stack([add(first[0], first_recv), add(last[0], last_recv)])
        halves = both[..., :group_width], both[..., group_width:]
        both_send = after(jnp.where(z % 2 == 0, halves[1], halves[0]), shifted[2])
        both = jnp.where(z % 2 == 0, halves[0], halves[1])
        both_recv = swap(both_send, "z", 1)
        keys = add(keys, after(keys_recv, both_send))
        values = add(values, after(values_recv, both_send))
        keys_recv, values_recv = swap(keys[1], "a", 2), swap(values[1], "a", 1)
        both = add(both, both_recv)
        both_recv = swap(both[1], "z", 2)
        shared_sum = jnp.concatenate(
            [
                add(keys[0], after(keys_recv, both)),
                add(values[0], after(values_recv, both)),
            ],
            1,
        )
        quarters = shared_sum.reshape(2, 2, kv_rows, -1)
        kept = add(pick(quarters, z % 2, 1), swap(pick(quarters, 1 - z % 2, 1), "z", 1))
        both = add(both[0], both_recv, f32)
        kept = after(kept, both)
        shared_g = add(pick(kept, z // 2), swap(pick(kept, 1 - z // 2), "z", 2), f32)
        query_g, out_g = both[0], both[1]
    else:

        def whole_sum(blocks):
            blocks = jnp.stack(blocks, 1)
            blocks = jnp.moveaxis(blocks, 2, 0) if blocks.ndim == 5 else blocks[None]
            blocks = blocks.reshape(blocks.shape[0], width, blocks.shape[-1])
            mine = lax.psum_scatter(blocks, ("a", "c"), scatter_dimension=1, tiled=True)
            return mine.astype(f32)

        query_g, out_g = (
            lax.psum_scatter(
                whole_sum(
                    [
                        jnp.stack(
                            [
                                m[:, 2 * r + i, :, k * group_width : (k + 1) * group_width]
                                for r in range(2)
                                for k in range(2)
                            ],
                            1,
                        )
                        for m in parts
                    ]
                ),
                "z",
                scatter_dimension=0,
            )
            for i in range(2)
        )
        shared_g = lax.psum_scatter(
            whole_sum(shared_parts)[0], "z", scatter_dimension=0, tiled=True
        )
    ffn_g = [
        add(got, jnp.where(c == 0, m[0], moved), f32)
        for m, got, moved in zip(ffn_sum, crossed, shifted)
    ]
    gate_up_g = jnp.stack(ffn_g[:2])
    kv_g = jnp.stack([shared_g[:, :group_width], shared_g[:, group_width : 2 * group_width]])
    gains_g = shared_g[:, 2 * group_width : 2 * group_width + 2].T

    layer_out = (middle + add(add(out_own, out_core, f32), after(out_pair, shared_parts[0]), f32)).astype(bf16)

    first_query, second_query, new_query = adamw_step(
        w_query, query_g, m_query, v_query, rate_query, decay_rate
    )
    first_kv, second_kv, new_kv = adamw_step(w_kv, kv_g, m_kv, v_kv, rate_shared, decay_rate)
    first_out, second_out, new_out = adamw_step(
        w_out, out_g.T, m_out, v_out, rate_output, decay_rate
    )
    first_gate_up, second_gate_up, new_gate_up = adamw_step(
        w_gate_up, gate_up_g, m_gate_up, v_gate_up, rate_gate_up, decay_rate
    )
    first_down, second_down, new_down = adamw_step(
        w_down, ffn_g[2].T, m_down, v_down, rate_down, decay_rate
    )
    first_gains, second_gains, new_gains = adamw_step(
        norm_gains, gains_g, m_gains, v_gains, rate_gains, 0.0
    )
    return (
        layer_out,
        input_grad,
        first_query,
        second_query,
        new_query,
        first_kv,
        second_kv,
        new_kv,
        first_out,
        second_out,
        new_out,
        first_gate_up,
        second_gate_up,
        new_gate_up,
        first_down,
        second_down,
        new_down,
        first_gains,
        second_gains,
        new_gains,
    )


def solution(mesh):
    n_dp, n_tensor = mesh.shape["dp"], mesh.shape["tensor"]
    fine = Mesh(mesh.devices.reshape(n_dp // 2, 2, n_tensor), ("a", "c", "z"))
    dp, every = ("a", "c"), ("a", "c", "z")
    token = P(every, None)
    query = P(dp, "z")
    shared = P(None, every, None)
    output = P("z", dp)
    gate_up = P(None, dp, "z")
    gains = P(None, every)
    in_specs = (token, token, P(dp), query, shared, output, gate_up, output, gains)
    in_specs += (query, query, shared, shared, output, output, gate_up, gate_up)
    in_specs += (output, output, gains, gains)
    out_specs = (token, token) + (query,) * 3 + (shared,) * 3 + (output,) * 3
    out_specs += (gate_up,) * 3 + (output,) * 3 + (gains,) * 3
    return jax.shard_map(body, mesh=fine, in_specs=in_specs, out_specs=out_specs, check_vma=False)
```

```python
import functools

import jax
import jax.numpy as jnp
from jax import lax
from jax.experimental import pallas as pl
from jax.experimental.pallas import tpu as pltpu
from jax.sharding import Mesh, PartitionSpec as P

KV = 5
HD = 64
LEN = 1024
STEP = 10
RB = 256

beta_one = 0.9
beta_two = 0.95
adam_eps = 1e-08
decay_rate = 0.1
rate_query = 0.06
rate_shared = 0.06
rate_output = 0.8
rate_gate_up = 0.06
rate_down = 0.05
rate_gains = 0.6
norm_eps = 1e-05
neg_fill = -1e30

bf16 = jnp.bfloat16
f32 = jnp.float32
NN = (((1,), (0,)), ((), ()))
NT = (((1,), (1,)), ((), ()))
TN = (((0,), (0,)), ((), ()))
VMEM_LIMIT = 46 * 2**20
WIDE = 2 * KV * HD


def dot(a, b, dims=NN):
    return lax.dot_general(a, b, dims, preferred_element_type=f32)


def rms_scale(matrix):
    return lax.rsqrt(jnp.mean(matrix * matrix, axis=-1, keepdims=True) + norm_eps)


def norm_back(matrix, gain_row, upstream):
    scaling = rms_scale(matrix)
    unit_rows = matrix * scaling
    weighted = upstream * gain_row
    inner_mean = jnp.mean(weighted * unit_rows, axis=-1, keepdims=True)
    return (scaling * (weighted - unit_rows * inner_mean), jnp.sum(upstream * unit_rows, axis=0))


def adamw_step(weight, gradient, moment_one, moment_two, step_rate, decay_coef):
    moment_one = beta_one * moment_one + (1.0 - beta_one) * gradient
    moment_two = beta_two * moment_two + (1.0 - beta_two) * gradient * gradient
    unbiased_one = moment_one / (1.0 - beta_one**STEP)
    unbiased_two = moment_two / (1.0 - beta_two**STEP)
    updated = weight - step_rate * (
        unbiased_one / (jnp.sqrt(unbiased_two) + adam_eps) + decay_coef * weight
    )
    return (moment_one, moment_two, updated)


def columns_to_rows(columns):
    n = columns[0].shape[0]
    wide = jnp.concatenate(columns + [jnp.zeros((n, 128 - len(columns)), f32)], 1)
    return jnp.transpose(wide)[:8]


def params(flops, megabytes, transcendentals=0, weight=2.5, limit=VMEM_LIMIT):
    return dict(
        compiler_params=pltpu.CompilerParams(vmem_limit_bytes=limit),
        cost_estimate=pl.CostEstimate(
            flops=int(flops * weight), bytes_accessed=int(megabytes * weight * 1e6), transcendentals=transcendentals
        ),
    )


def attend_forward_kernel(info, q_ref, before_ref, own_ref, o_ref, lse_ref, *, rows):
    second, prefix = info[0], info[1]
    width = KV * HD

    def run(is_second):
        for block in range(rows // RB):
            base = (rows if is_second else 0) + block * RB
            row_slice = slice(block * RB, (block + 1) * RB)
            if is_second:
                spans = [(before_ref, 0, rows, None)]
                if block:
                    spans.append((own_ref, 0, block * RB, None))
                spans.append((own_ref, block * RB, RB, rows + block * RB))
            else:
                spans = [(own_ref, 0, rows, 0)]
            masks = []
            for _, _, count, masked in spans:
                if masked is None:
                    masks.append(None)
                else:
                    at = lax.broadcasted_iota(jnp.int32, (RB, count), 1) + masked
                    row = lax.broadcasted_iota(jnp.int32, (RB, count), 0) + base
                    masks.append((at <= row) | (at < prefix))
            outs, logs = [], []
            for c in range(KV):
                cols = slice(c * HD, (c + 1) * HD)
                values = slice(width + c * HD, width + (c + 1) * HD)
                query = q_ref[0, row_slice, cols]
                scores = []
                for (ref, start, count, _), mask in zip(spans, masks):
                    part = dot(query, ref[start : start + count, cols], NT)
                    scores.append(part if mask is None else jnp.where(mask, part, neg_fill))
                highest = functools.reduce(
                    jnp.maximum, [jnp.max(s, axis=1, keepdims=True) for s in scores]
                )
                total, mixed = 0.0, 0.0
                for (ref, start, count, _), part in zip(spans, scores):
                    expo = jnp.exp(part - highest)
                    total = total + jnp.sum(expo, axis=1, keepdims=True)
                    mixed = mixed + dot(expo.astype(bf16), ref[start : start + count, values])
                outs.append((mixed / total).astype(bf16))
                logs.append(highest + jnp.log(total))
            o_ref[0, row_slice, :] = jnp.concatenate(outs, 1)
            lse_ref[0, :, row_slice] = columns_to_rows(logs)

    pl.when(second == 0)(lambda: run(False))
    pl.when(second == 1)(lambda: run(True))


def attend_forward(info, queries, before, own):
    groups, rows, width = queries.shape
    block = pl.BlockSpec((1, rows, width), lambda r, _: (r, 0, 0))
    whole = pl.BlockSpec(own.shape, lambda r, _: (0, 0))
    elements = groups * rows * KV * 2 * rows
    return pl.pallas_call(
        functools.partial(attend_forward_kernel, rows=rows),
        grid_spec=pltpu.PrefetchScalarGridSpec(
            num_scalar_prefetch=1,
            grid=(groups,),
            in_specs=[block, whole, whole],
            out_specs=[block, pl.BlockSpec((1, 8, rows), lambda r, _: (r, 0, 0))],
        ),
        out_shape=[
            jax.ShapeDtypeStruct(queries.shape, bf16),
            jax.ShapeDtypeStruct((groups, 8, rows), f32),
        ],
        name="attend_forward",
        **params(elements * 900, 4, elements, limit=28 * 2**20),
    )(info, queries, before, own)


def attend_backward_kernel(
    info, q_ref, before_ref, own_ref, do_ref, lse_ref, delta_ref, dq_ref, first_ref, last_ref, dk_acc, dv_acc, *, rows
):
    second, prefix = info[0], info[1]
    group = pl.program_id(0)
    width = KV * HD

    @pl.when(group == 0)
    def _():
        dk_acc[...] = jnp.zeros_like(dk_acc)
        dv_acc[...] = jnp.zeros_like(dv_acc)

    def run(is_second):
        for block in range(rows // RB):
            base = (rows if is_second else 0) + block * RB
            row_slice = slice(block * RB, (block + 1) * RB)
            steps = rows // RB
            if is_second:
                spans = [(before_ref, i * RB, i * RB, False) for i in range(steps)]
                spans += [(own_ref, i * RB, rows + i * RB, i == block) for i in range(block + 1)]
            else:
                spans = [(own_ref, i * RB, i * RB, True) for i in range(steps)]
            query_grads = []
            for c in range(KV):
                cols = slice(c * HD, (c + 1) * HD)
                values = slice(width + c * HD, width + (c + 1) * HD)
                query, out_grad = q_ref[0, row_slice, cols], do_ref[0, row_slice, cols]
                log_sum = lse_ref[0, c : c + 1, row_slice]
                delta = delta_ref[0, c : c + 1, row_slice]
                query_grad = jnp.zeros((RB, HD), f32)
                for ref, start, position, masked in spans:
                    key, value = ref[start : start + RB, cols], ref[start : start + RB, values]
                    scores = dot(key, query, NT) - log_sum
                    if masked:
                        at = lax.broadcasted_iota(jnp.int32, (RB, RB), 0) + position
                        row = lax.broadcasted_iota(jnp.int32, (RB, RB), 1) + base
                        scores = jnp.where((at <= row) | (at < prefix), scores, neg_fill)
                    probs = jnp.exp(scores)
                    probs_grad = dot(value, out_grad, NT)
                    score_grad = (probs * (probs_grad - delta)).astype(bf16)
                    at_keys = slice(position, position + RB)
                    dv_acc[c, at_keys, :] += dot(probs.astype(bf16), out_grad)
                    dk_acc[c, at_keys, :] += dot(score_grad, query)
                    query_grad = query_grad + dot(score_grad, key, TN)
                query_grads.append((query_grad * HD**-0.5).astype(bf16))
            dq_ref[0, row_slice, :] = jnp.concatenate(query_grads, 1)

    pl.when(second == 0)(lambda: run(False))
    pl.when(second == 1)(lambda: run(True))

    @pl.when(group == pl.num_programs(0) - 1)
    def _():
        for ref, part in ((first_ref, slice(0, rows)), (last_ref, slice(rows, 2 * rows))):
            ref[...] = jnp.concatenate(
                [acc[c, part, :] for acc in (dk_acc, dv_acc) for c in range(KV)], 1
            )


def attend_backward(info, queries, before, own, out_grad, log_sums, delta):
    groups, rows, width = queries.shape
    block = pl.BlockSpec((1, rows, width), lambda r, _: (r, 0, 0))
    whole = pl.BlockSpec(own.shape, lambda r, _: (0, 0))
    stats = pl.BlockSpec((1, 8, rows), lambda r, _: (r, 0, 0))
    elements = groups * rows * KV * 2 * rows
    return pl.pallas_call(
        functools.partial(attend_backward_kernel, rows=rows),
        grid_spec=pltpu.PrefetchScalarGridSpec(
            num_scalar_prefetch=1,
            grid=(groups,),
            in_specs=[block, whole, whole, block, stats, stats],
            out_specs=[block, whole, whole],
            scratch_shapes=[pltpu.VMEM((KV, 2 * rows, HD), f32)] * 2,
        ),
        out_shape=[jax.ShapeDtypeStruct(queries.shape, bf16)]
        + [jax.ShapeDtypeStruct(own.shape, f32)] * 2,
        name="attend_backward",
        **params(elements * 2500, 8, elements, limit=28 * 2**20),
    )(info, queries, before, own, out_grad, log_sums, delta)


BLOCKS = 4
SWAPPED = (0, 2, 1, 3)


def block_row(info, j, other):
    return (((info[2] ^ j) * 2) + (info[3] ^ other)) * 160


def pair_of(ref):
    return jnp.concatenate([ref[0], ref[1]], 1)


def put_together(info, refs, w_ref):
    width = KV * HD
    for i, ref in enumerate(refs):
        part, other = i // 2, i % 2
        for j in range(BLOCKS):
            at = block_row(info, SWAPPED[j] if part else j, other) + part * 80
            block = ref[j]
            w_ref[pl.ds(pl.multiple_of(at, 16), 80), :] = jnp.concatenate(
                [block[:80, :width], block[80:, :width]], 1
            )


def shared_kernel(info, tok_ref, ka, kb, va, vb, normed_ref, normed_t_ref, kv_ref, gain_ref, wkv_ref, gains):
    width = KV * HD
    for other, (k_ref, v_ref) in enumerate(((ka, va), (kb, vb))):
        for j in range(BLOCKS):
            at = pl.ds(pl.multiple_of(block_row(info, j, other), 160), 160)
            wkv_ref[at, :width] = k_ref[j][:, :width]
            gains[0, at, :] = k_ref[j][:, 256:].astype(f32)
            at = pl.ds(pl.multiple_of(block_row(info, SWAPPED[j], other), 160), 160)
            wkv_ref[at, width:] = v_ref[j][:, :width]
            gains[1, at, :] = v_ref[j][:, 256:].astype(f32)
    one = jnp.transpose(gains[0])[64:72]
    two = jnp.transpose(gains[1])[64:72]
    gain_ref[...] = jnp.concatenate([one[:1], two[:1], jnp.zeros((6, one.shape[1]), f32)], 0)
    tok = tok_ref[...].astype(f32)
    normed = (tok * rms_scale(tok) * one[:1]).astype(bf16)
    normed_ref[...] = normed
    normed_t_ref[...] = jnp.transpose(normed)
    kv_ref[...] = dot(normed, wkv_ref[...]).astype(bf16)


def project_shared(info, tokens, parts):
    rows, depth = tokens.shape
    width = 2 * KV * HD
    whole = lambda *shape: pl.BlockSpec(shape, lambda i, _: (0,) * len(shape))
    block = pl.BlockSpec((BLOCKS, 160, 384), lambda i, _: (0, 4, 0))
    return pl.pallas_call(
        shared_kernel,
        grid_spec=pltpu.PrefetchScalarGridSpec(
            num_scalar_prefetch=1,
            grid=(1,),
            in_specs=[whole(rows, depth)] + [block] * 4,
            out_specs=[
                whole(rows, depth),
                whole(depth, rows),
                whole(rows, width),
                whole(8, depth),
                whole(depth, width),
            ],
            scratch_shapes=[pltpu.VMEM((2, depth, 128), f32)],
        ),
        out_shape=[
            jax.ShapeDtypeStruct((rows, depth), bf16),
            jax.ShapeDtypeStruct((depth, rows), bf16),
            jax.ShapeDtypeStruct((rows, width), bf16),
            jax.ShapeDtypeStruct((8, depth), f32),
            jax.ShapeDtypeStruct((depth, width), bf16),
        ],
        name="project_shared",
        **params(2 * rows * depth * width, 8),
    )(info, tokens, *parts)


def query_kernel(info, x_ref, a0, b0, a1, b1, c0, d0, c1, d1, q_ref, w_ref, wo_ref):
    put_together(info, (a0, b0, a1, b1), w_ref)
    put_together(info, (c0, d0, c1, d1), wo_ref)
    result = (dot(x_ref[...], w_ref[...]).astype(bf16) * HD**-0.5).astype(bf16)
    q_ref[0] = result[:, : KV * HD]
    q_ref[1] = result[:, KV * HD :]


def project_queries(info, normed, parts):
    rows, depth = normed.shape
    query = pl.BlockSpec((BLOCKS, 160, 384), lambda r, _: (0, r, 0))
    output = pl.BlockSpec((BLOCKS, 160, 384), lambda r, _: (0, 2 + r, 0))
    weights = pl.BlockSpec((depth, WIDE), lambda r, _: (0, r))
    return pl.pallas_call(
        query_kernel,
        grid_spec=pltpu.PrefetchScalarGridSpec(
            num_scalar_prefetch=1,
            grid=(2,),
            in_specs=[pl.BlockSpec((rows, depth), lambda r, _: (0, 0))] + [query] * 4 + [output] * 4,
            out_specs=[
                pl.BlockSpec((2, rows, WIDE // 2), lambda r, _: (r, 0, 0)),
                weights,
                weights,
            ],
        ),
        out_shape=[jax.ShapeDtypeStruct((4, rows, WIDE // 2), bf16)]
        + [jax.ShapeDtypeStruct((depth, 2 * WIDE), bf16)] * 2,
        name="project_queries",
        **params(4 * rows * depth * WIDE, 14),
    )(info, normed, *parts, *parts)


def output_kernel(att_ref, w_ref, tok_ref, gain_ref, middle_ref, normed_ref, acc):
    part = dot(pair_of(att_ref), w_ref[...], NT)

    @pl.when(pl.program_id(0) == 0)
    def _():
        acc[...] = tok_ref[...].astype(f32) + part

    @pl.when(pl.program_id(0) == 1)
    def _():
        middle = acc[...] + part
        middle_ref[...] = middle
        normed_ref[...] = (middle * rms_scale(middle) * gain_ref[1:2]).astype(bf16)


def project_output(attended, w_out, tokens, gains):
    rows, depth = tokens.shape
    whole = lambda *shape: pl.BlockSpec(shape, lambda r: (0,) * len(shape))
    return pl.pallas_call(
        output_kernel,
        grid=(2,),
        in_specs=[
            pl.BlockSpec((2, rows, WIDE // 2), lambda r: (r, 0, 0)),
            pl.BlockSpec((depth, WIDE), lambda r: (0, r)),
            whole(rows, depth),
            whole(8, depth),
        ],
        out_specs=[whole(rows, depth)] * 2,
        out_shape=[
            jax.ShapeDtypeStruct((rows, depth), f32),
            jax.ShapeDtypeStruct((rows, depth), bf16),
        ],
        scratch_shapes=[pltpu.VMEM((rows, depth), f32)],
        name="project_output",
        **params(4 * rows * depth * WIDE, 12),
    )(attended, w_out, tokens, gains)


def feed_forward_kernel(xa, xb, ca, cb, w_ref, inner_ref, out_a, out_b, back_a, back_b):
    def run(x_ref, c_ref, out_ref, back_ref):
        x, cot = x_ref[...], c_ref[...]
        gate = dot(x, w_ref[0])
        up = dot(x, w_ref[1])
        hidden_grad = dot(cot, w_ref[2])
        sig = jax.nn.sigmoid(gate)
        silu = gate * sig
        hidden = (silu * up).astype(bf16)
        inner_ref[2] = hidden
        gate_grad = (hidden_grad * up * sig * (1.0 + gate * (1.0 - sig))).astype(bf16)
        inner_ref[0] = gate_grad
        up_grad = (hidden_grad * silu).astype(bf16)
        inner_ref[1] = up_grad
        out_ref[...] = dot(hidden, w_ref[2], NT).astype(bf16)
        back_ref[...] = (dot(gate_grad, w_ref[0], NT) + dot(up_grad, w_ref[1], NT)).astype(bf16)

    pl.when(pl.program_id(0) < pl.num_programs(0) // 2)(lambda: run(xa, ca, out_a, back_a))
    pl.when(pl.program_id(0) >= pl.num_programs(0) // 2)(lambda: run(xb, cb, out_b, back_b))


def feed_forward(normed, cots, weights):
    rows, depth = normed[0].shape
    width = weights.shape[2]
    tile = 256
    steps = rows // tile
    first = pl.BlockSpec((tile, depth), lambda i: (jnp.minimum(i, steps - 1), 0))
    last = pl.BlockSpec((tile, depth), lambda i: (jnp.maximum(i - steps, 0), 0))
    inner = pl.BlockSpec((3, tile, width), lambda i: (0, i, 0))
    whole = pl.BlockSpec(weights.shape, lambda i: (0, 0, 0), pipeline_mode=pl.Buffered(1))
    return pl.pallas_call(
        feed_forward_kernel,
        grid=(2 * steps,),
        in_specs=[first, last, first, last, whole],
        out_specs=[inner, first, last, first, last],
        out_shape=[jax.ShapeDtypeStruct((3, 2 * rows, width), bf16)]
        + [jax.ShapeDtypeStruct((rows, depth), bf16)] * 4,
        name="feed_forward",
        **params(24 * rows * depth * width, 24),
    )(*normed, *cots, weights)


def hidden_grad_kernel(x0, x1, x2, x3, c0, c1, c2, c3, near_ref, far_ref, out_ref):
    def run(lefts):
        rows = lefts[0].shape[0]
        total = 0.0
        for left, (right, at) in zip(lefts, ((near_ref, 0), (near_ref, 1), (far_ref, 0), (far_ref, 1))):
            total = total + dot(left[...], right[0, at * rows : (at + 1) * rows, :], TN)
        out_ref[0] = total.astype(bf16)

    pl.when(pl.program_id(0) < 2)(lambda: run((x0, x1, x2, x3)))
    pl.when(pl.program_id(0) == 2)(lambda: run((c0, c1, c2, c3)))


def hidden_grads(normed, cots, near, far):
    rows, depth = normed[0].shape
    width = near.shape[2]
    tile = 640
    last = depth // tile - 1
    left = pl.BlockSpec((rows, tile), lambda m, i: (0, jnp.where(m < 2, i, last)))
    cot = pl.BlockSpec((rows, tile), lambda m, i: (0, jnp.where(m < 2, 0, i)))
    right = pl.BlockSpec((1, 2 * rows, width), lambda m, i: (m, 0, 0))
    return pl.pallas_call(
        hidden_grad_kernel,
        grid=(3, depth // tile),
        in_specs=[left] * 4 + [cot] * 4 + [right] * 2,
        out_specs=pl.BlockSpec((1, tile, width), lambda m, i: (m, i, 0)),
        out_shape=jax.ShapeDtypeStruct((3, depth, width), bf16),
        name="hidden_grads",
        **params(24 * rows * depth * width, 28),
    )(*normed, *cots, near, far)


def middle_kernel(
    middle_ref, cot_ref, gain_ref, near_ref, core_ref, far_ref, w_ref, att_ref,
    grad_ref, low_t_ref, gain_grad_ref, do_ref, delta_ref, low,
):
    @pl.when(pl.program_id(0) == 0)
    def _():
        upstream = near_ref[...].astype(f32) + core_ref[...].astype(f32) + far_ref[...].astype(f32)
        middle = middle_ref[...]
        scaling = rms_scale(middle)
        unit_rows = middle * scaling
        gain_grad = jnp.sum(upstream * unit_rows, axis=0, keepdims=True)
        gain_grad_ref[...] = jnp.broadcast_to(gain_grad, gain_grad_ref.shape)
        weighted = upstream * gain_ref[1:2]
        inner_mean = jnp.mean(weighted * unit_rows, axis=-1, keepdims=True)
        grad = cot_ref[...].astype(f32) + scaling * (weighted - unit_rows * inner_mean)
        grad_ref[...] = grad
        low[...] = grad.astype(bf16)
        low_t_ref[...] = jnp.transpose(low[...])

    grad = dot(low[...], w_ref[...]).astype(bf16)
    do_ref[0] = grad[:, : WIDE // 2]
    do_ref[1] = grad[:, WIDE // 2 :]
    product = grad.astype(f32) * pair_of(att_ref).astype(f32)
    high = product.astype(bf16)
    rest = (product - high.astype(f32)).astype(bf16)
    row = lax.broadcasted_iota(jnp.int32, (16, WIDE), 0)
    head = jnp.where(row < 8, jnp.where(row < KV, row, -1), jnp.where(row < 8 + KV, row - 8 + KV, -1))
    column = lax.broadcasted_iota(jnp.int32, (16, WIDE), 1)
    member = ((column >= head * HD) & (column < (head + 1) * HD)).astype(f32).astype(bf16)
    delta = dot(member, high, NT) + dot(member, rest, NT)
    delta_ref[0] = delta[:8]
    delta_ref[1] = delta[8:]


def middle_backward(middle, cot, gains, near, core, far, w_out, attended):
    rows, depth = middle.shape
    block = pl.BlockSpec((2, rows, WIDE // 2), lambda r: (r, 0, 0))
    whole = lambda *shape: pl.BlockSpec(shape, lambda r: (0,) * len(shape))
    token = whole(rows, depth)
    return pl.pallas_call(
        middle_kernel,
        grid=(2,),
        in_specs=[token, token, whole(8, depth), token, token, token]
        + [pl.BlockSpec((depth, WIDE), lambda r: (0, r)), block],
        out_specs=[
            token,
            whole(depth, rows),
            whole(8, depth),
            block,
            pl.BlockSpec((2, 8, rows), lambda r: (r, 0, 0)),
        ],
        out_shape=[
            jax.ShapeDtypeStruct((rows, depth), f32),
            jax.ShapeDtypeStruct((depth, rows), bf16),
            jax.ShapeDtypeStruct((8, depth), f32),
            jax.ShapeDtypeStruct((4, rows, WIDE // 2), bf16),
            jax.ShapeDtypeStruct((4, 8, rows), f32),
        ],
        scratch_shapes=[pltpu.VMEM((rows, depth), bf16)],
        name="middle_backward",
        **params(4 * rows * depth * WIDE, 20),
    )(middle, cot, gains, near, core, far, w_out, attended)


def input_kernel(
    dq_ref, wq_ref, dkv_ref, wkv_ref, tok_ref, gain_ref, grad_ref, two_ref, out_ref, gain_grad_ref, acc
):
    group = pl.program_id(0)

    @pl.when(group == 0)
    def _():
        acc[...] = dot(dkv_ref[...], wkv_ref[...], NT)

    acc[...] += dot(pair_of(dq_ref), wq_ref[...], NT)

    @pl.when(group == pl.num_programs(0) - 1)
    def _():
        upstream = acc[...]
        tok = tok_ref[...].astype(f32)
        scaling = rms_scale(tok)
        unit_rows = tok * scaling
        one = jnp.sum(upstream * unit_rows, axis=0, keepdims=True)
        gain_grad_ref[...] = jnp.concatenate([one, two_ref[:7]], 0)
        weighted = upstream * gain_ref[0:1]
        inner_mean = jnp.mean(weighted * unit_rows, axis=-1, keepdims=True)
        out_ref[...] = grad_ref[...] + scaling * (weighted - unit_rows * inner_mean)


def input_backward(dq, wq, dkv, wkv, tokens, gains, middle_grad, gain_two):
    rows, depth = tokens.shape
    whole = lambda *shape: pl.BlockSpec(shape, lambda r: (0,) * len(shape))
    token = whole(rows, depth)
    return pl.pallas_call(
        input_kernel,
        grid=(2,),
        in_specs=[
            pl.BlockSpec((2, rows, WIDE // 2), lambda r: (r, 0, 0)),
            pl.BlockSpec((depth, WIDE), lambda r: (0, r)),
            whole(*dkv.shape),
            whole(*wkv.shape),
            token,
            whole(8, depth),
            token,
            whole(8, depth),
        ],
        out_specs=[token, whole(8, depth)],
        out_shape=[
            jax.ShapeDtypeStruct((rows, depth), f32),
            jax.ShapeDtypeStruct((8, depth), f32),
        ],
        scratch_shapes=[pltpu.VMEM((rows, depth), f32)],
        name="input_backward",
        **params(6 * rows * depth * WIDE, 20),
    )(dq, wq, dkv, wkv, tokens, gains, middle_grad, gain_two)


def group_grad_kernel(info, left_a, right_a, left_b, right_b, own_ref, other_ref, whole):
    @pl.when(pl.program_id(1) == 0)
    def _():
        whole[...] = dot(left_a[...], pair_of(right_a)).astype(bf16)

    @pl.when(pl.program_id(1) == 1)
    def _():
        whole[...] = dot(left_b[...], pair_of(right_b)).astype(bf16)

    for other, ref in enumerate((own_ref, other_ref)):
        for j in range(BLOCKS):
            ref[j, 0] = whole[pl.ds(pl.multiple_of(block_row(info, j, other), 160), 160), :]


def group_grads(info, left_a, right_a, left_b, right_b):
    groups, rows, width = right_a.shape
    depth = left_a.shape[0]
    left = pl.BlockSpec((depth, rows), lambda r, w, _: (0, 0))
    right = pl.BlockSpec((2, rows, width), lambda r, w, info: (r ^ (info[4] >> 1), 0, 0))
    block = pl.BlockSpec((BLOCKS, 1, 160, WIDE), lambda r, w, _: (0, 2 * r + w, 0, 0))
    return pl.pallas_call(
        group_grad_kernel,
        grid_spec=pltpu.PrefetchScalarGridSpec(
            num_scalar_prefetch=1,
            grid=(2, 2),
            in_specs=[left, right] * 2,
            out_specs=[block] * 2,
            scratch_shapes=[pltpu.VMEM((depth, WIDE), bf16)],
        ),
        out_shape=[jax.ShapeDtypeStruct((BLOCKS, groups, 160, WIDE), bf16)] * 2,
        name="group_grads",
        **params(8 * rows * depth * WIDE, 12),
    )(info, left_a, right_a, left_b, right_b)


def shared_grad_kernel(info, left_ref, right_ref, gain_ref, own_ref, other_ref, whole):
    wide = jnp.concatenate([gain_ref[...], jnp.zeros((120, gain_ref.shape[1]), f32)], 0)
    width = right_ref.shape[1]
    whole[:, width:] = jnp.transpose(wide).astype(bf16)
    whole[:, :width] = dot(left_ref[...], right_ref[...]).astype(bf16)
    for other, ref in enumerate((own_ref, other_ref)):
        for j in range(BLOCKS):
            at = pl.ds(pl.multiple_of(block_row(info, j, other), 160), 160)
            ref[j] = whole[at, :]


def shared_grads(info, left, right, gain_grads):
    rows, width = right.shape
    depth = left.shape[0]
    whole = lambda *shape: pl.BlockSpec(shape, lambda i, _: (0,) * len(shape))
    return pl.pallas_call(
        shared_grad_kernel,
        grid_spec=pltpu.PrefetchScalarGridSpec(
            num_scalar_prefetch=1,
            grid=(1,),
            in_specs=[whole(depth, rows), whole(rows, width), whole(8, depth)],
            out_specs=[whole(BLOCKS, 160, width + 128)] * 2,
            scratch_shapes=[pltpu.VMEM((depth, width + 128), bf16)],
        ),
        out_shape=[jax.ShapeDtypeStruct((BLOCKS, 160, width + 128), bf16)] * 2,
        name="shared_grads",
        **params(2 * rows * depth * width, 6),
    )(info, left, right, gain_grads)


def swap(value, axis, bit):
    size = lax.axis_size(axis)
    return lax.ppermute(value, axis, [(i, i ^ bit) for i in range(size)])


def core_swap(value):
    return swap(value, "c", 1)


def placed(own, other, bit, axis=0):
    return jnp.concatenate(
        [jnp.where(bit == 0, own, other), jnp.where(bit == 0, other, own)], axis
    )


def gather_line(own, z):
    pair = placed(own, swap(own, "z", 2), z // 2)
    size = own.shape[0]
    near = swap(pair, "z", 1)
    both = [jnp.where(z % 2 == 0, pair, near), jnp.where(z % 2 == 0, near, pair)]
    return jnp.concatenate(
        [part[i * size : (i + 1) * size] for i in range(2) for part in both], 0
    )


def gather_plane(blocks, bit):
    return jnp.concatenate([blocks, swap(blocks, "a", bit)], 0)


def add(one, two, kind=bf16):
    return (one.astype(f32) + two.astype(f32)).astype(kind)


def reduce_core(parts):
    own, other = parts
    return add(own, core_swap(other))


def reduce_plane(blocks, bits):
    if bits[0] == 1:
        blocks = blocks.reshape((2, 2) + blocks.shape[1:])
        blocks = add(blocks[:, 0], swap(blocks[:, 1], "a", 1))
    else:
        blocks = add(blocks[:2], swap(blocks[2:], "a", 2))
    return add(blocks[0], swap(blocks[1], "a", bits[1]))


def pick(stacked, index, axis=0):
    return lax.dynamic_index_in_dim(stacked, index, axis, keepdims=False)


def after(value, *earlier):
    return lax.optimization_barrier((value,) + earlier)[0]


def head_weights(w_query, w_kv, w_out, norm_gains, z, beside):
    w_rows, group_width = w_query.shape
    kv_rows = w_kv.shape[1]
    n_a, n_z = lax.axis_size("a"), lax.axis_size("z")
    pad = lambda m: jnp.pad(m.astype(bf16), ((0, 0), (0, 384 - m.shape[1])))
    shared = [pad(jnp.concatenate([w_kv[i], norm_gains[i][:, None]], 1)) for i in range(2)]
    query, output = pad(w_query), pad(w_out.T)
    if n_a == BLOCKS:
        half = w_rows // 2
        line = gather_line(jnp.concatenate([query, output] + shared, 0)[None], z)
        moved = beside(line)
        packs = []
        for i, bits in enumerate(((1, 2), (2, 1))):
            starts = (i * half, w_rows + i * half, 2 * w_rows + i * kv_rows)
            counts = (half, half, kv_rows)
            own = [line[:, s : s + n].reshape(n_z * n, 384) for s, n in zip(starts, counts)]
            blocks = gather_plane(jnp.concatenate(own, 0)[None], bits[0])
            packs.append((blocks, swap(blocks, "a", bits[1])))
        return packs, moved
    every = ("a", "c", "z")

    def groups(own):
        got = lax.all_gather(own, every, axis=0).reshape(2 * n_a, n_z, w_rows, 384)
        return jnp.transpose(got, (1, 0, 2, 3)).reshape(n_z, BLOCKS, 2, 160, 384)

    query, output = groups(query), groups(output)
    result = []
    for i in range(2):
        kv = lax.all_gather(shared[i], every, axis=0).reshape(BLOCKS, 2, 160, 384)
        halves = [
            jnp.transpose(m[:, :, :, i * 80 : (i + 1) * 80], (1, 2, 0, 3, 4)).reshape(
                BLOCKS, 2, n_z * 80, 384
            )
            for m in (query, output)
        ]
        part = jnp.concatenate(halves + [kv], 2)
        if i:
            part = part[jnp.array(SWAPPED)]
        result += [part[:, 0], part[:, 1]]
    return result, beside(query)


def body(
    tokens,
    cotangent,
    prefix_len,
    w_query,
    w_kv,
    w_out,
    w_gate_up,
    w_down,
    norm_gains,
    m_query,
    v_query,
    m_kv,
    v_kv,
    m_out,
    v_out,
    m_gate_up,
    v_gate_up,
    m_down,
    v_down,
    m_gains,
    v_gains,
):
    rows, width = tokens.shape
    a, c, z = lax.axis_index("a"), lax.axis_index("c"), lax.axis_index("z")
    n_a, n_z = lax.axis_size("a"), lax.axis_size("z")
    plane = n_a == BLOCKS
    w_rows, group_width = w_query.shape
    kv_rows = w_kv.shape[1]
    hidden_width = w_gate_up.shape[2]
    second = (z % (LEN // rows)) == 1
    seq_at = z // (LEN // rows)
    at = [a, c, z] if plane else [0, 0, 0]
    info = jnp.stack([second, pick(prefix_len, seq_at)] + at).astype(jnp.int32)

    ffn_own = jnp.concatenate([w_gate_up, w_down.T[None]], 0).astype(bf16)
    cross = [(n_z + zz, zz) for zz in range(n_z)] + [(zz, n_z + (zz ^ 2)) for zz in range(n_z)]
    far_core = [(n_z + zz, n_z + (zz ^ 2)) for zz in range(n_z)]

    def cross_line(line):
        block = after(ffn_own, line)
        return lax.ppermute(block, ("c", "z"), cross), lax.ppermute(block, ("c", "z"), far_core)

    parts, moved = head_weights(w_query, w_kv, w_out, norm_gains, z, cross_line)
    crossed, shifted = moved
    ffn_blocks = jnp.concatenate(
        [jnp.where(c == 0, ffn_own, crossed), jnp.where(c == 0, crossed, shifted)], 1
    )
    if plane:
        ffn_blocks = after(ffn_blocks, *(received for _, received in parts))
        first, last = (jnp.concatenate(pair, 0) for pair in parts)
        parts = first, core_swap(first), last, core_swap(last)
    ffn_w = lax.all_gather(ffn_blocks, "a", axis=1, tiled=True)

    normed_one, normed_one_t, kv_own, gains, w_shared = project_shared(info, tokens, parts)
    before = lax.ppermute(kv_own, "z", [(i, i + 1) for i in range(0, n_z, 2)])
    queries, w_groups, out_groups = project_queries(info, normed_one, parts)
    before = after(before, queries)
    cot_core = core_swap(after(cotangent, before))
    cot_pair = swap(after(cotangent, crossed, shifted), "z", 1)
    attended, log_sums = attend_forward(info, queries, before, kv_own)
    cot_pair = after(cot_pair, attended)
    cots = cotangent, cot_core, cot_pair, core_swap(cot_pair)
    middle, normed_two = project_output(attended, out_groups, after(tokens, cots[3]), gains)

    two_core, two_pair = core_swap(normed_two), swap(normed_two, "z", 1)
    inner_near, out_own, out_core, back_own, back_core = feed_forward(
        (normed_two, two_core), cots[:2], ffn_w
    )
    back_core = core_swap(back_core)
    two_pair = after(two_pair, inner_near)
    twos = (normed_two, two_core, two_pair, core_swap(two_pair))
    inner_far, out_far, out_far_core, back_far, back_far_core = feed_forward(
        twos[2:], cots[2:], ffn_w
    )
    back_sum = add(back_far, core_swap(back_far_core))
    back_pair = swap(back_sum, "z", 1)
    ffn_grad = hidden_grads(twos, cots, inner_near, after(inner_far, back_sum, back_core))
    out_sum = add(out_far, core_swap(out_far_core))
    ffn_sum = lax.psum_scatter(
        after(ffn_grad, back_pair, out_sum), "a", scatter_dimension=1, tiled=True
    )

    middle_grad, middle_low_t, gain_two_grad, attended_grad, delta = middle_backward(
        middle, cotangent, gains, back_own, back_core, after(back_pair, ffn_grad), out_groups, attended
    )
    out_pair = swap(after(out_sum, attended_grad), "z", 1)
    out_core = core_swap(out_core)
    dq, first_grad, last_grad = attend_backward(
        info, queries, before, kv_own, attended_grad, log_sums, delta
    )
    to_before = first_grad.astype(bf16)
    dq = after(dq, out_core, out_pair, to_before)
    from_after = lax.ppermute(to_before, "z", [(i + 1, i) for i in range(0, n_z, 2)])
    parts = group_grads(info, normed_one_t, dq, middle_low_t, attended)
    if plane:
        parts = parts[0], core_swap(parts[1])
        first = [m[:, :2].reshape((2, 2, 2) + m.shape[2:]) for m in parts]
        last = [m[:, 2:] for m in parts]
        first_send = add(first[0][:, 1], first[1][:, 1])
        last_send = add(last[0][2:], last[1][2:])
        from_after = after(from_after, first_send, last_send, ffn_sum)
        first_recv, last_recv = swap(first_send, "a", 1), swap(last_send, "a", 2)
    dkv = jnp.where(second, last_grad, first_grad + from_after.astype(f32)).astype(bf16)
    input_grad, gain_grads = input_backward(
        dq, w_groups, dkv, w_shared, tokens, gains, middle_grad, gain_two_grad
    )
    ffn_sum = ffn_sum.reshape(3, 2, w_rows, hidden_width)
    crossed = [
        lax.ppermute(jnp.where(c == 0, m[1], m[0]), ("c", "z"), [(d, s) for s, d in cross])
        for m in ffn_sum
    ]
    shifted = [lax.ppermute(m[1], ("c", "z"), far_core) for m in ffn_sum]
    shared_parts = shared_grads(info, normed_one_t, dkv, after(gain_grads, crossed[0]))

    if plane:
        shared_own, shared_other = shared_parts
        shared_recv = core_swap(shared_other)
        first_recv = after(first_recv, shared_other, shifted[0], crossed[1])
        last_recv = after(last_recv, shared_other)
        first = add(add(first[0][:, 0], first[1][:, 0], f32), first_recv)
        last = add(add(last[0][:2], last[1][:2], f32), last_recv)
        first_recv, last_recv = swap(first[1], "a", 2), swap(last[1], "a", 1)
        shared_sum = add(shared_own, after(shared_recv, first, last))
        keys, values = shared_sum[..., :group_width], shared_sum[..., group_width:]
        keys = keys.reshape((2, 2) + keys.shape[1:])
        keys, keys_send, values, values_send = keys[:, 0], keys[:, 1], values[:2], values[2:]
        keys_recv, values_recv = swap(keys_send, "a", 1), swap(values_send, "a", 2)
        first_recv, last_recv = (
            after(r, keys_send, values_send, shifted[1], crossed[2]) for r in (first_recv, last_recv)
        )
        both = jnp.stack([add(first[0], first_recv), add(last[0], last_recv)])
        halves = both[..., :group_width], both[..., group_width:]
        both_send = after(jnp.where(z % 2 == 0, halves[1], halves[0]), shifted[2])
        both = jnp.where(z % 2 == 0, halves[0], halves[1])
        both_recv = swap(both_send, "z", 1)
        keys = add(keys, after(keys_recv, both_send))
        values = add(values, after(values_recv, both_send))
        keys_recv, values_recv = swap(keys[1], "a", 2), swap(values[1], "a", 1)
        both = add(both, both_recv)
        both_recv = swap(both[1], "z", 2)
        shared_sum = jnp.concatenate(
            [
                add(keys[0], after(keys_recv, both)),
                add(values[0], after(values_recv, both)),
            ],
            1,
        )
        quarters = shared_sum.reshape(2, 2, kv_rows, -1)
        kept = add(pick(quarters, z % 2, 1), swap(pick(quarters, 1 - z % 2, 1), "z", 1))
        both = add(both[0], both_recv, f32)
        kept = after(kept, both)
        shared_g = add(pick(kept, z // 2), swap(pick(kept, 1 - z // 2), "z", 2), f32)
        query_g, out_g = both[0], both[1]
    else:

        def whole_sum(blocks):
            blocks = jnp.stack(blocks, 1)
            blocks = jnp.moveaxis(blocks, 2, 0) if blocks.ndim == 5 else blocks[None]
            blocks = blocks.reshape(blocks.shape[0], width, blocks.shape[-1])
            mine = lax.psum_scatter(blocks, ("a", "c"), scatter_dimension=1, tiled=True)
            return mine.astype(f32)

        query_g, out_g = (
            lax.psum_scatter(
                whole_sum(
                    [
                        jnp.stack(
                            [
                                m[:, 2 * r + i, :, k * group_width : (k + 1) * group_width]
                                for r in range(2)
                                for k in range(2)
                            ],
                            1,
                        )
                        for m in parts
                    ]
                ),
                "z",
                scatter_dimension=0,
            )
            for i in range(2)
        )
        shared_g = lax.psum_scatter(
            whole_sum(shared_parts)[0], "z", scatter_dimension=0, tiled=True
        )
    ffn_g = [
        add(got, jnp.where(c == 0, m[0], moved), f32)
        for m, got, moved in zip(ffn_sum, crossed, shifted)
    ]
    gate_up_g = jnp.stack(ffn_g[:2])
    kv_g = jnp.stack([shared_g[:, :group_width], shared_g[:, group_width : 2 * group_width]])
    gains_g = shared_g[:, 2 * group_width : 2 * group_width + 2].T

    layer_out = (middle + add(add(out_own, out_core, f32), after(out_pair, shared_parts[0]), f32)).astype(bf16)

    first_query, second_query, new_query = adamw_step(
        w_query, query_g, m_query, v_query, rate_query, decay_rate
    )
    first_kv, second_kv, new_kv = adamw_step(w_kv, kv_g, m_kv, v_kv, rate_shared, decay_rate)
    first_out, second_out, new_out = adamw_step(
        w_out, out_g.T, m_out, v_out, rate_output, decay_rate
    )
    first_gate_up, second_gate_up, new_gate_up = adamw_step(
        w_gate_up, gate_up_g, m_gate_up, v_gate_up, rate_gate_up, decay_rate
    )
    first_down, second_down, new_down = adamw_step(
        w_down, ffn_g[2].T, m_down, v_down, rate_down, decay_rate
    )
    first_gains, second_gains, new_gains = adamw_step(
        norm_gains, gains_g, m_gains, v_gains, rate_gains, 0.0
    )
    return (
        layer_out,
        input_grad,
        first_query,
        second_query,
        new_query,
        first_kv,
        second_kv,
        new_kv,
        first_out,
        second_out,
        new_out,
        first_gate_up,
        second_gate_up,
        new_gate_up,
        first_down,
        second_down,
        new_down,
        first_gains,
        second_gains,
        new_gains,
    )


def solution(mesh):
    n_dp, n_tensor = mesh.shape["dp"], mesh.shape["tensor"]
    fine = Mesh(mesh.devices.reshape(n_dp // 2, 2, n_tensor), ("a", "c", "z"))
    dp, every = ("a", "c"), ("a", "c", "z")
    token = P(every, None)
    query = P(dp, "z")
    shared = P(None, every, None)
    output = P("z", dp)
    gate_up = P(None, dp, "z")
    gains = P(None, every)
    in_specs = (token, token, P(dp), query, shared, output, gate_up, output, gains)
    in_specs += (query, query, shared, shared, output, output, gate_up, gate_up)
    in_specs += (output, output, gains, gains)
    out_specs = (token, token) + (query,) * 3 + (shared,) * 3 + (output,) * 3
    out_specs += (gate_up,) * 3 + (output,) * 3 + (gains,) * 3
    return jax.shard_map(body, mesh=fine, in_specs=in_specs, out_specs=out_specs, check_vma=False)
```

```python
import functools

import jax
import jax.numpy as jnp
from jax import lax
from jax.experimental import pallas as pl
from jax.experimental.pallas import tpu as pltpu
from jax.sharding import Mesh, PartitionSpec as P

KV = 5
HD = 64
LEN = 1024
STEP = 10
RB = 256

beta_one = 0.9
beta_two = 0.95
adam_eps = 1e-08
decay_rate = 0.1
rate_query = 0.06
rate_shared = 0.06
rate_output = 0.8
rate_gate_up = 0.06
rate_down = 0.05
rate_gains = 0.6
norm_eps = 1e-05
neg_fill = -1e30

bf16 = jnp.bfloat16
f32 = jnp.float32
NN = (((1,), (0,)), ((), ()))
NT = (((1,), (1,)), ((), ()))
TN = (((0,), (0,)), ((), ()))
VMEM_LIMIT = 46 * 2**20
WIDE = 2 * KV * HD


def dot(a, b, dims=NN):
    return lax.dot_general(a, b, dims, preferred_element_type=f32)


def rms_scale(matrix):
    return lax.rsqrt(jnp.mean(matrix * matrix, axis=-1, keepdims=True) + norm_eps)


def norm_back(matrix, gain_row, upstream):
    scaling = rms_scale(matrix)
    unit_rows = matrix * scaling
    weighted = upstream * gain_row
    inner_mean = jnp.mean(weighted * unit_rows, axis=-1, keepdims=True)
    return (scaling * (weighted - unit_rows * inner_mean), jnp.sum(upstream * unit_rows, axis=0))


def adamw_step(weight, gradient, moment_one, moment_two, step_rate, decay_coef):
    moment_one = beta_one * moment_one + (1.0 - beta_one) * gradient
    moment_two = beta_two * moment_two + (1.0 - beta_two) * gradient * gradient
    unbiased_one = moment_one / (1.0 - beta_one**STEP)
    unbiased_two = moment_two / (1.0 - beta_two**STEP)
    updated = weight - step_rate * (
        unbiased_one / (jnp.sqrt(unbiased_two) + adam_eps) + decay_coef * weight
    )
    return (moment_one, moment_two, updated)


def columns_to_rows(columns):
    n = columns[0].shape[0]
    wide = jnp.concatenate(columns + [jnp.zeros((n, 128 - len(columns)), f32)], 1)
    return jnp.transpose(wide)[:8]


def params(flops, megabytes, transcendentals=0, weight=2.5, limit=VMEM_LIMIT):
    return dict(
        compiler_params=pltpu.CompilerParams(vmem_limit_bytes=limit),
        cost_estimate=pl.CostEstimate(
            flops=int(flops * weight), bytes_accessed=int(megabytes * weight * 1e6), transcendentals=transcendentals
        ),
    )


def attend_forward_kernel(info, q_ref, before_ref, own_ref, o_ref, lse_ref, *, rows):
    second, prefix = info[0], info[1]
    width = KV * HD

    def run(is_second):
        for block in range(rows // RB):
            base = (rows if is_second else 0) + block * RB
            row_slice = slice(block * RB, (block + 1) * RB)
            if is_second:
                spans = [(before_ref, 0, rows, None)]
                if block:
                    spans.append((own_ref, 0, block * RB, None))
                spans.append((own_ref, block * RB, RB, rows + block * RB))
            else:
                spans = [(own_ref, 0, rows, 0)]
            masks = []
            for _, _, count, masked in spans:
                if masked is None:
                    masks.append(None)
                else:
                    at = lax.broadcasted_iota(jnp.int32, (RB, count), 1) + masked
                    row = lax.broadcasted_iota(jnp.int32, (RB, count), 0) + base
                    masks.append((at <= row) | (at < prefix))
            outs, logs = [], []
            for c in range(KV):
                cols = slice(c * HD, (c + 1) * HD)
                values = slice(width + c * HD, width + (c + 1) * HD)
                query = q_ref[0, row_slice, cols]
                scores = []
                for (ref, start, count, _), mask in zip(spans, masks):
                    part = dot(query, ref[start : start + count, cols], NT)
                    scores.append(part if mask is None else jnp.where(mask, part, neg_fill))
                highest = functools.reduce(
                    jnp.maximum, [jnp.max(s, axis=1, keepdims=True) for s in scores]
                )
                total, mixed = 0.0, 0.0
                for (ref, start, count, _), part in zip(spans, scores):
                    expo = jnp.exp(part - highest)
                    total = total + jnp.sum(expo, axis=1, keepdims=True)
                    mixed = mixed + dot(expo.astype(bf16), ref[start : start + count, values])
                outs.append((mixed / total).astype(bf16))
                logs.append(highest + jnp.log(total))
            o_ref[0, row_slice, :] = jnp.concatenate(outs, 1)
            lse_ref[0, :, row_slice] = columns_to_rows(logs)

    pl.when(second == 0)(lambda: run(False))
    pl.when(second == 1)(lambda: run(True))


def attend_forward(info, queries, before, own):
    groups, rows, width = queries.shape
    block = pl.BlockSpec((1, rows, width), lambda r, _: (r, 0, 0))
    whole = pl.BlockSpec(own.shape, lambda r, _: (0, 0))
    elements = groups * rows * KV * 2 * rows
    return pl.pallas_call(
        functools.partial(attend_forward_kernel, rows=rows),
        grid_spec=pltpu.PrefetchScalarGridSpec(
            num_scalar_prefetch=1,
            grid=(groups,),
            in_specs=[block, whole, whole],
            out_specs=[block, pl.BlockSpec((1, 8, rows), lambda r, _: (r, 0, 0))],
        ),
        out_shape=[
            jax.ShapeDtypeStruct(queries.shape, bf16),
            jax.ShapeDtypeStruct((groups, 8, rows), f32),
        ],
        name="attend_forward",
        **params(elements * 900, 4, elements, limit=20 * 2**20),
    )(info, queries, before, own)


def attend_backward_kernel(
    info, q_ref, before_ref, own_ref, do_ref, lse_ref, delta_ref, dq_ref, first_ref, last_ref, dk_acc, dv_acc, *, rows
):
    second, prefix = info[0], info[1]
    group = pl.program_id(0)
    width = KV * HD

    @pl.when(group == 0)
    def _():
        dk_acc[...] = jnp.zeros_like(dk_acc)
        dv_acc[...] = jnp.zeros_like(dv_acc)

    def run(is_second):
        for block in range(rows // RB):
            base = (rows if is_second else 0) + block * RB
            row_slice = slice(block * RB, (block + 1) * RB)
            steps = rows // RB
            if is_second:
                spans = [(before_ref, i * RB, i * RB, False) for i in range(steps)]
                spans += [(own_ref, i * RB, rows + i * RB, i == block) for i in range(block + 1)]
            else:
                spans = [(own_ref, i * RB, i * RB, True) for i in range(steps)]
            query_grads = []
            for c in range(KV):
                cols = slice(c * HD, (c + 1) * HD)
                values = slice(width + c * HD, width + (c + 1) * HD)
                query, out_grad = q_ref[0, row_slice, cols], do_ref[0, row_slice, cols]
                log_sum = lse_ref[0, c : c + 1, row_slice]
                delta = delta_ref[0, c : c + 1, row_slice]
                query_grad = jnp.zeros((RB, HD), f32)
                for ref, start, position, masked in spans:
                    key, value = ref[start : start + RB, cols], ref[start : start + RB, values]
                    scores = dot(key, query, NT) - log_sum
                    if masked:
                        at = lax.broadcasted_iota(jnp.int32, (RB, RB), 0) + position
                        row = lax.broadcasted_iota(jnp.int32, (RB, RB), 1) + base
                        scores = jnp.where((at <= row) | (at < prefix), scores, neg_fill)
                    probs = jnp.exp(scores)
                    probs_grad = dot(value, out_grad, NT)
                    score_grad = (probs * (probs_grad - delta)).astype(bf16)
                    at_keys = slice(position, position + RB)
                    dv_acc[c, at_keys, :] += dot(probs.astype(bf16), out_grad)
                    dk_acc[c, at_keys, :] += dot(score_grad, query)
                    query_grad = query_grad + dot(score_grad, key, TN)
                query_grads.append((query_grad * HD**-0.5).astype(bf16))
            dq_ref[0, row_slice, :] = jnp.concatenate(query_grads, 1)

    pl.when(second == 0)(lambda: run(False))
    pl.when(second == 1)(lambda: run(True))

    @pl.when(group == pl.num_programs(0) - 1)
    def _():
        for ref, part in ((first_ref, slice(0, rows)), (last_ref, slice(rows, 2 * rows))):
            ref[...] = jnp.concatenate(
                [acc[c, part, :] for acc in (dk_acc, dv_acc) for c in range(KV)], 1
            )


def attend_backward(info, queries, before, own, out_grad, log_sums, delta):
    groups, rows, width = queries.shape
    block = pl.BlockSpec((1, rows, width), lambda r, _: (r, 0, 0))
    whole = pl.BlockSpec(own.shape, lambda r, _: (0, 0))
    stats = pl.BlockSpec((1, 8, rows), lambda r, _: (r, 0, 0))
    elements = groups * rows * KV * 2 * rows
    return pl.pallas_call(
        functools.partial(attend_backward_kernel, rows=rows),
        grid_spec=pltpu.PrefetchScalarGridSpec(
            num_scalar_prefetch=1,
            grid=(groups,),
            in_specs=[block, whole, whole, block, stats, stats],
            out_specs=[block, whole, whole],
            scratch_shapes=[pltpu.VMEM((KV, 2 * rows, HD), f32)] * 2,
        ),
        out_shape=[jax.ShapeDtypeStruct(queries.shape, bf16)]
        + [jax.ShapeDtypeStruct(own.shape, f32)] * 2,
        name="attend_backward",
        **params(elements * 2500, 8, elements, limit=20 * 2**20),
    )(info, queries, before, own, out_grad, log_sums, delta)


BLOCKS = 4
SWAPPED = (0, 2, 1, 3)


def block_row(info, j, other):
    return (((info[2] ^ j) * 2) + (info[3] ^ other)) * 160


def pair_of(ref):
    return jnp.concatenate([ref[0], ref[1]], 1)


def put_together(info, refs, w_ref):
    width = KV * HD
    for i, ref in enumerate(refs):
        part, other = i // 2, i % 2
        for j in range(BLOCKS):
            at = block_row(info, SWAPPED[j] if part else j, other) + part * 80
            block = ref[j]
            w_ref[pl.ds(pl.multiple_of(at, 16), 80), :] = jnp.concatenate(
                [block[:80, :width], block[80:, :width]], 1
            )


def shared_kernel(info, tok_ref, ka, kb, va, vb, normed_ref, kv_ref, gain_ref, wkv_ref, gains):
    width = KV * HD
    for other, (k_ref, v_ref) in enumerate(((ka, va), (kb, vb))):
        for j in range(BLOCKS):
            at = pl.ds(pl.multiple_of(block_row(info, j, other), 160), 160)
            wkv_ref[at, :width] = k_ref[j][:, :width]
            gains[0, at, :] = k_ref[j][:, 256:].astype(f32)
            at = pl.ds(pl.multiple_of(block_row(info, SWAPPED[j], other), 160), 160)
            wkv_ref[at, width:] = v_ref[j][:, :width]
            gains[1, at, :] = v_ref[j][:, 256:].astype(f32)
    one = jnp.transpose(gains[0])[64:72]
    two = jnp.transpose(gains[1])[64:72]
    gain_ref[...] = jnp.concatenate([one[:1], two[:1], jnp.zeros((6, one.shape[1]), f32)], 0)
    tok = tok_ref[...].astype(f32)
    normed = (tok * rms_scale(tok) * one[:1]).astype(bf16)
    normed_ref[...] = normed
    kv_ref[...] = dot(normed, wkv_ref[...]).astype(bf16)


def project_shared(info, tokens, parts):
    rows, depth = tokens.shape
    width = 2 * KV * HD
    whole = lambda *shape: pl.BlockSpec(shape, lambda i, _: (0,) * len(shape))
    block = pl.BlockSpec((BLOCKS, 160, 384), lambda i, _: (0, 4, 0))
    return pl.pallas_call(
        shared_kernel,
        grid_spec=pltpu.PrefetchScalarGridSpec(
            num_scalar_prefetch=1,
            grid=(1,),
            in_specs=[whole(rows, depth)] + [block] * 4,
            out_specs=[
                whole(rows, depth),
                whole(rows, width),
                whole(8, depth),
                whole(depth, width),
            ],
            scratch_shapes=[pltpu.VMEM((2, depth, 128), f32)],
        ),
        out_shape=[
            jax.ShapeDtypeStruct((rows, depth), bf16),
            jax.ShapeDtypeStruct((rows, width), bf16),
            jax.ShapeDtypeStruct((8, depth), f32),
            jax.ShapeDtypeStruct((depth, width), bf16),
        ],
        name="project_shared",
        **params(2 * rows * depth * width, 8),
    )(info, tokens, *parts)


def query_kernel(info, x_ref, a0, b0, a1, b1, c0, d0, c1, d1, q_ref, w_ref, wo_ref, t_ref):
    @pl.when(pl.program_id(0) == 0)
    def _():
        t_ref[...] = jnp.transpose(x_ref[...])

    put_together(info, (a0, b0, a1, b1), w_ref)
    put_together(info, (c0, d0, c1, d1), wo_ref)
    result = (dot(x_ref[...], w_ref[...]).astype(bf16) * HD**-0.5).astype(bf16)
    q_ref[0] = result[:, : KV * HD]
    q_ref[1] = result[:, KV * HD :]


def project_queries(info, normed, parts):
    rows, depth = normed.shape
    query = pl.BlockSpec((BLOCKS, 160, 384), lambda r, _: (0, r, 0))
    output = pl.BlockSpec((BLOCKS, 160, 384), lambda r, _: (0, 2 + r, 0))
    weights = pl.BlockSpec((depth, WIDE), lambda r, _: (0, r))
    return pl.pallas_call(
        query_kernel,
        grid_spec=pltpu.PrefetchScalarGridSpec(
            num_scalar_prefetch=1,
            grid=(2,),
            in_specs=[pl.BlockSpec((rows, depth), lambda r, _: (0, 0))] + [query] * 4 + [output] * 4,
            out_specs=[
                pl.BlockSpec((2, rows, WIDE // 2), lambda r, _: (r, 0, 0)),
                weights,
                weights,
                pl.BlockSpec((depth, rows), lambda r, _: (0, 0)),
            ],
        ),
        out_shape=[jax.ShapeDtypeStruct((4, rows, WIDE // 2), bf16)]
        + [jax.ShapeDtypeStruct((depth, 2 * WIDE), bf16)] * 2
        + [jax.ShapeDtypeStruct((depth, rows), bf16)],
        name="project_queries",
        **params(4 * rows * depth * WIDE, 14),
    )(info, normed, *parts, *parts)


def output_kernel(att_ref, w_ref, tok_ref, gain_ref, middle_ref, normed_ref, acc):
    part = dot(pair_of(att_ref), w_ref[...], NT)

    @pl.when(pl.program_id(0) == 0)
    def _():
        acc[...] = tok_ref[...].astype(f32) + part

    @pl.when(pl.program_id(0) == 1)
    def _():
        middle = acc[...] + part
        middle_ref[...] = middle
        normed_ref[...] = (middle * rms_scale(middle) * gain_ref[1:2]).astype(bf16)


def project_output(attended, w_out, tokens, gains):
    rows, depth = tokens.shape
    whole = lambda *shape: pl.BlockSpec(shape, lambda r: (0,) * len(shape))
    return pl.pallas_call(
        output_kernel,
        grid=(2,),
        in_specs=[
            pl.BlockSpec((2, rows, WIDE // 2), lambda r: (r, 0, 0)),
            pl.BlockSpec((depth, WIDE), lambda r: (0, r)),
            whole(rows, depth),
            whole(8, depth),
        ],
        out_specs=[whole(rows, depth)] * 2,
        out_shape=[
            jax.ShapeDtypeStruct((rows, depth), f32),
            jax.ShapeDtypeStruct((rows, depth), bf16),
        ],
        scratch_shapes=[pltpu.VMEM((rows, depth), f32)],
        name="project_output",
        **params(4 * rows * depth * WIDE, 12),
    )(attended, w_out, tokens, gains)


def feed_forward_kernel(xa, xb, ca, cb, w_ref, inner_ref, out_a, out_b, back_a, back_b):
    def run(x_ref, c_ref, out_ref, back_ref):
        x, cot = x_ref[...], c_ref[...]
        gate = dot(x, w_ref[0])
        up = dot(x, w_ref[1])
        hidden_grad = dot(cot, w_ref[2])
        sig = jax.nn.sigmoid(gate)
        silu = gate * sig
        hidden = (silu * up).astype(bf16)
        inner_ref[2] = hidden
        gate_grad = (hidden_grad * up * sig * (1.0 + gate * (1.0 - sig))).astype(bf16)
        inner_ref[0] = gate_grad
        up_grad = (hidden_grad * silu).astype(bf16)
        inner_ref[1] = up_grad
        out_ref[...] = dot(hidden, w_ref[2], NT).astype(bf16)
        back_ref[...] = (dot(gate_grad, w_ref[0], NT) + dot(up_grad, w_ref[1], NT)).astype(bf16)

    pl.when(pl.program_id(0) < pl.num_programs(0) // 2)(lambda: run(xa, ca, out_a, back_a))
    pl.when(pl.program_id(0) >= pl.num_programs(0) // 2)(lambda: run(xb, cb, out_b, back_b))


def feed_forward(normed, cots, weights):
    rows, depth = normed[0].shape
    width = weights.shape[2]
    tile = 256
    steps = rows // tile
    first = pl.BlockSpec((tile, depth), lambda i: (jnp.minimum(i, steps - 1), 0))
    last = pl.BlockSpec((tile, depth), lambda i: (jnp.maximum(i - steps, 0), 0))
    inner = pl.BlockSpec((3, tile, width), lambda i: (0, i, 0))
    whole = pl.BlockSpec(weights.shape, lambda i: (0, 0, 0), pipeline_mode=pl.Buffered(1))
    return pl.pallas_call(
        feed_forward_kernel,
        grid=(2 * steps,),
        in_specs=[first, last, first, last, whole],
        out_specs=[inner, first, last, first, last],
        out_shape=[jax.ShapeDtypeStruct((3, 2 * rows, width), bf16)]
        + [jax.ShapeDtypeStruct((rows, depth), bf16)] * 4,
        name="feed_forward",
        **params(24 * rows * depth * width, 24),
    )(*normed, *cots, weights)


def hidden_grad_kernel(x0, x1, x2, x3, c0, c1, c2, c3, near_ref, far_ref, out_ref):
    def run(lefts):
        rows = lefts[0].shape[0]
        total = 0.0
        for left, (right, at) in zip(lefts, ((near_ref, 0), (near_ref, 1), (far_ref, 0), (far_ref, 1))):
            total = total + dot(left[...], right[0, at * rows : (at + 1) * rows, :], TN)
        out_ref[0] = total.astype(bf16)

    pl.when(pl.program_id(0) < 2)(lambda: run((x0, x1, x2, x3)))
    pl.when(pl.program_id(0) == 2)(lambda: run((c0, c1, c2, c3)))


def hidden_grads(normed, cots, near, far):
    rows, depth = normed[0].shape
    width = near.shape[2]
    tile = 640
    last = depth // tile - 1
    left = pl.BlockSpec((rows, tile), lambda m, i: (0, jnp.where(m < 2, i, last)))
    cot = pl.BlockSpec((rows, tile), lambda m, i: (0, jnp.where(m < 2, 0, i)))
    right = pl.BlockSpec((1, 2 * rows, width), lambda m, i: (m, 0, 0))
    return pl.pallas_call(
        hidden_grad_kernel,
        grid=(3, depth // tile),
        in_specs=[left] * 4 + [cot] * 4 + [right] * 2,
        out_specs=pl.BlockSpec((1, tile, width), lambda m, i: (m, i, 0)),
        out_shape=jax.ShapeDtypeStruct((3, depth, width), bf16),
        name="hidden_grads",
        **params(24 * rows * depth * width, 28),
    )(*normed, *cots, near, far)


def middle_kernel(
    middle_ref, cot_ref, gain_ref, near_ref, core_ref, far_ref, w_ref, att_ref,
    grad_ref, low_t_ref, gain_grad_ref, do_ref, delta_ref, low,
):
    @pl.when(pl.program_id(0) == 0)
    def _():
        upstream = near_ref[...].astype(f32) + core_ref[...].astype(f32) + far_ref[...].astype(f32)
        middle = middle_ref[...]
        scaling = rms_scale(middle)
        unit_rows = middle * scaling
        gain_grad = jnp.sum(upstream * unit_rows, axis=0, keepdims=True)
        gain_grad_ref[...] = jnp.broadcast_to(gain_grad, gain_grad_ref.shape)
        weighted = upstream * gain_ref[1:2]
        inner_mean = jnp.mean(weighted * unit_rows, axis=-1, keepdims=True)
        grad = cot_ref[...].astype(f32) + scaling * (weighted - unit_rows * inner_mean)
        grad_ref[...] = grad
        low[...] = grad.astype(bf16)
        low_t_ref[...] = jnp.transpose(low[...])

    grad = dot(low[...], w_ref[...]).astype(bf16)
    do_ref[0] = grad[:, : WIDE // 2]
    do_ref[1] = grad[:, WIDE // 2 :]
    product = grad.astype(f32) * pair_of(att_ref).astype(f32)
    high = product.astype(bf16)
    rest = (product - high.astype(f32)).astype(bf16)
    row = lax.broadcasted_iota(jnp.int32, (16, WIDE), 0)
    head = jnp.where(row < 8, jnp.where(row < KV, row, -1), jnp.where(row < 8 + KV, row - 8 + KV, -1))
    column = lax.broadcasted_iota(jnp.int32, (16, WIDE), 1)
    member = ((column >= head * HD) & (column < (head + 1) * HD)).astype(f32).astype(bf16)
    delta = dot(member, high, NT) + dot(member, rest, NT)
    delta_ref[0] = delta[:8]
    delta_ref[1] = delta[8:]


def middle_backward(middle, cot, gains, near, core, far, w_out, attended):
    rows, depth = middle.shape
    block = pl.BlockSpec((2, rows, WIDE // 2), lambda r: (r, 0, 0))
    whole = lambda *shape: pl.BlockSpec(shape, lambda r: (0,) * len(shape))
    token = whole(rows, depth)
    return pl.pallas_call(
        middle_kernel,
        grid=(2,),
        in_specs=[token, token, whole(8, depth), token, token, token]
        + [pl.BlockSpec((depth, WIDE), lambda r: (0, r)), block],
        out_specs=[
            token,
            whole(depth, rows),
            whole(8, depth),
            block,
            pl.BlockSpec((2, 8, rows), lambda r: (r, 0, 0)),
        ],
        out_shape=[
            jax.ShapeDtypeStruct((rows, depth), f32),
            jax.ShapeDtypeStruct((depth, rows), bf16),
            jax.ShapeDtypeStruct((8, depth), f32),
            jax.ShapeDtypeStruct((4, rows, WIDE // 2), bf16),
            jax.ShapeDtypeStruct((4, 8, rows), f32),
        ],
        scratch_shapes=[pltpu.VMEM((rows, depth), bf16)],
        name="middle_backward",
        **params(4 * rows * depth * WIDE, 20),
    )(middle, cot, gains, near, core, far, w_out, attended)


def input_kernel(
    dq_ref, wq_ref, dkv_ref, wkv_ref, tok_ref, gain_ref, grad_ref, two_ref, out_ref, gain_grad_ref, acc
):
    group = pl.program_id(0)

    @pl.when(group == 0)
    def _():
        acc[...] = dot(dkv_ref[...], wkv_ref[...], NT)

    acc[...] += dot(pair_of(dq_ref), wq_ref[...], NT)

    @pl.when(group == pl.num_programs(0) - 1)
    def _():
        upstream = acc[...]
        tok = tok_ref[...].astype(f32)
        scaling = rms_scale(tok)
        unit_rows = tok * scaling
        one = jnp.sum(upstream * unit_rows, axis=0, keepdims=True)
        gain_grad_ref[...] = jnp.concatenate([one, two_ref[:7]], 0)
        weighted = upstream * gain_ref[0:1]
        inner_mean = jnp.mean(weighted * unit_rows, axis=-1, keepdims=True)
        out_ref[...] = grad_ref[...] + scaling * (weighted - unit_rows * inner_mean)


def input_backward(dq, wq, dkv, wkv, tokens, gains, middle_grad, gain_two):
    rows, depth = tokens.shape
    whole = lambda *shape: pl.BlockSpec(shape, lambda r: (0,) * len(shape))
    token = whole(rows, depth)
    return pl.pallas_call(
        input_kernel,
        grid=(2,),
        in_specs=[
            pl.BlockSpec((2, rows, WIDE // 2), lambda r: (r, 0, 0)),
            pl.BlockSpec((depth, WIDE), lambda r: (0, r)),
            whole(*dkv.shape),
            whole(*wkv.shape),
            token,
            whole(8, depth),
            token,
            whole(8, depth),
        ],
        out_specs=[token, whole(8, depth)],
        out_shape=[
            jax.ShapeDtypeStruct((rows, depth), f32),
            jax.ShapeDtypeStruct((8, depth), f32),
        ],
        scratch_shapes=[pltpu.VMEM((rows, depth), f32)],
        name="input_backward",
        **params(6 * rows * depth * WIDE, 20),
    )(dq, wq, dkv, wkv, tokens, gains, middle_grad, gain_two)


def group_grad_kernel(info, left_a, right_a, left_b, right_b, own_ref, other_ref, whole):
    @pl.when(pl.program_id(1) == 0)
    def _():
        whole[...] = dot(left_a[...], pair_of(right_a)).astype(bf16)

    @pl.when(pl.program_id(1) == 1)
    def _():
        whole[...] = dot(left_b[...], pair_of(right_b)).astype(bf16)

    for other, ref in enumerate((own_ref, other_ref)):
        for j in range(BLOCKS):
            ref[j, 0] = whole[pl.ds(pl.multiple_of(block_row(info, j, other), 160), 160), :]


def group_grads(info, left_a, right_a, left_b, right_b):
    groups, rows, width = right_a.shape
    depth = left_a.shape[0]
    left = pl.BlockSpec((depth, rows), lambda r, w, _: (0, 0))
    right = pl.BlockSpec((2, rows, width), lambda r, w, info: (r ^ (info[4] >> 1), 0, 0))
    block = pl.BlockSpec((BLOCKS, 1, 160, WIDE), lambda r, w, _: (0, 2 * r + w, 0, 0))
    return pl.pallas_call(
        group_grad_kernel,
        grid_spec=pltpu.PrefetchScalarGridSpec(
            num_scalar_prefetch=1,
            grid=(2, 2),
            in_specs=[left, right] * 2,
            out_specs=[block] * 2,
            scratch_shapes=[pltpu.VMEM((depth, WIDE), bf16)],
        ),
        out_shape=[jax.ShapeDtypeStruct((BLOCKS, groups, 160, WIDE), bf16)] * 2,
        name="group_grads",
        **params(8 * rows * depth * WIDE, 12),
    )(info, left_a, right_a, left_b, right_b)


def shared_grad_kernel(info, left_ref, right_ref, gain_ref, own_ref, other_ref, whole):
    wide = jnp.concatenate([gain_ref[...], jnp.zeros((120, gain_ref.shape[1]), f32)], 0)
    width = right_ref.shape[1]
    whole[:, width:] = jnp.transpose(wide).astype(bf16)
    whole[:, :width] = dot(left_ref[...], right_ref[...]).astype(bf16)
    for other, ref in enumerate((own_ref, other_ref)):
        for j in range(BLOCKS):
            at = pl.ds(pl.multiple_of(block_row(info, j, other), 160), 160)
            ref[j] = whole[at, :]


def shared_grads(info, left, right, gain_grads):
    rows, width = right.shape
    depth = left.shape[0]
    whole = lambda *shape: pl.BlockSpec(shape, lambda i, _: (0,) * len(shape))
    return pl.pallas_call(
        shared_grad_kernel,
        grid_spec=pltpu.PrefetchScalarGridSpec(
            num_scalar_prefetch=1,
            grid=(1,),
            in_specs=[whole(depth, rows), whole(rows, width), whole(8, depth)],
            out_specs=[whole(BLOCKS, 160, width + 128)] * 2,
            scratch_shapes=[pltpu.VMEM((depth, width + 128), bf16)],
        ),
        out_shape=[jax.ShapeDtypeStruct((BLOCKS, 160, width + 128), bf16)] * 2,
        name="shared_grads",
        **params(2 * rows * depth * width, 6),
    )(info, left, right, gain_grads)


def swap(value, axis, bit):
    size = lax.axis_size(axis)
    return lax.ppermute(value, axis, [(i, i ^ bit) for i in range(size)])


def core_swap(value):
    return swap(value, "c", 1)


def placed(own, other, bit, axis=0):
    return jnp.concatenate(
        [jnp.where(bit == 0, own, other), jnp.where(bit == 0, other, own)], axis
    )


def gather_line(own, z):
    pair = placed(own, swap(own, "z", 2), z // 2)
    size = own.shape[0]
    near = swap(pair, "z", 1)
    both = [jnp.where(z % 2 == 0, pair, near), jnp.where(z % 2 == 0, near, pair)]
    return jnp.concatenate(
        [part[i * size : (i + 1) * size] for i in range(2) for part in both], 0
    )


def gather_plane(blocks, bit):
    return jnp.concatenate([blocks, swap(blocks, "a", bit)], 0)


def add(one, two, kind=bf16):
    return (one.astype(f32) + two.astype(f32)).astype(kind)


def reduce_core(parts):
    own, other = parts
    return add(own, core_swap(other))


def reduce_plane(blocks, bits):
    if bits[0] == 1:
        blocks = blocks.reshape((2, 2) + blocks.shape[1:])
        blocks = add(blocks[:, 0], swap(blocks[:, 1], "a", 1))
    else:
        blocks = add(blocks[:2], swap(blocks[2:], "a", 2))
    return add(blocks[0], swap(blocks[1], "a", bits[1]))


def pick(stacked, index, axis=0):
    return lax.dynamic_index_in_dim(stacked, index, axis, keepdims=False)


def after(value, *earlier):
    return lax.optimization_barrier((value,) + earlier)[0]


def head_weights(w_query, w_kv, w_out, norm_gains, z, beside):
    w_rows, group_width = w_query.shape
    kv_rows = w_kv.shape[1]
    n_a, n_z = lax.axis_size("a"), lax.axis_size("z")
    pad = lambda m: jnp.pad(m.astype(bf16), ((0, 0), (0, 384 - m.shape[1])))
    shared = [pad(jnp.concatenate([w_kv[i], norm_gains[i][:, None]], 1)) for i in range(2)]
    query, output = pad(w_query), pad(w_out.T)
    if n_a == BLOCKS:
        half = w_rows // 2
        line = gather_line(jnp.concatenate([query, output] + shared, 0)[None], z)
        moved = beside(line)
        packs = []
        for i, bits in enumerate(((1, 2), (2, 1))):
            starts = (i * half, w_rows + i * half, 2 * w_rows + i * kv_rows)
            counts = (half, half, kv_rows)
            own = [line[:, s : s + n].reshape(n_z * n, 384) for s, n in zip(starts, counts)]
            blocks = gather_plane(jnp.concatenate(own, 0)[None], bits[0])
            packs.append((blocks, swap(blocks, "a", bits[1])))
        return packs, moved
    every = ("a", "c", "z")

    def groups(own):
        got = lax.all_gather(own, every, axis=0).reshape(2 * n_a, n_z, w_rows, 384)
        return jnp.transpose(got, (1, 0, 2, 3)).reshape(n_z, BLOCKS, 2, 160, 384)

    query, output = groups(query), groups(output)
    result = []
    for i in range(2):
        kv = lax.all_gather(shared[i], every, axis=0).reshape(BLOCKS, 2, 160, 384)
        halves = [
            jnp.transpose(m[:, :, :, i * 80 : (i + 1) * 80], (1, 2, 0, 3, 4)).reshape(
                BLOCKS, 2, n_z * 80, 384
            )
            for m in (query, output)
        ]
        part = jnp.concatenate(halves + [kv], 2)
        if i:
            part = part[jnp.array(SWAPPED)]
        result += [part[:, 0], part[:, 1]]
    return result, beside(query)


def body(
    tokens,
    cotangent,
    prefix_len,
    w_query,
    w_kv,
    w_out,
    w_gate_up,
    w_down,
    norm_gains,
    m_query,
    v_query,
    m_kv,
    v_kv,
    m_out,
    v_out,
    m_gate_up,
    v_gate_up,
    m_down,
    v_down,
    m_gains,
    v_gains,
):
    rows, width = tokens.shape
    a, c, z = lax.axis_index("a"), lax.axis_index("c"), lax.axis_index("z")
    n_a, n_z = lax.axis_size("a"), lax.axis_size("z")
    plane = n_a == BLOCKS
    w_rows, group_width = w_query.shape
    kv_rows = w_kv.shape[1]
    hidden_width = w_gate_up.shape[2]
    second = (z % (LEN // rows)) == 1
    seq_at = z // (LEN // rows)
    at = [a, c, z] if plane else [0, 0, 0]
    info = jnp.stack([second, pick(prefix_len, seq_at)] + at).astype(jnp.int32)

    ffn_own = jnp.concatenate([w_gate_up, w_down.T[None]], 0).astype(bf16)
    cross = [(n_z + zz, zz) for zz in range(n_z)] + [(zz, n_z + (zz ^ 2)) for zz in range(n_z)]
    far_core = [(n_z + zz, n_z + (zz ^ 2)) for zz in range(n_z)]

    def cross_line(line):
        block = after(ffn_own, line)
        return lax.ppermute(block, ("c", "z"), cross), lax.ppermute(block, ("c", "z"), far_core)

    parts, moved = head_weights(w_query, w_kv, w_out, norm_gains, z, cross_line)
    crossed, shifted = moved
    ffn_blocks = jnp.concatenate(
        [jnp.where(c == 0, ffn_own, crossed), jnp.where(c == 0, crossed, shifted)], 1
    )
    if plane:
        ffn_blocks = after(ffn_blocks, *(received for _, received in parts))
        first, last = (jnp.concatenate(pair, 0) for pair in parts)
        parts = first, core_swap(first), last, core_swap(last)
    ffn_w = lax.all_gather(ffn_blocks, "a", axis=1, tiled=True)

    normed_one, kv_own, gains, w_shared = project_shared(info, tokens, parts)
    before = lax.ppermute(kv_own, "z", [(i, i + 1) for i in range(0, n_z, 2)])
    queries, w_groups, out_groups, normed_one_t = project_queries(info, normed_one, parts)
    before = after(before, queries)
    cot_core = core_swap(after(cotangent, before))
    cot_pair = swap(after(cotangent, crossed, shifted), "z", 1)
    attended, log_sums = attend_forward(info, queries, before, kv_own)
    cot_pair = after(cot_pair, attended)
    cots = cotangent, cot_core, cot_pair, core_swap(cot_pair)
    middle, normed_two = project_output(attended, out_groups, after(tokens, cots[3]), gains)

    two_core, two_pair = core_swap(normed_two), swap(normed_two, "z", 1)
    inner_near, out_own, out_core, back_own, back_core = feed_forward(
        (normed_two, two_core), cots[:2], ffn_w
    )
    back_core = core_swap(back_core)
    two_pair = after(two_pair, inner_near)
    twos = (normed_two, two_core, two_pair, core_swap(two_pair))
    inner_far, out_far, out_far_core, back_far, back_far_core = feed_forward(
        twos[2:], cots[2:], ffn_w
    )
    back_sum = add(back_far, core_swap(back_far_core))
    back_pair = swap(back_sum, "z", 1)
    ffn_grad = hidden_grads(twos, cots, inner_near, after(inner_far, back_sum, back_core))
    out_sum = add(out_far, core_swap(out_far_core))
    ffn_sum = lax.psum_scatter(
        after(ffn_grad, back_pair, out_sum), "a", scatter_dimension=1, tiled=True
    )

    middle_grad, middle_low_t, gain_two_grad, attended_grad, delta = middle_backward(
        middle, cotangent, gains, back_own, back_core, after(back_pair, ffn_grad), out_groups, attended
    )
    out_pair = swap(after(out_sum, attended_grad), "z", 1)
    out_core = core_swap(out_core)
    dq, first_grad, last_grad = attend_backward(
        info, queries, before, kv_own, attended_grad, log_sums, delta
    )
    to_before = first_grad.astype(bf16)
    dq = after(dq, out_core, out_pair, to_before)
    from_after = lax.ppermute(to_before, "z", [(i + 1, i) for i in range(0, n_z, 2)])
    parts = group_grads(info, normed_one_t, dq, middle_low_t, attended)
    if plane:
        parts = parts[0], core_swap(parts[1])
        first = [m[:, :2].reshape((2, 2, 2) + m.shape[2:]) for m in parts]
        last = [m[:, 2:] for m in parts]
        first_send = add(first[0][:, 1], first[1][:, 1])
        last_send = add(last[0][2:], last[1][2:])
        from_after = after(from_after, first_send, last_send, ffn_sum)
        first_recv, last_recv = swap(first_send, "a", 1), swap(last_send, "a", 2)
    dkv = jnp.where(second, last_grad, first_grad + from_after.astype(f32)).astype(bf16)
    input_grad, gain_grads = input_backward(
        dq, w_groups, dkv, w_shared, tokens, gains, middle_grad, gain_two_grad
    )
    ffn_sum = ffn_sum.reshape(3, 2, w_rows, hidden_width)
    crossed = [
        lax.ppermute(jnp.where(c == 0, m[1], m[0]), ("c", "z"), [(d, s) for s, d in cross])
        for m in ffn_sum
    ]
    shifted = [lax.ppermute(m[1], ("c", "z"), far_core) for m in ffn_sum]
    shared_parts = shared_grads(info, normed_one_t, dkv, after(gain_grads, crossed[0]))

    if plane:
        shared_own, shared_other = shared_parts
        shared_recv = core_swap(shared_other)
        first_recv = after(first_recv, shared_other, shifted[0], crossed[1])
        last_recv = after(last_recv, shared_other)
        first = add(add(first[0][:, 0], first[1][:, 0], f32), first_recv)
        last = add(add(last[0][:2], last[1][:2], f32), last_recv)
        first_recv, last_recv = swap(first[1], "a", 2), swap(last[1], "a", 1)
        shared_sum = add(shared_own, after(shared_recv, first, last))
        keys, values = shared_sum[..., :group_width], shared_sum[..., group_width:]
        keys = keys.reshape((2, 2) + keys.shape[1:])
        keys, keys_send, values, values_send = keys[:, 0], keys[:, 1], values[:2], values[2:]
        keys_recv, values_recv = swap(keys_send, "a", 1), swap(values_send, "a", 2)
        first_recv, last_recv = (
            after(r, keys_send, values_send, shifted[1], crossed[2]) for r in (first_recv, last_recv)
        )
        both = jnp.stack([add(first[0], first_recv), add(last[0], last_recv)])
        halves = both[..., :group_width], both[..., group_width:]
        both_send = after(jnp.where(z % 2 == 0, halves[1], halves[0]), shifted[2])
        both = jnp.where(z % 2 == 0, halves[0], halves[1])
        both_recv = swap(both_send, "z", 1)
        keys = add(keys, after(keys_recv, both_send))
        values = add(values, after(values_recv, both_send))
        keys_recv, values_recv = swap(keys[1], "a", 2), swap(values[1], "a", 1)
        both = add(both, both_recv)
        both_recv = swap(both[1], "z", 2)
        shared_sum = jnp.concatenate(
            [
                add(keys[0], after(keys_recv, both)),
                add(values[0], after(values_recv, both)),
            ],
            1,
        )
        quarters = shared_sum.reshape(2, 2, kv_rows, -1)
        kept = add(pick(quarters, z % 2, 1), swap(pick(quarters, 1 - z % 2, 1), "z", 1))
        both = add(both[0], both_recv, f32)
        kept = after(kept, both)
        shared_g = add(pick(kept, z // 2), swap(pick(kept, 1 - z // 2), "z", 2), f32)
        query_g, out_g = both[0], both[1]
    else:

        def whole_sum(blocks):
            blocks = jnp.stack(blocks, 1)
            blocks = jnp.moveaxis(blocks, 2, 0) if blocks.ndim == 5 else blocks[None]
            blocks = blocks.reshape(blocks.shape[0], width, blocks.shape[-1])
            mine = lax.psum_scatter(blocks, ("a", "c"), scatter_dimension=1, tiled=True)
            return mine.astype(f32)

        query_g, out_g = (
            lax.psum_scatter(
                whole_sum(
                    [
                        jnp.stack(
                            [
                                m[:, 2 * r + i, :, k * group_width : (k + 1) * group_width]
                                for r in range(2)
                                for k in range(2)
                            ],
                            1,
                        )
                        for m in parts
                    ]
                ),
                "z",
                scatter_dimension=0,
            )
            for i in range(2)
        )
        shared_g = lax.psum_scatter(
            whole_sum(shared_parts)[0], "z", scatter_dimension=0, tiled=True
        )
    ffn_g = [
        add(got, jnp.where(c == 0, m[0], moved), f32)
        for m, got, moved in zip(ffn_sum, crossed, shifted)
    ]
    gate_up_g = jnp.stack(ffn_g[:2])
    kv_g = jnp.stack([shared_g[:, :group_width], shared_g[:, group_width : 2 * group_width]])
    gains_g = shared_g[:, 2 * group_width : 2 * group_width + 2].T

    layer_out = (middle + add(add(out_own, out_core, f32), after(out_pair, shared_parts[0]), f32)).astype(bf16)

    first_query, second_query, new_query = adamw_step(
        w_query, query_g, m_query, v_query, rate_query, decay_rate
    )
    first_kv, second_kv, new_kv = adamw_step(w_kv, kv_g, m_kv, v_kv, rate_shared, decay_rate)
    first_out, second_out, new_out = adamw_step(
        w_out, out_g.T, m_out, v_out, rate_output, decay_rate
    )
    first_gate_up, second_gate_up, new_gate_up = adamw_step(
        w_gate_up, gate_up_g, m_gate_up, v_gate_up, rate_gate_up, decay_rate
    )
    first_down, second_down, new_down = adamw_step(
        w_down, ffn_g[2].T, m_down, v_down, rate_down, decay_rate
    )
    first_gains, second_gains, new_gains = adamw_step(
        norm_gains, gains_g, m_gains, v_gains, rate_gains, 0.0
    )
    return (
        layer_out,
        input_grad,
        first_query,
        second_query,
        new_query,
        first_kv,
        second_kv,
        new_kv,
        first_out,
        second_out,
        new_out,
        first_gate_up,
        second_gate_up,
        new_gate_up,
        first_down,
        second_down,
        new_down,
        first_gains,
        second_gains,
        new_gains,
    )


def solution(mesh):
    n_dp, n_tensor = mesh.shape["dp"], mesh.shape["tensor"]
    fine = Mesh(mesh.devices.reshape(n_dp // 2, 2, n_tensor), ("a", "c", "z"))
    dp, every = ("a", "c"), ("a", "c", "z")
    token = P(every, None)
    query = P(dp, "z")
    shared = P(None, every, None)
    output = P("z", dp)
    gate_up = P(None, dp, "z")
    gains = P(None, every)
    in_specs = (token, token, P(dp), query, shared, output, gate_up, output, gains)
    in_specs += (query, query, shared, shared, output, output, gate_up, gate_up)
    in_specs += (output, output, gains, gains)
    out_specs = (token, token) + (query,) * 3 + (shared,) * 3 + (output,) * 3
    out_specs += (gate_up,) * 3 + (output,) * 3 + (gains,) * 3
    return jax.shard_map(body, mesh=fine, in_specs=in_specs, out_specs=out_specs, check_vma=False)
```
